32 devices in a mesh: section: 4 (over y, x), rows: 8 (over z, core).
Axes of the slice: x: 2, y: 2, z: 4, core: 2. Of those that a mesh axis runs over, the one named last changes fastest.
Arguments:
- node_features: bfloat16 [4, 128, 512], P(None, 'rows'), may hold values from -6 to 6
- edge_features: bfloat16 [4, 1024, 512], P(None, 'rows'), may hold values from -6 to 6
- sender_owner: int32 [4, 8, 128, 1], P(None, 'rows'), may hold values from 0 to 7; in each aligned block of 128 rows (0 to 127, 128 to 255, ..., all dimensions but the last counted through in order) at most 32 rows name the same one
- sender_local: int32 [4, 8, 128], P(None, 'rows'), may hold values from 0 to 15
- receivers: int32 [4, 8, 128], P(None, 'rows'), may hold values from 0 to 15, never falling along the last dimension, each value on 1 to 16 neighbouring positions
- cotangent: bfloat16 [4, 128, 512], P(None, 'rows'), may hold values from -6 to 6
- edge_w_one: bfloat16 [2, 1536, 512], replicated, may hold values from -0.15625 to 0.15625
- edge_b_one: bfloat16 [2, 512], replicated, may hold values from -3 to 3
- edge_w_two: bfloat16 [2, 512, 512], replicated, may hold values from -0.25 to 0.25
- edge_b_two: bfloat16 [2, 512], replicated, may hold values from -3 to 3
- edge_gain: bfloat16 [2, 512], replicated, may hold values from 0.5 to 1.5
- edge_shift: bfloat16 [2, 512], replicated, may hold values from -3 to 3
- node_w_one: bfloat16 [2, 1024, 512], replicated, may hold values from -0.1875 to 0.1875
- node_b_one: bfloat16 [2, 512], replicated, may hold values from -3 to 3
- node_w_two: bfloat16 [2, 512, 512], replicated, may hold values from -0.25 to 0.25
- node_b_two: bfloat16 [2, 512], replicated, may hold values from -3 to 3
- node_gain: bfloat16 [2, 512], replicated, may hold values from 0.5 to 1.5
- node_shift: bfloat16 [2, 512], replicated, may hold values from -3 to 3
Outputs:
- final_nodes: bfloat16 [4, 128, 512], P('section', 'rows')
- grad_nodes: float32 [4, 128, 512], P('section', 'rows')
- grad_edges: float32 [4, 1024, 512], P('section', 'rows')
- grad_edge_w_one: float32 [2, 1536, 512], P(None, 'rows')
- grad_edge_b_one: float32 [2, 512], P(None, 'rows')
- grad_edge_w_two: float32 [2, 512, 512], P(None, 'rows')
- grad_edge_b_two: float32 [2, 512], P(None, 'rows')
- grad_edge_gain: float32 [2, 512], P(None, 'rows')
- grad_edge_shift: float32 [2, 512], P(None, 'rows')
- grad_node_w_one: float32 [2, 1024, 512], P(None, 'rows')
- grad_node_b_one: float32 [2, 512], P(None, 'rows')
- grad_node_w_two: float32 [2, 512, 512], P(None, 'rows')
- grad_node_b_two: float32 [2, 512], P(None, 'rows')
- grad_node_gain: float32 [2, 512], P(None, 'rows')
- grad_node_shift: float32 [2, 512], P(None, 'rows')
The draws below stay inside these ranges and needn't reach their ends.
Inputs may be any that keep to these rules, and one draw needn't show every extreme that they name: `sender_owner`: within one micro-batch, the 128 edges of one node block name any one node block as owner at most 32 times; in every draw some block is named exactly 32 times. `receivers`: within one node block of one micro-batch the values never fall; every node has 1 to 16 incoming edges, and in each node block of each micro-batch some node has exactly 16.
All inputs are finite; a program needn't handle non-finite values.
Results may differ from the reference program's by a relative error of at most 0.015.
Values may be sent and summed in bfloat16 or wider, within the bound.
A program may use at most 128 MiB of HBM per device.

```python
import math
import jax
import jax.numpy as jnp
import numpy as np
from jax import lax

D = 512
H = 512
NODE_DEV = 16
MICRO = 4
LAYERS = 2
SHARDS = 8
EDGE_DEV = 128
PAIR_CAP = 32
NODES = 128
EDGES = 1024


def plant(values, own_key, smallest, top_value):
    place = [jax.random.randint(jax.random.fold_in(own_key, axis), (), 0, length) for axis, length in enumerate(values.shape)]
    longest = values.shape.index(max(values.shape))
    beside = place[:longest] + [(place[longest] + 1) % values.shape[longest]] + place[longest + 1:]
    return values.at[tuple(place)].set(smallest).at[tuple(beside)].set(top_value)


def block_scale(own_key, extent, shards, least, largest):
    def one(position, blocks):
        draws = jax.random.uniform(jax.random.fold_in(jax.random.fold_in(own_key, 6), position), (blocks,), jnp.float32, least / len(shards), largest / len(shards))
        return jnp.repeat(jnp.exp(draws), extent[position] // blocks).reshape((-1,) + (1,) * (len(extent) - position - 1))

    factor_of = one(*shards[0])
    for cut in shards[1:]:
        factor_of = factor_of * one(*cut)
    return factor_of


def profile(number_of, total, limit, lean):
    loads = [(1 << 20) // math.isqrt(standing ** lean) + 1 for standing in range(2, number_of + 1)]
    surplus, holding = total - limit - (number_of - 1), [1] * (number_of - 1)
    while surplus > 0:
        movable = [i for i in range(number_of - 1) if holding[i] < limit]
        mass, left = sum([loads[i] for i in movable]), surplus
        for i in movable:
            addition = min(limit - holding[i], max(1, left * loads[i] // mass), surplus)
            holding[i] = holding[i] + addition
            surplus = surplus - addition
    return np.array([limit] + holding)


def ragged_sizes(rng, count, total, reach, lean):
    if count == 2:
        one = jax.random.randint(rng, (), max(1, total - reach), min(reach, total - 1) + 1)
        return jnp.stack([one, total - one])
    sizes = jnp.asarray(profile(count, total, reach, lean), jnp.int32)
    twos = (count - 1) // 2
    source_of, receiver = sizes[1:1 + 2 * twos:2], sizes[2:2 + 2 * twos:2]
    slack = jnp.minimum(source_of - 1, reach - receiver)
    passed = jax.random.randint(jax.random.fold_in(rng, 1), (twos,), 0, 1 << 20) % (slack + 1)
    sizes = sizes.at[1:1 + 2 * twos:2].set(source_of - passed).at[2:2 + 2 * twos:2].set(receiver + passed)
    return sizes[jax.random.permutation(jax.random.fold_in(rng, 2), count)]


def routed_block(stream_key, own, number, rows, count, top, reach, skew):
    sequence = jax.random.permutation(stream_key, count)
    packed, usual = portions_of(count, rows * top, reach, skew, True), portions_of(count, rows * top, reach, skew, False)
    places = jnp.arange(count)

    def named(tallies, offset_by):
        used = int((tallies > 0).sum())
        fixed = max(1, used // 4)
        passed = fixed + (places - fixed + offset_by * (used - fixed)) % max(1, count - fixed)
        return jnp.zeros((count,), jnp.int32).at[sequence[jnp.where(places < fixed, places, passed)]].set(jnp.asarray(tallies, jnp.int32))

    tallies = jnp.where(number % 4 == 0, named(packed, number // 4), named(usual, number - number // 4 - 1))
    mixed = jax.random.permutation(jax.random.fold_in(own, 3), count)
    giver, receiver = mixed[0:count // 2 * 2:2], mixed[1:count // 2 * 2:2]
    room = jnp.minimum(tallies[giver] - 1, reach - tallies[receiver]) // 2
    room = jnp.where((giver == sequence[0]) | (receiver == sequence[0]) | (tallies[receiver] == 0), 0, jnp.maximum(room, 0))
    passed = jax.random.randint(jax.random.fold_in(own, 4), (count // 2,), 0, 1 << 20) % (room + 1)
    tallies = tallies.at[giver].add(-passed).at[receiver].add(passed)
    labels = jnp.searchsorted(jnp.cumsum(tallies), jnp.arange(rows * top), side="right").astype(jnp.int32)
    listing = labels.reshape(top, rows).T
    listing = listing[jax.random.permutation(jax.random.fold_in(own, 1), rows)]
    offset_by = jax.random.randint(jax.random.fold_in(own, 2), (rows, 1), 0, top)
    return jnp.take_along_axis(listing, (jnp.arange(top)[None, :] + offset_by) % top, axis=1)


def portions_of(count, total, most, lean, full):
    loads = [(1 << 20) // math.isqrt(grade ** lean) + 1 for grade in range(1, count + 1)]
    largest = most if full else min(most, max(-(-total // count), total * loads[0] // sum(loads)))
    least = 1 if total - largest >= count - 1 else 0
    given, spare = [largest] + [least] * (count - 1), total - largest - least * (count - 1)
    while spare > 0:
        movable = [i for i in range(1, count) if given[i] < largest] or [i for i in range(1, count) if given[i] < most]
        whole, remaining = sum([loads[i] for i in movable]), spare
        for i in movable:
            extra = min(most - given[i], max(1, remaining * loads[i] // whole), spare)
            given[i] = given[i] + extra
            spare = spare - extra
    return np.array(given)


def noise(own_key, extent, spread, most, shards=(), kind=jnp.bfloat16):
    drawn = jax.random.normal(own_key, extent, jnp.float32) * spread
    if len(shards) > 0:
        drawn = block_scale(own_key, extent, shards, -0.22, 0.18) * drawn
    return jnp.clip(drawn, min=-most, max=most).astype(kind)


def setup_inputs(seed: int = 0) -> dict:
    splits = jax.random.split(jax.random.key(seed), 19)
    node_features = noise(splits[0], (MICRO, NODES, D), 1.0, 6.0, ((1, 8),))
    edge_features = noise(splits[1], (MICRO, EDGES, D), 1.0, 6.0, ((1, 8),))
    sender_owner_keys = jax.random.split(jax.random.fold_in(splits[2], 1), MICRO * SHARDS * EDGE_DEV // EDGE_DEV)
    sender_owner_turns = jax.random.permutation(jax.random.fold_in(splits[2], 3), MICRO * SHARDS * EDGE_DEV // EDGE_DEV)
    sender_owner = jax.vmap(lambda own, number: routed_block(jax.random.fold_in(splits[2], 2), own, number, EDGE_DEV, SHARDS, 1, PAIR_CAP, 2))(sender_owner_keys, sender_owner_turns).reshape((MICRO, SHARDS, EDGE_DEV, 1))
    sender_local = plant(jax.random.randint(splits[3], (MICRO, SHARDS, EDGE_DEV), 0, NODE_DEV), jax.random.fold_in(splits[3], 1), 0, NODE_DEV - 1).astype(jnp.int32)
    receivers = jax.vmap(lambda own: jnp.searchsorted(jnp.cumsum(ragged_sizes(own, NODE_DEV, EDGE_DEV, 2 * EDGE_DEV // NODE_DEV, 2)), jnp.arange(EDGE_DEV), side="right"))(jax.random.split(splits[4], MICRO * SHARDS)).reshape((MICRO, SHARDS, EDGE_DEV)).astype(jnp.int32)
    cotangent = noise(splits[5], (MICRO, NODES, D), 1.0, 6.0, ((1, 8),))
    edge_w_one = noise(splits[6], (LAYERS, 3 * D, H), (3 * D) ** -0.5, 0.15625)
    edge_b_one = noise(splits[7], (LAYERS, H), 0.5, 3.0)
    edge_w_two = noise(splits[8], (LAYERS, H, D), H ** -0.5, 0.25)
    edge_b_two = noise(splits[9], (LAYERS, D), 0.5, 3.0)
    edge_gain = jnp.clip(jax.random.uniform(splits[10], (LAYERS, D), jnp.float32, 0.5, 1.5), 0.5, 1.5).astype(jnp.bfloat16)
    edge_shift = noise(splits[11], (LAYERS, D), 0.5, 3.0)
    node_w_one = noise(splits[12], (LAYERS, 2 * D, H), (2 * D) ** -0.5, 0.1875)
    node_b_one = noise(splits[13], (LAYERS, H), 0.5, 3.0)
    node_w_two = noise(splits[14], (LAYERS, H, D), H ** -0.5, 0.25)
    node_b_two = noise(splits[15], (LAYERS, D), 0.5, 3.0)
    node_gain = jnp.clip(jax.random.uniform(splits[16], (LAYERS, D), jnp.float32, 0.5, 1.5), 0.5, 1.5).astype(jnp.bfloat16)
    node_shift = noise(splits[17], (LAYERS, D), 0.5, 3.0)
    return {"node_features": node_features, "edge_features": edge_features, "sender_owner": sender_owner, "sender_local": sender_local, "receivers": receivers, "cotangent": cotangent, "edge_w_one": edge_w_one, "edge_b_one": edge_b_one, "edge_w_two": edge_w_two, "edge_b_two": edge_b_two, "edge_gain": edge_gain, "edge_shift": edge_shift, "node_w_one": node_w_one, "node_b_one": node_b_one, "node_w_two": node_w_two, "node_b_two": node_b_two, "node_gain": node_gain, "node_shift": node_shift}


norm_epsilon = 1e-05

@jax.custom_vjp
def low(v):
    return lax.optimization_barrier(v.astype(jnp.bfloat16)).astype(jnp.float32)

@jax.custom_vjp
def low_back(v):
    return v

def low_keep(v):
    return (low(v), None)

def low_pass(kept, grad):
    return (grad,)

def back_keep(v):
    return (v, None)

def back_low(kept, grad):
    return (low(grad),)
low.defvjp(low_keep, low_pass)
low_back.defvjp(back_keep, back_low)

def product(left, right):
    return jnp.dot(left, right, precision=lax.Precision.HIGHEST, preferred_element_type=jnp.float32)

def branch_mlp(inputs, weights):
    w_one, b_one, w_two, b_two, weight_gain, weight_shift = weights
    hidden_pre = low_back(product(inputs, w_one) + b_one)
    hidden = low(jax.nn.silu(hidden_pre))
    lifted = low_back(product(hidden, w_two) + b_two)
    center = lifted - lax.optimization_barrier(jnp.mean(lifted, axis=-1, keepdims=True))
    normed = center * lax.rsqrt(lax.optimization_barrier(jnp.mean(center * center, axis=-1, keepdims=True)) + norm_epsilon)
    return normed * weight_gain + weight_shift

def edge_section(node_state, edge_state, senders, targets, weights):
    inputs = jnp.concatenate([edge_state, node_state[senders], node_state[targets]], axis=1)
    return (node_state, edge_state + branch_mlp(inputs, weights))

def node_section(node_state, edge_state, senders, targets, weights):
    gathered_sum = low(jax.ops.segment_sum(edge_state, targets, num_segments=NODES))
    inputs = jnp.concatenate([node_state, gathered_sum], axis=1)
    return (node_state + branch_mlp(inputs, weights), edge_state)

def reference(node_features, edge_features, sender_owner, sender_local, receivers, cotangent, edge_w_one, edge_b_one, edge_w_two, edge_b_two, edge_gain, edge_shift, node_w_one, node_b_one, node_w_two, node_b_two, node_gain, node_shift):
    sender_index = (sender_owner[..., 0] * NODE_DEV + sender_local).reshape(MICRO, EDGES).astype(jnp.int32)
    block_start = jnp.arange(SHARDS, dtype=jnp.int32) * NODE_DEV
    receiver_index = (receivers + block_start[None, :, None]).reshape(MICRO, EDGES).astype(jnp.int32)
    edge_params = tuple((param_array.astype(jnp.float32) for param_array in (edge_w_one, edge_b_one, edge_w_two, edge_b_two, edge_gain, edge_shift)))
    node_params = tuple((param_array.astype(jnp.float32) for param_array in (node_w_one, node_b_one, node_w_two, node_b_two, node_gain, node_shift)))

    def forward(nodes, edges, edge_set, node_set):

        def micro_step(pieces):
            node_state, edge_state, senders, targets = pieces
            for section_number in range(2 * LAYERS):
                if section_number > 0:
                    node_state = low_back(low(node_state))
                    edge_state = low_back(low(edge_state))
                if section_number % 2 == 0:
                    layer_params = tuple((param_array[section_number // 2] for param_array in edge_set))
                    node_state, edge_state = jax.checkpoint(edge_section)(node_state, edge_state, senders, targets, layer_params)
                else:
                    layer_params = tuple((param_array[section_number // 2] for param_array in node_set))
                    node_state, edge_state = jax.checkpoint(node_section)(node_state, edge_state, senders, targets, layer_params)
            return low(node_state)
        return lax.map(jax.checkpoint(micro_step), (nodes, edges, sender_index, receiver_index))
    final_nodes, pullback = jax.vjp(forward, node_features.astype(jnp.float32), edge_features.astype(jnp.float32), edge_params, node_params)
    grad_nodes, grad_edges, edge_grads, node_grads = pullback(cotangent.astype(jnp.float32))
    return (final_nodes.astype(jnp.bfloat16), grad_nodes, grad_edges, edge_grads[0], edge_grads[1], edge_grads[2], edge_grads[3], edge_grads[4], edge_grads[5], node_grads[0], node_grads[1], node_grads[2], node_grads[3], node_grads[4], node_grads[5])
```

```python
import jax
import jax.numpy as jnp
from jax import lax
from jax.sharding import PartitionSpec as P

norm_epsilon = 1e-05
f32 = jnp.float32
bf16 = jnp.bfloat16


def dot(left, right):
    return jnp.dot(left, right, preferred_element_type=f32)


def contract_rows(left, right):
    return lax.dot_general(left, right, (((0,), (0,)), ((), ())), preferred_element_type=f32)


def contract_cols(left, right):
    return lax.dot_general(left, right, (((1,), (1,)), ((), ())), preferred_element_type=f32)


def mlp_forward(hidden_pre, weights):
    b_one, w_two, b_two, gain, shift = weights
    hidden_pre = hidden_pre + b_one.astype(f32)
    hidden = jax.nn.silu(hidden_pre).astype(bf16)
    lifted = dot(hidden, w_two) + b_two.astype(f32)
    center = lifted - jnp.mean(lifted, axis=-1, keepdims=True)
    norm_scale = lax.rsqrt(jnp.mean(center * center, axis=-1, keepdims=True) + norm_epsilon)
    normed = center * norm_scale
    branch = normed * gain.astype(f32) + shift.astype(f32)
    return branch, (hidden_pre, hidden, normed, norm_scale)


def mlp_backward(weights, saved, grad_branch):
    b_one, w_two, b_two, gain, shift = weights
    hidden_pre, hidden, normed, norm_scale = saved
    grad_normed = grad_branch * gain.astype(f32)
    grad_lifted = norm_scale * (
        grad_normed
        - jnp.mean(grad_normed, axis=-1, keepdims=True)
        - normed * jnp.mean(grad_normed * normed, axis=-1, keepdims=True)
    )
    grad_lifted = grad_lifted.astype(bf16)
    grad_hidden = contract_cols(grad_lifted, w_two)
    sigma = jax.nn.sigmoid(hidden_pre)
    grad_pre = (grad_hidden * (sigma * (1.0 + hidden_pre * (1.0 - sigma)))).astype(bf16)
    terms = (
        jnp.sum(grad_pre.astype(f32), axis=0),
        contract_rows(hidden, grad_lifted),
        jnp.sum(grad_lifted.astype(f32), axis=0),
        jnp.sum(grad_branch * normed, axis=0),
        jnp.sum(grad_branch, axis=0),
    )
    return grad_pre, terms


def body(node_features, edge_features, sender_owner, sender_local, receivers, cotangent, *weights):
    micro = lax.axis_index("section")
    micro_count, node_dev, width = node_features.shape
    shards = lax.axis_size("rows")
    edge_weights, node_weights = weights[:6], weights[6:]
    layers = edge_weights[0].shape[0]

    def pick(array):
        return lax.dynamic_index_in_dim(array, micro, 0, keepdims=False)

    node = pick(node_features)
    edge = pick(edge_features)
    senders = pick(sender_owner)[0, :, 0] * node_dev + pick(sender_local)[0]
    targets = pick(receivers)[0]
    onehot_sender = (
        senders[:, None] == jnp.arange(shards * node_dev, dtype=jnp.int32)[None, :]
    ).astype(bf16)
    onehot_target = (targets[:, None] == jnp.arange(node_dev, dtype=jnp.int32)[None, :]).astype(
        bf16
    )

    stash = []
    for layer in range(layers):
        w_one, *edge_rest = (w[layer] for w in edge_weights)
        all_nodes = lax.all_gather(node, "rows", axis=0, tiled=True)
        sent = dot(onehot_sender, all_nodes).astype(bf16)
        received = dot(onehot_target, node).astype(bf16)
        pre = dot(jnp.concatenate([edge, sent, received], axis=1), w_one)
        branch, edge_saved = mlp_forward(pre, edge_rest)
        edge_in = edge
        edge = (edge.astype(f32) + branch).astype(bf16)
        v_one, *node_rest = (w[layer] for w in node_weights)
        gathered = contract_rows(onehot_target, edge).astype(bf16)
        node_in = node
        branch, node_saved = mlp_forward(
            dot(jnp.concatenate([node, gathered], axis=1), v_one), node_rest
        )
        node = (node.astype(f32) + branch).astype(bf16)
        stash.append((node_in, edge_in, gathered, edge_saved, node_saved))

    final = node
    grad_node = pick(cotangent).astype(f32)
    grad_edge = jnp.zeros(edge.shape, f32)
    edge_terms, node_terms = [], []
    for layer in reversed(range(layers)):
        node_in, edge_in, gathered, edge_saved, node_saved = stash[layer]
        w_one, *edge_rest = (w[layer] for w in edge_weights)
        v_one, *node_rest = (w[layer] for w in node_weights)
        grad_pre, terms = mlp_backward(node_rest, node_saved, grad_node)
        v_grad = contract_rows(jnp.concatenate([node_in, gathered], axis=1), grad_pre)
        node_terms.insert(0, (v_grad,) + terms)
        grad_x = contract_cols(grad_pre, v_one)
        grad_node = (grad_node + grad_x[:, :width]).astype(bf16).astype(f32)
        grad_aggregate = grad_x[:, width:].astype(bf16)
        grad_edge = (grad_edge + dot(onehot_target, grad_aggregate)).astype(bf16).astype(f32)
        grad_pre, terms = mlp_backward(edge_rest, edge_saved, grad_edge)
        by_sender = contract_rows(onehot_sender, grad_pre).astype(bf16)
        by_sender = lax.psum_scatter(by_sender, "rows", scatter_dimension=0, tiled=True)
        by_target = contract_rows(onehot_target, grad_pre).astype(bf16)
        w_grad = jnp.concatenate(
            [
                contract_rows(edge_in, grad_pre),
                contract_rows(node_in, by_sender),
                contract_rows(node_in, by_target),
            ],
            axis=0,
        )
        edge_terms.insert(0, (w_grad,) + terms)
        grad_edge = grad_edge + contract_cols(grad_pre, w_one[:width])
        grad_node = (
            grad_node
            + contract_cols(by_sender, w_one[width : 2 * width])
            + contract_cols(by_target, w_one[2 * width :])
        )
        if layer > 0:
            grad_edge = grad_edge.astype(bf16).astype(f32)
            grad_node = grad_node.astype(bf16).astype(f32)

    def totals(terms):
        stacked = [jnp.stack(parts) for parts in zip(*terms)]
        scattered = [
            lax.psum_scatter(part.astype(bf16), "rows", scatter_dimension=1, tiled=True)
            for part in stacked
        ]
        return [lax.psum(part, "section").astype(f32) for part in scattered]

    return (final, grad_node, grad_edge) + tuple(
        x for x in totals(edge_terms) + totals(node_terms)
    )


def solution(mesh):
    def whole(*args):
        out = body(*args)
        return tuple(x[None] for x in out[:3]) + out[3:]

    in_specs = (
        P(None, "rows", None),
        P(None, "rows", None),
        P(None, "rows", None, None),
        P(None, "rows", None),
        P(None, "rows", None),
        P(None, "rows", None),
    ) + (P(),) * 12
    state = P("section", "rows", None)
    matrix, vector = P(None, "rows", None), P(None, "rows")
    out_specs = (state,) * 3 + (matrix, vector, matrix, vector, vector, vector) * 2
    return jax.shard_map(whole, mesh=mesh, in_specs=in_specs, out_specs=out_specs, check_vma=False)
```

```python
import functools
from types import SimpleNamespace

import jax
import jax.numpy as jnp
from jax import lax
from jax.experimental import pallas as pl
from jax.experimental.pallas import tpu as pltpu
from jax.sharding import PartitionSpec as P

f32 = jnp.float32
bf16 = jnp.bfloat16
MESH = pl.DeviceIdType.MESH
norm_epsilon = 1e-05
vector_rows = 16
w_one, b_one, w_two, b_two, gain, shift = range(6)


def dot(left, right):
    return jnp.dot(left, right, preferred_element_type=f32)


def contract_rows(left, right):
    return lax.dot_general(left, right, (((0,), (0,)), ((), ())), preferred_element_type=f32)


def contract_cols(left, right):
    return lax.dot_general(left, right, (((1,), (1,)), ((), ())), preferred_element_type=f32)


def whole_tiles(rows):
    return -(-rows // 16) * 16


def each(count, visit):
    if count <= 8:
        for i in range(count):
            visit(i)
    else:

        def step(i, carry):
            visit(i)
            return carry

        lax.fori_loop(0, count, step, 0)


def layer_norm(lifted):
    center = lifted - jnp.mean(lifted, axis=-1, keepdims=True)
    scale = lax.rsqrt(jnp.mean(center * center, axis=-1, keepdims=True) + norm_epsilon)
    return center * scale, scale


def activate(pre):
    sigma = jax.nn.sigmoid(pre)
    return (pre * sigma).astype(bf16), sigma * (1.0 + pre * (1.0 - sigma))


def branch_back(grad_branch, gain_row, normed, scale):
    grad_normed = grad_branch * gain_row
    return (
        scale
        * (
            grad_normed
            - jnp.mean(grad_normed, axis=-1, keepdims=True)
            - normed * jnp.mean(grad_normed * normed, axis=-1, keepdims=True)
        )
    ).astype(bf16)


def column_sums(grad_pre, grad_lifted, grad_branch, normed):
    rows = [
        jnp.sum(grad_pre.astype(f32), axis=0, keepdims=True),
        jnp.sum(grad_lifted.astype(f32), axis=0, keepdims=True),
        jnp.sum(grad_branch * normed, axis=0, keepdims=True),
        jnp.sum(grad_branch, axis=0, keepdims=True),
    ]
    rows.append(jnp.zeros((vector_rows - 4, grad_branch.shape[1]), f32))
    return jnp.concatenate(rows, axis=0).astype(bf16)


def send(source, target, send_sem, recv_sem, device):
    pltpu.make_async_remote_copy(
        src_ref=source,
        dst_ref=target,
        send_sem=send_sem,
        recv_sem=recv_sem,
        device_id=device,
        device_id_type=MESH,
    ).start()


def ended(buffer, sem):
    pltpu.make_async_copy(buffer, buffer, sem).wait()


def kernel(plan, *refs):
    v = SimpleNamespace(**dict(zip(plan.names, refs)))
    layers, sections, shards = plan.layers, plan.sections, plan.shards
    node_dev, edge_dev, width = plan.node_dev, plan.edge_dev, plan.width
    quarter, pairs, plane = width // sections, shards // 2, 2 * sections
    nodes_total = shards * node_dev
    three_rows, two_rows, one_rows = (part * width // shards for part in (3, 2, 1))
    edge_weights, node_weights = refs[plan.weights : plan.weights + 6], refs[
        plan.weights + 6 : plan.weights + 12
    ]
    edge_v, node_v = refs[plan.weights_v : plan.weights_v + 6], refs[
        plan.weights_v + 6 : plan.weights_v + 12
    ]
    grads = refs[plan.grads : plan.grads + 12]
    section, row = lax.axis_index("section"), lax.axis_index("rows")
    pair, core = row // 2, row % 2
    plane_slot = section * 2 + core

    def group(data, send_sem, recv_sem):
        return SimpleNamespace(data=data, send=send_sem, recv=recv_sem)

    def pair_group(own, come, send_sem, recv_sem, total, full, full_send, full_recv):
        return SimpleNamespace(
            own=own,
            come=come,
            send=send_sem,
            recv=recv_sem,
            total=total,
            full=full,
            full_send=full_send,
            full_recv=full_recv,
        )

    lefts = group(v.lefts, v.lefts_send, v.lefts_recv)
    rights = group(v.rights, v.rights_send, v.rights_recv)
    node_lefts = group(v.node_lefts, v.node_lefts_send, v.node_lefts_recv)
    node_rights = group(v.node_rights, v.node_rights_send, v.node_rights_recv)
    sum_rights = group(v.sum_rights, v.sum_rights_send, v.sum_rights_recv)
    edge_pairs, lift_pairs, node_pairs = (
        pair_group(*refs[start : start + 8])
        for start in range(plan.pair_groups, plan.pair_groups + 24, 8)
    )

    loads = {}

    def load(key, source, target):
        copy = pltpu.make_async_copy(source, target, v.load_sem.at[len(loads)])
        copy.start()
        loads[key] = copy

    load(0, v.node_features.at[section], v.nodes.at[0, row])
    load(1, v.owner.at[section], v.owner_v)
    load(2, v.local.at[section], v.local_v)
    load(3, v.receivers.at[section], v.receivers_v)
    load(4, v.edge_features.at[section], v.edge_in.at[0])
    for kind in (b_one, b_two, gain, shift):
        load((0, kind), edge_weights[kind], edge_v[kind])
        load((1, kind), node_weights[kind], node_v[kind])
    for layer in range(layers):
        for kind in (w_one, w_two):
            load((0, kind, layer), edge_weights[kind].at[layer], edge_v[kind].at[layer])
        for kind in (w_one, w_two):
            load((1, kind, layer), node_weights[kind].at[layer], node_v[kind].at[layer])
    load(5, v.cotangent.at[section], v.cotangent_v)

    barrier = pltpu.get_barrier_semaphore()

    def greet(device):
        pl.semaphore_signal(barrier, inc=1, device_id=device, device_id_type=MESH)

    each(shards - 1, lambda i: greet((section, (row + 1 + i) % shards)))
    for step in range(1, sections):
        for other in range(2):
            greet(((section + step) % sections, pair * 2 + other))

    def peer_rows(visit):
        each(shards - 1, lambda i: visit((row + 1 + i) % shards))

    def send_nodes(layer):
        def one(peer):
            send(
                v.nodes.at[layer, row],
                v.nodes.at[layer, row],
                v.nodes_send.at[layer, peer],
                v.nodes_recv.at[layer, row],
                (section, peer),
            )

        peer_rows(one)

    def send_sums(layer):
        def one(peer):
            send(
                v.sums.at[layer, peer],
                v.sums_in.at[layer, row],
                v.sums_send.at[layer, peer],
                v.sums_recv.at[layer, row],
                (section, peer),
            )

        peer_rows(one)

    def from_rows(data, sem, layer):
        peer_rows(lambda peer: ended(data.at[layer, peer], sem.at[layer, peer]))

    def to_plane(group, layer, sources):
        def one(target_section, other):
            source = sources[other](target_section)
            send(
                source,
                group.data.at[layer, plane_slot, pl.ds(0, source.shape[0])],
                group.send.at[layer, target_section * 2 + other],
                group.recv.at[layer, plane_slot],
                (target_section, pair * 2 + other),
            )

        for step in range(1, sections):
            for other in range(2):
                if sources[other] is not None:
                    one((section + step) % sections, other)
        for other in range(2):
            if sources[other] is None:
                continue

            @pl.when(core != other)
            def _(other=other):
                one(section, other)

            @pl.when(core == other)
            def _(other=other):
                source = sources[other](section)
                group.data[layer, plane_slot, 0 : source.shape[0]] = source[...]

    def from_plane(group, layer, rows):
        for step in range(1, plane):
            slot = (plane_slot + step) % plane
            ended(group.data.at[layer, slot, pl.ds(0, rows)], group.recv.at[layer, slot])

    def plane_left(group, layer, rows):
        def one(target_section, other):
            ended(
                group.data.at[layer, 0, pl.ds(0, rows[other])],
                group.send.at[layer, target_section * 2 + other],
            )

        for other in range(2):
            if rows[other]:
                for step in range(1, sections):
                    one((section + step) % sections, other)
                pl.when(core != other)(functools.partial(one, section, other))

    def peer_pairs(visit):
        each(pairs - 1, lambda i: visit((pair + 1 + i) % pairs))

    def send_pairs(group, layer):
        def one(peer):
            send(
                group.own.at[layer, peer],
                group.come.at[layer, pair],
                group.send.at[layer, peer],
                group.recv.at[layer, pair],
                (section, peer * 2 + core),
            )

        peer_pairs(one)

    def share(group, layer, target_section, other):
        send(
            group.total.at[layer, other],
            group.full.at[layer, section],
            group.full_send.at[layer, target_section * 2 + other],
            group.full_recv.at[layer, section],
            (target_section, pair * 2 + other),
        )

    def add_pairs(group, layer):
        peer_pairs(lambda peer: ended(group.come.at[layer, peer], group.recv.at[layer, peer]))
        group.come[layer, pair] = group.own[layer, pair]
        total = group.come[layer, 0].astype(f32)
        for peer in range(1, pairs):
            total = total + group.come[layer, peer].astype(f32)
        group.total[layer] = total.astype(bf16)
        for step in range(1, sections):
            for other in range(2):
                share(group, layer, (section + step) % sections, other)
        share(group, layer, section, 1 - core)
        group.full[layer, section] = group.total[layer, core]

    def pairs_left(group, layer):
        peer_pairs(lambda peer: ended(group.own.at[layer, peer], group.send.at[layer, peer]))
        for step in range(1, plane):
            ended(group.total.at[layer, 0], group.full_send.at[layer, (plane_slot + step) % plane])

    def from_givers(group, layer, giver):
        for step in range(1, sections):
            slot = (section + step) % sections
            ended(group.full.at[layer, slot], group.full_recv.at[layer, slot])

        @pl.when(core != giver)
        def _():
            ended(group.full.at[layer, section], group.full_recv.at[layer, section])

    def store_blocks(target, product, offset, rows):
        padded = whole_tiles(rows)
        for owner in range(shards):
            block = product[owner * rows : (owner + 1) * rows]
            if padded != rows:
                block = jnp.concatenate([block, jnp.zeros((padded - rows, quarter), f32)], axis=0)
            target[owner // 2, owner % 2, offset : offset + padded] = block.astype(bf16)

    def store_vectors(target, total, offset):
        for owner in range(shards):
            target[owner // 2, owner % 2, offset : offset + vector_rows] = total.astype(bf16)

    def quarters(target, offset, value):
        rows = value.shape[0]
        for part in range(sections):
            target[part, offset : offset + rows] = value[
                :, part * quarter : (part + 1) * quarter
            ].astype(bf16)

    def vector(ref, layer):
        return ref[...].astype(f32)[layer : layer + 1]

    pl.semaphore_wait(barrier, shards - 1 + 2 * (sections - 1))
    loads[0].wait()
    send_nodes(0)
    loads[4].wait()
    to_plane(lefts, 0, (lambda s: v.edge_in.at[0], None))

    for key in (1, 2, 3):
        loads[key].wait()
    sender_row = v.owner_v[...] * node_dev + v.local_v[...]
    target_row = v.receivers_v[...]
    eye = lax.broadcasted_iota(jnp.int32, (edge_dev, edge_dev), 0) == lax.broadcasted_iota(
        jnp.int32, (edge_dev, edge_dev), 1
    )

    def to_column(values):
        spread = jnp.broadcast_to(values, (edge_dev, edge_dev))
        column = jnp.sum(jnp.where(eye, spread, 0).astype(f32), axis=1, keepdims=True)
        return column.astype(jnp.int32)

    def one_hot(values, count, axis):
        places = (count, edge_dev) if axis == 0 else (edge_dev, count)
        match = lax.broadcasted_iota(jnp.int32, places, axis) == values
        return jnp.where(match, 1.0, 0.0).astype(bf16)

    v.from_nodes[...] = one_hot(to_column(sender_row), nodes_total, 1)
    v.to_nodes[...] = one_hot(sender_row, nodes_total, 0)
    v.from_targets[...] = one_hot(to_column(target_row), node_dev, 1)
    v.to_targets[...] = one_hot(target_row, node_dev, 0)
    for kind in (b_one, b_two, gain, shift):
        loads[(0, kind)].wait()
        loads[(1, kind)].wait()

    def edge_forward(layer):
        node = v.nodes[layer, row]
        edge = v.edge_in[layer]
        loads[(0, w_one, layer)].wait()
        received = dot(v.from_targets[...], node).astype(bf16)
        v.work[...] = (
            dot(edge, edge_v[w_one][layer, 0:width])
            + dot(received, edge_v[w_one][layer, 2 * width : 3 * width])
            + vector(edge_v[b_one], layer)
        )
        from_rows(v.nodes, v.nodes_recv, layer)
        sent = dot(v.from_nodes[...], v.nodes[layer].reshape(nodes_total, width)).astype(bf16)
        hidden, slope = activate(
            v.work[...] + dot(sent, edge_v[w_one][layer, width : 2 * width])
        )
        v.edge_hidden[layer] = hidden
        v.edge_slope[layer] = slope
        to_plane(lefts, layer, (None, lambda s: v.edge_hidden.at[layer]))
        loads[(0, w_two, layer)].wait()
        normed, scale = layer_norm(
            dot(hidden, edge_v[w_two][layer]) + vector(edge_v[b_two], layer)
        )
        v.edge_normed[layer] = normed
        v.edge_scale[layer] = scale
        edge = (
            edge.astype(f32)
            + (normed * vector(edge_v[gain], layer) + vector(edge_v[shift], layer))
        ).astype(bf16)
        if layer + 1 < layers:
            v.edge_in[layer + 1] = edge
            to_plane(lefts, layer + 1, (lambda s: v.edge_in.at[layer + 1], None))
        return node, dot(v.to_targets[...], edge).astype(bf16)

    def node_forward(layer, node, gathered):
        loads[(1, w_one, layer)].wait()
        hidden, slope = activate(
            dot(node, node_v[w_one][layer, 0:width])
            + dot(gathered, node_v[w_one][layer, width : 2 * width])
            + vector(node_v[b_one], layer)
        )
        v.node_slope[layer] = slope
        loads[(1, w_two, layer)].wait()
        normed, scale = layer_norm(
            dot(hidden, node_v[w_two][layer]) + vector(node_v[b_two], layer)
        )
        v.node_normed[layer] = normed
        v.node_scale[layer] = scale
        new_node = (
            node.astype(f32)
            + (normed * vector(node_v[gain], layer) + vector(node_v[shift], layer))
        ).astype(bf16)
        if layer + 1 < layers:
            v.nodes[layer + 1, row] = new_node
            send_nodes(layer + 1)
        else:
            v.final[0] = new_node
        v.node_lefts_own[layer, 0:node_dev] = node
        v.node_lefts_own[layer, node_dev : 2 * node_dev] = gathered
        v.node_lefts_own[layer, 2 * node_dev : 3 * node_dev] = hidden
        to_plane(
            node_lefts,
            layer,
            (
                lambda s: v.node_lefts_own.at[layer, pl.ds(0, node_dev)],
                lambda s: v.node_lefts_own.at[layer],
            ),
        )

    for layer in range(layers):
        node, gathered = edge_forward(layer)
        node_forward(layer, node, gathered)

    def node_products(layer):
        @pl.when(core == 1)
        def _():
            from_plane(node_lefts, layer, 3 * node_dev)
            from_plane(node_rights, layer, 2 * node_dev + vector_rows)
            own = plane * node_dev
            state = v.node_lefts[layer, :, 0:node_dev].reshape(own, width)
            gathered = v.node_lefts[layer, :, node_dev : 2 * node_dev].reshape(own, width)
            hidden = v.node_lefts[layer, :, 2 * node_dev : 3 * node_dev].reshape(own, width)
            grad_pre = v.node_rights[layer, :, 0:node_dev].reshape(own, quarter)
            grad_lifted = v.node_rights[layer, :, node_dev : 2 * node_dev].reshape(own, quarter)
            vectors = v.node_rights[layer, :, 2 * node_dev : 2 * node_dev + vector_rows]
            v.product[0:width] = contract_rows(state, grad_pre)
            v.product[width : 2 * width] = contract_rows(gathered, grad_pre)
            v.product[2 * width : 3 * width] = contract_rows(hidden, grad_lifted)
            target = node_pairs.own.at[layer]
            store_blocks(target, v.product, 0, two_rows)
            start = whole_tiles(two_rows)
            store_blocks(target, v.product.at[pl.ds(2 * width, width)], start, one_rows)
            start += whole_tiles(one_rows)
            store_vectors(target, jnp.sum(vectors.astype(f32), axis=0), start)
            send_pairs(node_pairs, layer)

    def edge_products(layer):
        own = plane * edge_dev

        @pl.when(core == 0)
        def _():
            from_plane(lefts, layer, edge_dev)
            from_plane(rights, layer, edge_dev)
            v.product[0:width] = contract_rows(
                v.lefts[layer].reshape(own, width),
                v.rights[layer, :, 0:edge_dev].reshape(own, quarter),
            )
            from_plane(node_lefts, layer, node_dev)
            from_plane(sum_rights, layer, 2 * node_dev)
            own_nodes = plane * node_dev
            state = v.node_lefts[layer, :, 0:node_dev].reshape(own_nodes, width)
            for part in range(2):
                start = part * node_dev
                v.product[(1 + part) * width : (2 + part) * width] = contract_rows(
                    state,
                    v.sum_rights[layer, :, start : start + node_dev].reshape(own_nodes, quarter),
                )
            store_blocks(edge_pairs.own.at[layer], v.product, 0, three_rows)
            send_pairs(edge_pairs, layer)

        @pl.when(core == 1)
        def _():
            from_plane(lefts, layer, edge_dev)
            from_plane(rights, layer, edge_dev + vector_rows)
            v.product[0:width] = contract_rows(
                v.lefts[layer].reshape(own, width),
                v.rights[layer, :, 0:edge_dev].reshape(own, quarter),
            )
            vectors = v.rights[layer, :, edge_dev : edge_dev + vector_rows]
            target = lift_pairs.own.at[layer]
            store_blocks(target, v.product, 0, one_rows)
            store_vectors(target, jnp.sum(vectors.astype(f32), axis=0), whole_tiles(one_rows))
            send_pairs(lift_pairs, layer)

    def add_node_products(layer):
        pl.when(core == 1)(lambda: add_pairs(node_pairs, layer))

    def add_edge_products(layer):
        pl.when(core == 0)(lambda: add_pairs(edge_pairs, layer))
        pl.when(core == 1)(lambda: add_pairs(lift_pairs, layer))

    def take_columns(value):
        per = quarter // one_rows
        taken = jnp.zeros((vector_rows, one_rows), f32)
        for place in range(per):
            taken = taken + jnp.where(
                row % per == place, value[:, place * one_rows : (place + 1) * one_rows], 0.0
            )
        return taken

    def write_outputs(layer):
        from_givers(edge_pairs, layer, 0)
        from_givers(lift_pairs, layer, 1)
        from_givers(node_pairs, layer, 1)
        node_start = whole_tiles(two_rows)
        for part in range(sections):
            columns = slice(part * quarter, (part + 1) * quarter)

            def put(target, group, start, rows):
                value = group.full[layer, part, start : start + whole_tiles(rows)]
                target[layer, :, columns] = value.astype(f32)[0:rows]

            put(grads[w_one], edge_pairs, 0, three_rows)
            put(grads[w_two], lift_pairs, 0, one_rows)
            put(grads[6 + w_one], node_pairs, 0, two_rows)
            put(grads[6 + w_two], node_pairs, node_start, one_rows)
        holder = row // (quarter // one_rows)
        start = whole_tiles(one_rows)
        edge_vectors = take_columns(
            lift_pairs.full[layer, holder, start : start + vector_rows].astype(f32)
        )
        start += node_start
        node_vectors = take_columns(
            node_pairs.full[layer, holder, start : start + vector_rows].astype(f32)
        )
        for place, kind in enumerate((b_one, b_two, gain, shift)):
            grads[kind][layer : layer + 1] = edge_vectors[place : place + 1]
            grads[6 + kind][layer : layer + 1] = node_vectors[place : place + 1]

    def node_backward(layer):
        grad_branch = v.grad_node[...]
        normed = v.node_normed[layer]
        grad_lifted = branch_back(
            grad_branch, vector(node_v[gain], layer), normed, v.node_scale[layer]
        )
        grad_hidden = contract_cols(grad_lifted, node_v[w_two][layer])
        grad_pre = (grad_hidden * v.node_slope[layer]).astype(bf16)
        aggregate = contract_cols(grad_pre, node_v[w_one][layer, width : 2 * width])
        high = aggregate.astype(bf16)
        low = (aggregate - high.astype(f32)).astype(bf16)
        grad_edge = dot(v.from_targets[...], high) + dot(v.from_targets[...], low)
        if layer + 1 < layers:
            grad_edge = grad_edge + v.grad_edge[...]
        v.grad_edge[...] = grad_edge.astype(bf16).astype(f32)
        grad_node = grad_branch + contract_cols(grad_pre, node_v[w_one][layer, 0:width])
        v.grad_node[...] = grad_node.astype(bf16).astype(f32)
        target = v.node_rights_own.at[layer]
        quarters(target, 0, grad_pre)
        quarters(target, node_dev, grad_lifted)
        quarters(target, 2 * node_dev, column_sums(grad_pre, grad_lifted, grad_branch, normed))
        to_plane(node_rights, layer, (None, lambda s: v.node_rights_own.at[layer, s]))

    def edge_backward(layer):
        grad_branch = v.grad_edge[...]
        normed = v.edge_normed[layer]
        grad_lifted = branch_back(
            grad_branch, vector(edge_v[gain], layer), normed, v.edge_scale[layer]
        )
        grad_hidden = contract_cols(grad_lifted, edge_v[w_two][layer])
        grad_pre = (grad_hidden * v.edge_slope[layer]).astype(bf16)
        sums = dot(v.to_nodes[...], grad_pre).astype(bf16)
        v.sums[layer] = sums.reshape(shards, node_dev, width)
        send_sums(layer)
        target = v.lift_rights_own.at[layer]
        quarters(target, 0, grad_lifted)
        quarters(target, edge_dev, column_sums(grad_pre, grad_lifted, grad_branch, normed))
        quarters(v.pre_rights_own.at[layer], 0, grad_pre)
        to_plane(
            rights,
            layer,
            (
                lambda s: v.pre_rights_own.at[layer, s],
                lambda s: v.lift_rights_own.at[layer, s],
            ),
        )
        grad_edge = grad_branch + contract_cols(grad_pre, edge_v[w_one][layer, 0:width])
        by_target = dot(v.to_targets[...], grad_pre).astype(bf16)
        v.grad_node[...] = v.grad_node[...] + contract_cols(
            by_target, edge_v[w_one][layer, 2 * width : 3 * width]
        )
        if layer > 0:
            v.grad_edge[...] = grad_edge.astype(bf16).astype(f32)
        else:
            v.grad_edges[0] = grad_edge
        return by_target

    def sender_backward(layer, by_target):
        from_rows(v.sums_in, v.sums_recv, layer)
        v.sums_in[layer, row] = v.sums[layer, row]
        by_sender = jnp.sum(v.sums_in[layer].astype(f32), axis=0).astype(bf16)
        target = v.sum_rights_own.at[layer]
        quarters(target, 0, by_sender)
        quarters(target, node_dev, by_target)
        to_plane(sum_rights, layer, (lambda s: v.sum_rights_own.at[layer, s], None))
        grad_node = v.grad_node[...] + contract_cols(
            by_sender, edge_v[w_one][layer, width : 2 * width]
        )
        if layer > 0:
            v.grad_node[...] = grad_node.astype(bf16).astype(f32)
        else:
            v.grad_nodes[0] = grad_node

    loads[5].wait()
    v.grad_node[...] = v.cotangent_v[...].astype(f32)
    for layer in reversed(range(layers)):
        node_backward(layer)
        by_target = edge_backward(layer)
        node_products(layer)
        sender_backward(layer, by_target)
        edge_products(layer)
        add_node_products(layer)
        add_edge_products(layer)

    for layer in range(layers):
        write_outputs(layer)

    for layer in range(layers):
        from_rows(v.nodes, v.nodes_send, layer)
        from_rows(v.sums, v.sums_send, layer)
        plane_left(lefts, layer, (edge_dev, edge_dev))
        plane_left(node_lefts, layer, (node_dev, 3 * node_dev))
        plane_left(node_rights, layer, (0, 2 * node_dev + vector_rows))
        plane_left(rights, layer, (edge_dev, edge_dev + vector_rows))
        plane_left(sum_rights, layer, (2 * node_dev, 0))

        @pl.when(core == 0)
        def _():
            pairs_left(edge_pairs, layer)

        @pl.when(core == 1)
        def _():
            pairs_left(node_pairs, layer)
            pairs_left(lift_pairs, layer)


def copy_kernel(count, *refs):
    for source, target in zip(refs[:count], refs[count:]):
        target[...] = source[...]


def fused(sections, shards, node_features, edge_features, owner, local, receivers, cotangent, *weights):
    micro_count, node_dev, width = node_features.shape
    edge_dev = edge_features.shape[1]
    layers = weights[0].shape[0]
    quarter, pairs, plane = width // sections, shards // 2, 2 * sections
    nodes_total = shards * node_dev

    def shape(*dims, kind=f32):
        return jax.ShapeDtypeStruct(dims, kind)

    def vmem(*dims, kind=bf16):
        return pltpu.VMEM(dims, kind)

    def sems(*dims):
        return pltpu.SemaphoreType.DMA(dims)

    inputs = dict(
        node_features=node_features,
        edge_features=edge_features,
        owner=owner,
        local=local,
        receivers=receivers,
        cotangent=cotangent,
    )
    outputs = dict(
        final=shape(1, node_dev, width, kind=bf16),
        grad_nodes=shape(1, node_dev, width),
        grad_edges=shape(1, edge_dev, width),
    )
    weight_grads = [
        shape(layers, weight.shape[1] // shards, *weight.shape[2:]) for weight in weights
    ]
    blank = SimpleNamespace(
        load_sem=sems(14 + 4 * layers),
        owner_v=vmem(1, edge_dev, kind=jnp.int32),
        local_v=vmem(1, edge_dev, kind=jnp.int32),
        receivers_v=vmem(1, edge_dev, kind=jnp.int32),
        cotangent_v=vmem(node_dev, width),
        from_nodes=vmem(edge_dev, nodes_total),
        to_nodes=vmem(nodes_total, edge_dev),
        from_targets=vmem(edge_dev, node_dev),
        to_targets=vmem(node_dev, edge_dev),
        work=vmem(edge_dev, width, kind=f32),
        grad_node=vmem(node_dev, width, kind=f32),
        grad_edge=vmem(edge_dev, width, kind=f32),
        product=vmem(3 * width, quarter, kind=f32),
        edge_in=vmem(layers, edge_dev, width),
        edge_hidden=vmem(layers, edge_dev, width),
        edge_slope=vmem(layers, edge_dev, width, kind=f32),
        edge_normed=vmem(layers, edge_dev, width, kind=f32),
        edge_scale=vmem(layers, edge_dev, 1, kind=f32),
        node_slope=vmem(layers, node_dev, width, kind=f32),
        node_normed=vmem(layers, node_dev, width, kind=f32),
        node_scale=vmem(layers, node_dev, 1, kind=f32),
        nodes=vmem(layers, shards, node_dev, width),
        nodes_send=sems(layers, shards),
        nodes_recv=sems(layers, shards),
        sums=vmem(layers, shards, node_dev, width),
        sums_in=vmem(layers, shards, node_dev, width),
        sums_send=sems(layers, shards),
        sums_recv=sems(layers, shards),
        lefts=vmem(layers, plane, edge_dev, width),
        lefts_send=sems(layers, plane),
        lefts_recv=sems(layers, plane),
        pre_rights_own=vmem(layers, sections, edge_dev, quarter),
        lift_rights_own=vmem(layers, sections, edge_dev + vector_rows, quarter),
        rights=vmem(layers, plane, edge_dev + vector_rows, quarter),
        rights_send=sems(layers, plane),
        rights_recv=sems(layers, plane),
        node_lefts_own=vmem(layers, 3 * node_dev, width),
        node_lefts=vmem(layers, plane, 3 * node_dev, width),
        node_lefts_send=sems(layers, plane),
        node_lefts_recv=sems(layers, plane),
        node_rights_own=vmem(layers, sections, 2 * node_dev + vector_rows, quarter),
        node_rights=vmem(layers, plane, 2 * node_dev + vector_rows, quarter),
        node_rights_send=sems(layers, plane),
        node_rights_recv=sems(layers, plane),
        sum_rights_own=vmem(layers, sections, 2 * node_dev, quarter),
        sum_rights=vmem(layers, plane, 2 * node_dev, quarter),
        sum_rights_send=sems(layers, plane),
        sum_rights_recv=sems(layers, plane),
    )
    scratch = vars(blank)
    lift_block = whole_tiles(width // shards) + vector_rows
    pair_groups = []
    for block in (
        whole_tiles(3 * width // shards),
        lift_block,
        whole_tiles(2 * width // shards) + lift_block,
    ):
        pair_groups += [
            vmem(layers, pairs, 2, block, quarter),
            vmem(layers, pairs, 2, block, quarter),
            sems(layers, pairs),
            sems(layers, pairs),
            vmem(layers, 2, block, quarter),
            vmem(layers, sections, block, quarter),
            sems(layers, plane),
            sems(layers, sections),
        ]
    weights_v = [pltpu.VMEM(weight.shape, weight.dtype) for weight in weights]
    out_shape = list(outputs.values()) + weight_grads
    ins = len(inputs) + len(weights)
    outs = ins + len(out_shape)
    plan = SimpleNamespace(
        names=list(inputs)
        + list(range(len(weights)))
        + list(outputs)
        + list(range(len(weights)))
        + list(scratch),
        weights=len(inputs),
        grads=ins + len(outputs),
        pair_groups=outs + len(scratch),
        weights_v=outs + len(scratch) + len(pair_groups),
        layers=layers,
        sections=sections,
        shards=shards,
        node_dev=node_dev,
        edge_dev=edge_dev,
        width=width,
    )
    plan.names = [str(name) for name in plan.names]
    results = pl.pallas_call(
        functools.partial(kernel, plan),
        out_shape=out_shape,
        in_specs=[pl.BlockSpec(memory_space=pltpu.HBM)] * ins,
        out_specs=[pl.BlockSpec(memory_space=pltpu.VMEM)] * len(out_shape),
        scratch_shapes=list(scratch.values()) + pair_groups + weights_v,
        compiler_params=pltpu.CompilerParams(
            collective_id=0, has_side_effects=True, vmem_limit_bytes=60 << 20
        ),
    )(*inputs.values(), *weights)
    return pl.pallas_call(
        functools.partial(copy_kernel, len(out_shape)),
        out_shape=out_shape,
        in_specs=[pl.BlockSpec(memory_space=pltpu.VMEM)] * len(out_shape),
        out_specs=[pl.BlockSpec(memory_space=pltpu.VMEM)] * len(out_shape),
    )(*results)


def solution(mesh):
    sections, shards = mesh.shape["section"], mesh.shape["rows"]

    def body(node_features, edge_features, owner, *rest):
        owner = owner.reshape(owner.shape[:-1])
        return fused(sections, shards, node_features, edge_features, owner, *rest)

    in_specs = (
        P(None, "rows", None),
        P(None, "rows", None),
        P(None, "rows", None, None),
        P(None, "rows", None),
        P(None, "rows", None),
        P(None, "rows", None),
    ) + (P(),) * 12
    state = P("section", "rows", None)
    matrix, vector = P(None, "rows", None), P(None, "rows")
    out_specs = (state,) * 3 + (matrix, vector, matrix, vector, vector, vector) * 2
    return jax.shard_map(body, mesh=mesh, in_specs=in_specs, out_specs=out_specs, check_vma=False)
```

```python
import functools
from types import SimpleNamespace

import jax
import jax.numpy as jnp
from jax import lax
from jax.experimental import pallas as pl
from jax.experimental.pallas import tpu as pltpu
from jax.sharding import PartitionSpec as P

f32 = jnp.float32
bf16 = jnp.bfloat16
MESH = pl.DeviceIdType.MESH
norm_epsilon = 1e-05
vector_rows = 16
w_one, b_one, w_two, b_two, gain, shift = range(6)


def dot(left, right):
    return jnp.dot(left, right, preferred_element_type=f32)


def contract_rows(left, right):
    return lax.dot_general(left, right, (((0,), (0,)), ((), ())), preferred_element_type=f32)


def contract_cols(left, right):
    return lax.dot_general(left, right, (((1,), (1,)), ((), ())), preferred_element_type=f32)


def whole_tiles(rows):
    return -(-rows // 16) * 16


def each(count, visit):
    if count <= 8:
        for i in range(count):
            visit(i)
    else:

        def step(i, carry):
            visit(i)
            return carry

        lax.fori_loop(0, count, step, 0)


def layer_norm(lifted):
    center = lifted - jnp.mean(lifted, axis=-1, keepdims=True)
    scale = lax.rsqrt(jnp.mean(center * center, axis=-1, keepdims=True) + norm_epsilon)
    return center * scale, scale


def activate(pre):
    sigma = jax.nn.sigmoid(pre)
    return (pre * sigma).astype(bf16), sigma * (1.0 + pre * (1.0 - sigma))


def branch_back(grad_branch, gain_row, normed, scale):
    grad_normed = grad_branch * gain_row
    return (
        scale
        * (
            grad_normed
            - jnp.mean(grad_normed, axis=-1, keepdims=True)
            - normed * jnp.mean(grad_normed * normed, axis=-1, keepdims=True)
        )
    ).astype(bf16)


def column_sums(grad_pre, grad_lifted, grad_branch, normed):
    rows = [
        jnp.sum(grad_pre.astype(f32), axis=0, keepdims=True),
        jnp.sum(grad_lifted.astype(f32), axis=0, keepdims=True),
        jnp.sum(grad_branch * normed, axis=0, keepdims=True),
        jnp.sum(grad_branch, axis=0, keepdims=True),
    ]
    rows.append(jnp.zeros((vector_rows - 4, grad_branch.shape[1]), f32))
    return jnp.concatenate(rows, axis=0).astype(bf16)


def send(source, target, send_sem, recv_sem, device):
    pltpu.make_async_remote_copy(
        src_ref=source,
        dst_ref=target,
        send_sem=send_sem,
        recv_sem=recv_sem,
        device_id=device,
        device_id_type=MESH,
    ).start()


def ended(buffer, sem):
    pltpu.make_async_copy(buffer, buffer, sem).wait()


def kernel(plan, *refs):
    v = SimpleNamespace(**dict(zip(plan.names, refs)))
    layers, sections, shards = plan.layers, plan.sections, plan.shards
    node_dev, edge_dev, width = plan.node_dev, plan.edge_dev, plan.width
    quarter, pairs, plane = width // sections, shards // 2, 2 * sections
    nodes_total = shards * node_dev
    three_rows, two_rows, one_rows = (part * width // shards for part in (3, 2, 1))
    edge_weights, node_weights = refs[plan.weights : plan.weights + 6], refs[
        plan.weights + 6 : plan.weights + 12
    ]
    edge_v, node_v = refs[plan.weights_v : plan.weights_v + 6], refs[
        plan.weights_v + 6 : plan.weights_v + 12
    ]
    section, row = lax.axis_index("section"), lax.axis_index("rows")
    pair, core = row // 2, row % 2
    plane_slot = section * 2 + core

    def group(data, send_sem, recv_sem):
        return SimpleNamespace(data=data, send=send_sem, recv=recv_sem)

    def pair_group(place, full, own, come, send_sem, recv_sem, total, full_send, full_recv):
        return SimpleNamespace(
            place=place,
            own=own,
            come=come,
            send=send_sem,
            recv=recv_sem,
            total=total,
            full=full,
            full_send=full_send,
            full_recv=full_recv,
        )

    node_lefts = group(v.node_lefts, v.node_lefts_send, v.node_lefts_recv)
    node_rights = group(v.node_rights, v.node_rights_send, v.node_rights_recv)
    sum_rights = group(v.sum_rights, v.sum_rights_send, v.sum_rights_recv)
    edge_pairs, lift_pairs, node_pairs = (
        pair_group(
            place,
            refs[plan.fulls + place],
            *refs[plan.pair_groups + 7 * place : plan.pair_groups + 7 * place + 7],
        )
        for place in range(3)
    )

    loads = {}

    def load(key, source, target):
        copy = pltpu.make_async_copy(source, target, v.load_sem.at[len(loads)])
        copy.start()
        loads[key] = copy

    load(0, v.node_features.at[section], v.nodes.at[0, row])
    load(1, v.owner.at[section], v.owner_v)
    load(2, v.local.at[section], v.local_v)
    load(3, v.receivers.at[section], v.receivers_v)
    load(4, v.edge_features.at[section], v.edge_in.at[0])
    for kind in (b_one, b_two, gain, shift):
        load((0, kind), edge_weights[kind], edge_v[kind])
        load((1, kind), node_weights[kind], node_v[kind])
    for layer in range(layers):
        for kind in (w_one, w_two):
            load((0, kind, layer), edge_weights[kind].at[layer], edge_v[kind].at[layer])
        for kind in (w_one, w_two):
            load((1, kind, layer), node_weights[kind].at[layer], node_v[kind].at[layer])
    load(5, v.cotangent.at[section], v.cotangent_v)

    barrier = pltpu.get_barrier_semaphore()

    def greet(device):
        pl.semaphore_signal(barrier, inc=1, device_id=device, device_id_type=MESH)

    each(shards - 1, lambda i: greet((section, (row + 1 + i) % shards)))
    for step in range(1, sections):
        for other in range(2):
            greet(((section + step) % sections, pair * 2 + other))

    def peer_rows(visit):
        each(shards - 1, lambda i: visit((row + 1 + i) % shards))

    def send_nodes(layer, source):
        def one(peer):
            send(
                source,
                v.nodes.at[layer, row],
                v.nodes_send.at[layer, peer],
                v.nodes_recv.at[layer, row],
                (section, peer),
            )

        peer_rows(one)

    def send_sums(layer):
        def one(peer):
            send(
                v.sums.at[layer, peer],
                v.sums_in.at[layer, row],
                v.sums_send.at[layer, peer],
                v.sums_recv.at[layer, row],
                (section, peer),
            )

        peer_rows(one)

    def from_rows(data, sem, layer):
        peer_rows(lambda peer: ended(data.at[layer, peer], sem.at[layer, peer]))

    def to_plane(group, layer, sources):
        def one(target_section, other):
            source = sources[other](target_section)
            send(
                source,
                group.data.at[layer, plane_slot, pl.ds(0, source.shape[0])],
                group.send.at[layer, target_section * 2 + other],
                group.recv.at[layer, plane_slot],
                (target_section, pair * 2 + other),
            )

        for step in range(1, sections):
            for other in range(2):
                if sources[other] is not None:
                    one((section + step) % sections, other)
        for other in range(2):
            if sources[other] is None:
                continue

            @pl.when(core != other)
            def _(other=other):
                one(section, other)

            @pl.when(core == other)
            def _(other=other):
                source = sources[other](section)
                group.data[layer, plane_slot, 0 : source.shape[0]] = source[...]

    def from_plane(group, layer, rows):
        for step in range(1, plane):
            slot = (plane_slot + step) % plane
            ended(group.data.at[layer, slot, pl.ds(0, rows)], group.recv.at[layer, slot])

    def plane_left(group, layer, rows):
        def one(target_section, other):
            ended(
                group.data.at[layer, 0, pl.ds(0, rows[other])],
                group.send.at[layer, target_section * 2 + other],
            )

        for other in range(2):
            if rows[other]:
                for step in range(1, sections):
                    one((section + step) % sections, other)
                pl.when(core != other)(functools.partial(one, section, other))

    def to_mate(taker, buffer, send_sem, recv_sem, source):
        @pl.when(core != taker)
        def _():
            send(
                source,
                buffer.at[pl.ds(0, source.shape[0])],
                send_sem,
                recv_sem,
                (section, row + 1 - 2 * core),
            )

    def to_mate_left(taker, layer, states):
        to_mate(
            taker,
            v.mate_left.at[layer],
            v.mate_left_send.at[layer],
            v.mate_left_recv.at[layer],
            states.at[layer],
        )

    def to_mate_right(taker, layer, source):
        to_mate(
            taker,
            v.mate_right.at[layer],
            v.mate_right_send.at[layer],
            v.mate_right_recv.at[layer],
            source.at[layer],
        )

    def from_mate(layer, rows):
        ended(v.mate_left.at[layer], v.mate_left_recv.at[layer])
        ended(v.mate_right.at[layer, pl.ds(0, rows)], v.mate_right_recv.at[layer])

    def send_parts(layer, rows):
        for step in range(1, sections):
            target = (section + step) % sections
            send(
                v.parts.at[layer, target, pl.ds(0, rows)],
                v.parts_in.at[layer, section, pl.ds(0, rows)],
                v.parts_send.at[layer, target],
                v.parts_recv.at[layer, section],
                (target, row),
            )

    def from_sections(buffer, sem, layer, rows):
        for step in range(1, sections):
            other = (section + step) % sections
            ended(buffer.at[layer, other, pl.ds(0, rows)], sem.at[layer, other])

    def peer_pairs(visit):
        each(pairs - 1, lambda i: visit((pair + 1 + i) % pairs))

    def send_pairs(group, layer):
        def one(peer):
            send(
                group.own.at[layer, peer],
                group.come.at[layer, pair],
                group.send.at[layer, peer],
                group.recv.at[layer, pair],
                (section, peer * 2 + core),
            )

        peer_pairs(one)

    def share(group, layer, target_section, other):
        send(
            group.total.at[layer, other],
            group.full.at[layer, section],
            group.full_send.at[layer, target_section * 2 + other],
            group.full_recv.at[layer, section],
            (target_section, pair * 2 + other),
        )

    def add_pairs(group, layer):
        peer_pairs(lambda peer: ended(group.come.at[layer, peer], group.recv.at[layer, peer]))
        group.come[layer, pair] = group.own[layer, pair]
        total = group.come[layer, 0].astype(f32)
        for peer in range(1, pairs):
            total = total + group.come[layer, peer].astype(f32)
        group.total[layer] = total.astype(bf16)
        for step in range(1, sections):
            for other in range(2):
                share(group, layer, (section + step) % sections, other)
        share(group, layer, section, 1 - core)
        copy = pltpu.make_async_copy(
            group.total.at[layer, core], group.full.at[layer, section], v.own_sem.at[group.place]
        )
        copy.start()
        copy.wait()

    def pairs_left(group, layer):
        peer_pairs(lambda peer: ended(group.own.at[layer, peer], group.send.at[layer, peer]))
        for step in range(1, plane):
            ended(group.total.at[layer, 0], group.full_send.at[layer, (plane_slot + step) % plane])

    def from_givers(group, layer, giver):
        for step in range(1, sections):
            slot = (section + step) % sections
            ended(group.full.at[layer, slot], group.full_recv.at[layer, slot])

        @pl.when(core != giver)
        def _():
            ended(group.full.at[layer, section], group.full_recv.at[layer, section])

    def store_blocks(target, product, offset, rows):
        padded = whole_tiles(rows)
        for owner in range(shards):
            block = product[owner * rows : (owner + 1) * rows]
            if padded != rows:
                block = jnp.concatenate([block, jnp.zeros((padded - rows, quarter), f32)], axis=0)
            target[owner // 2, owner % 2, offset : offset + padded] = block.astype(bf16)

    def store_vectors(target, total, offset):
        for owner in range(shards):
            target[owner // 2, owner % 2, offset : offset + vector_rows] = total.astype(bf16)

    def quarters(target, offset, value):
        rows = value.shape[0]
        for part in range(sections):
            target[part, offset : offset + rows] = value[
                :, part * quarter : (part + 1) * quarter
            ].astype(bf16)

    def write(place, value, staged, target):
        staged[0] = value
        pltpu.make_async_copy(staged, target, v.write_sem.at[place]).start()

    def vector(ref, layer):
        return ref[...].astype(f32)[layer : layer + 1]

    pl.semaphore_wait(barrier, shards - 1 + 2 * (sections - 1))
    send_nodes(0, v.node_features.at[section])
    loads[0].wait()
    loads[4].wait()
    to_mate_left(0, 0, v.edge_in)

    for key in (1, 2, 3):
        loads[key].wait()
    sender_row = v.owner_v[...] * node_dev + v.local_v[...]
    target_row = v.receivers_v[...]
    eye = lax.broadcasted_iota(jnp.int32, (edge_dev, edge_dev), 0) == lax.broadcasted_iota(
        jnp.int32, (edge_dev, edge_dev), 1
    )

    def to_column(values):
        spread = jnp.broadcast_to(values, (edge_dev, edge_dev))
        column = jnp.sum(jnp.where(eye, spread, 0).astype(f32), axis=1, keepdims=True)
        return column.astype(jnp.int32)

    def one_hot(values, count, axis):
        places = (count, edge_dev) if axis == 0 else (edge_dev, count)
        match = lax.broadcasted_iota(jnp.int32, places, axis) == values
        return jnp.where(match, 1.0, 0.0).astype(bf16)

    v.from_nodes[...] = one_hot(to_column(sender_row), nodes_total, 1)
    v.to_nodes[...] = one_hot(sender_row, nodes_total, 0)
    v.from_targets[...] = one_hot(to_column(target_row), node_dev, 1)
    v.to_targets[...] = one_hot(target_row, node_dev, 0)
    for kind in (b_one, b_two, gain, shift):
        loads[(0, kind)].wait()
        loads[(1, kind)].wait()

    def edge_forward(layer):
        node = v.nodes[layer, row]
        edge = v.edge_in[layer]
        loads[(0, w_one, layer)].wait()
        received = dot(v.from_targets[...], node).astype(bf16)
        v.work[...] = (
            dot(edge, edge_v[w_one][layer, 0:width])
            + dot(received, edge_v[w_one][layer, 2 * width : 3 * width])
            + vector(edge_v[b_one], layer)
        )
        from_rows(v.nodes, v.nodes_recv, layer)
        sent = dot(v.from_nodes[...], v.nodes[layer].reshape(nodes_total, width)).astype(bf16)
        hidden, slope = activate(
            v.work[...] + dot(sent, edge_v[w_one][layer, width : 2 * width])
        )
        v.edge_hidden[layer] = hidden
        v.edge_slope[layer] = slope
        to_mate_left(1, layer, v.edge_hidden)
        loads[(0, w_two, layer)].wait()
        normed, scale = layer_norm(
            dot(hidden, edge_v[w_two][layer]) + vector(edge_v[b_two], layer)
        )
        v.edge_normed[layer] = normed
        v.edge_scale[layer] = scale
        edge = (
            edge.astype(f32)
            + (normed * vector(edge_v[gain], layer) + vector(edge_v[shift], layer))
        ).astype(bf16)
        if layer + 1 < layers:
            v.edge_in[layer + 1] = edge
            to_mate_left(0, layer + 1, v.edge_in)
        return node, dot(v.to_targets[...], edge).astype(bf16)

    def node_forward(layer, node, gathered):
        loads[(1, w_one, layer)].wait()
        hidden, slope = activate(
            dot(node, node_v[w_one][layer, 0:width])
            + dot(gathered, node_v[w_one][layer, width : 2 * width])
            + vector(node_v[b_one], layer)
        )
        v.node_slope[layer] = slope
        loads[(1, w_two, layer)].wait()
        normed, scale = layer_norm(
            dot(hidden, node_v[w_two][layer]) + vector(node_v[b_two], layer)
        )
        v.node_normed[layer] = normed
        v.node_scale[layer] = scale
        new_node = (
            node.astype(f32)
            + (normed * vector(node_v[gain], layer) + vector(node_v[shift], layer))
        ).astype(bf16)
        if layer + 1 < layers:
            v.nodes[layer + 1, row] = new_node
            send_nodes(layer + 1, v.nodes.at[layer + 1, row])
        else:
            write(0, new_node, v.final_v, v.final)
        v.node_lefts_own[layer, 0:node_dev] = node
        v.node_lefts_own[layer, node_dev : 2 * node_dev] = gathered
        v.node_lefts_own[layer, 2 * node_dev : 3 * node_dev] = hidden
        to_plane(
            node_lefts,
            layer,
            (
                lambda s: v.node_lefts_own.at[layer, pl.ds(0, node_dev)],
                lambda s: v.node_lefts_own.at[layer],
            ),
        )

    for layer in range(layers):
        node, gathered = edge_forward(layer)
        node_forward(layer, node, gathered)

    def node_products(layer):
        @pl.when(core == 1)
        def _():
            from_plane(node_lefts, layer, 3 * node_dev)
            from_plane(node_rights, layer, 2 * node_dev + vector_rows)
            own = plane * node_dev
            state = v.node_lefts[layer, :, 0:node_dev].reshape(own, width)
            gathered = v.node_lefts[layer, :, node_dev : 2 * node_dev].reshape(own, width)
            hidden = v.node_lefts[layer, :, 2 * node_dev : 3 * node_dev].reshape(own, width)
            grad_pre = v.node_rights[layer, :, 0:node_dev].reshape(own, quarter)
            grad_lifted = v.node_rights[layer, :, node_dev : 2 * node_dev].reshape(own, quarter)
            vectors = v.node_rights[layer, :, 2 * node_dev : 2 * node_dev + vector_rows]
            v.product[0:width] = contract_rows(state, grad_pre)
            v.product[width : 2 * width] = contract_rows(gathered, grad_pre)
            v.product[2 * width : 3 * width] = contract_rows(hidden, grad_lifted)
            target = node_pairs.own.at[layer]
            store_blocks(target, v.product, 0, two_rows)
            start = whole_tiles(two_rows)
            store_blocks(target, v.product.at[pl.ds(2 * width, width)], start, one_rows)
            start += whole_tiles(one_rows)
            store_vectors(target, jnp.sum(vectors.astype(f32), axis=0), start)
            send_pairs(node_pairs, layer)

    def edge_parts(layer):
        def multiply(own_left, own_right):
            left = jnp.concatenate([own_left[layer], v.mate_left[layer]], axis=0)
            right = jnp.concatenate(
                [own_right[layer, 0:edge_dev], v.mate_right[layer, 0:edge_dev]], axis=0
            )
            for part in range(sections):
                columns = slice(part * quarter, (part + 1) * quarter)
                v.parts[layer, part, 0:width] = contract_rows(left, right[:, columns]).astype(bf16)

        @pl.when(core == 0)
        def _():
            from_mate(layer, edge_dev)
            multiply(v.edge_in, v.pre_own)
            send_parts(layer, width)

        @pl.when(core == 1)
        def _():
            from_mate(layer, edge_dev + vector_rows)
            multiply(v.edge_hidden, v.lift_own)
            vectors = (
                v.lift_own[layer, edge_dev : edge_dev + vector_rows].astype(f32)
                + v.mate_right[layer, edge_dev : edge_dev + vector_rows].astype(f32)
            ).astype(bf16)
            for part in range(sections):
                v.parts[layer, part, width : width + vector_rows] = vectors[
                    :, part * quarter : (part + 1) * quarter
                ]
            send_parts(layer, width + vector_rows)

    def add_parts(layer, start, rows):
        total = v.parts[layer, section, start : start + rows].astype(f32)
        for step in range(1, sections):
            other = (section + step) % sections
            total = total + v.parts_in[layer, other, start : start + rows].astype(f32)
        return total

    def edge_products(layer):
        @pl.when(core == 0)
        def _():
            from_plane(node_lefts, layer, node_dev)
            from_plane(sum_rights, layer, 2 * node_dev)
            own_nodes = plane * node_dev
            state = v.node_lefts[layer, :, 0:node_dev].reshape(own_nodes, width)
            for part in range(2):
                start = part * node_dev
                v.product[(1 + part) * width : (2 + part) * width] = contract_rows(
                    state,
                    v.sum_rights[layer, :, start : start + node_dev].reshape(own_nodes, quarter),
                )
            from_sections(v.parts_in, v.parts_recv, layer, width)
            v.product[0:width] = add_parts(layer, 0, width)
            store_blocks(edge_pairs.own.at[layer], v.product, 0, three_rows)
            send_pairs(edge_pairs, layer)

        @pl.when(core == 1)
        def _():
            from_sections(v.parts_in, v.parts_recv, layer, width + vector_rows)
            v.product[0:width] = add_parts(layer, 0, width)
            target = lift_pairs.own.at[layer]
            store_blocks(target, v.product, 0, one_rows)
            store_vectors(target, add_parts(layer, width, vector_rows), whole_tiles(one_rows))
            send_pairs(lift_pairs, layer)

    def add_node_products(layer):
        pl.when(core == 1)(lambda: add_pairs(node_pairs, layer))

    def add_edge_products(layer):
        pl.when(core == 0)(lambda: add_pairs(edge_pairs, layer))
        pl.when(core == 1)(lambda: add_pairs(lift_pairs, layer))

    def node_backward(layer):
        grad_branch = v.grad_node[...]
        normed = v.node_normed[layer]
        grad_lifted = branch_back(
            grad_branch, vector(node_v[gain], layer), normed, v.node_scale[layer]
        )
        grad_hidden = contract_cols(grad_lifted, node_v[w_two][layer])
        grad_pre = (grad_hidden * v.node_slope[layer]).astype(bf16)
        aggregate = contract_cols(grad_pre, node_v[w_one][layer, width : 2 * width])
        high = aggregate.astype(bf16)
        low = (aggregate - high.astype(f32)).astype(bf16)
        grad_edge = dot(v.from_targets[...], high) + dot(v.from_targets[...], low)
        if layer + 1 < layers:
            grad_edge = grad_edge + v.grad_edge[...]
        v.grad_edge[...] = grad_edge.astype(bf16).astype(f32)
        grad_node = grad_branch + contract_cols(grad_pre, node_v[w_one][layer, 0:width])
        v.grad_node[...] = grad_node.astype(bf16).astype(f32)
        target = v.node_rights_own.at[layer]
        quarters(target, 0, grad_pre)
        quarters(target, node_dev, grad_lifted)
        quarters(target, 2 * node_dev, column_sums(grad_pre, grad_lifted, grad_branch, normed))
        to_plane(node_rights, layer, (None, lambda s: v.node_rights_own.at[layer, s]))

    def edge_backward(layer):
        grad_branch = v.grad_edge[...]
        normed = v.edge_normed[layer]
        grad_lifted = branch_back(
            grad_branch, vector(edge_v[gain], layer), normed, v.edge_scale[layer]
        )
        grad_hidden = contract_cols(grad_lifted, edge_v[w_two][layer])
        grad_pre = (grad_hidden * v.edge_slope[layer]).astype(bf16)
        sums = dot(v.to_nodes[...], grad_pre).astype(bf16)
        v.sums[layer] = sums.reshape(shards, node_dev, width)
        send_sums(layer)
        v.pre_own[layer] = grad_pre
        v.lift_own[layer, 0:edge_dev] = grad_lifted
        v.lift_own[layer, edge_dev : edge_dev + vector_rows] = column_sums(
            grad_pre, grad_lifted, grad_branch, normed
        )
        to_mate_right(0, layer, v.pre_own)
        to_mate_right(1, layer, v.lift_own)
        grad_edge = grad_branch + contract_cols(grad_pre, edge_v[w_one][layer, 0:width])
        by_target = dot(v.to_targets[...], grad_pre).astype(bf16)
        v.grad_node[...] = v.grad_node[...] + contract_cols(
            by_target, edge_v[w_one][layer, 2 * width : 3 * width]
        )
        if layer > 0:
            v.grad_edge[...] = grad_edge.astype(bf16).astype(f32)
        else:
            write(1, grad_edge, v.grad_edges_v, v.grad_edges)
        return by_target

    def sender_backward(layer, by_target):
        from_rows(v.sums_in, v.sums_recv, layer)
        v.sums_in[layer, row] = v.sums[layer, row]
        by_sender = jnp.sum(v.sums_in[layer].astype(f32), axis=0).astype(bf16)
        target = v.sum_rights_own.at[layer]
        quarters(target, 0, by_sender)
        quarters(target, node_dev, by_target)
        to_plane(sum_rights, layer, (lambda s: v.sum_rights_own.at[layer, s], None))
        grad_node = v.grad_node[...] + contract_cols(
            by_sender, edge_v[w_one][layer, width : 2 * width]
        )
        if layer > 0:
            v.grad_node[...] = grad_node.astype(bf16).astype(f32)
        else:
            write(2, grad_node, v.grad_nodes_v, v.grad_nodes)

    loads[5].wait()
    v.grad_node[...] = v.cotangent_v[...].astype(f32)
    for layer in reversed(range(layers)):
        node_backward(layer)
        by_target = edge_backward(layer)
        if layer + 1 < layers:
            edge_products(layer + 1)
        edge_parts(layer)
        node_products(layer)
        sender_backward(layer, by_target)
        if layer + 1 < layers:
            add_node_products(layer + 1)
            add_edge_products(layer + 1)
    edge_products(0)
    add_node_products(0)
    add_edge_products(0)

    for place, (staged, target) in enumerate(
        ((v.final_v, v.final), (v.grad_edges_v, v.grad_edges), (v.grad_nodes_v, v.grad_nodes))
    ):
        pltpu.make_async_copy(staged, target, v.write_sem.at[place]).wait()
    for layer in range(layers):
        from_givers(edge_pairs, layer, 0)
        from_givers(lift_pairs, layer, 1)
        from_givers(node_pairs, layer, 1)
        from_rows(v.nodes, v.nodes_send, layer)
        from_rows(v.sums, v.sums_send, layer)
        plane_left(node_lefts, layer, (node_dev, 3 * node_dev))
        plane_left(node_rights, layer, (0, 2 * node_dev + vector_rows))
        plane_left(sum_rights, layer, (2 * node_dev, 0))
        ended(v.mate_left.at[layer], v.mate_left_send.at[layer])

        @pl.when(core == 0)
        def _():
            ended(v.mate_right.at[layer], v.mate_right_send.at[layer])
            from_sections(v.parts, v.parts_send, layer, width)
            pairs_left(edge_pairs, layer)

        @pl.when(core == 1)
        def _():
            ended(v.mate_right.at[layer, pl.ds(0, edge_dev)], v.mate_right_send.at[layer])
            from_sections(v.parts, v.parts_send, layer, width + vector_rows)
            pairs_left(node_pairs, layer)
            pairs_left(lift_pairs, layer)


def write_kernel(shards, *refs):
    final, grad_nodes, grad_edges, edge_full, lift_full, node_full = refs[:6]
    out_final, out_nodes, out_edges = refs[6:9]
    grads = refs[9:]
    row = lax.axis_index("rows")
    layers, sections, quarter = edge_full.shape[0], edge_full.shape[1], edge_full.shape[3]
    width = sections * quarter
    three_rows, two_rows, one_rows = (part * width // shards for part in (3, 2, 1))
    node_start = whole_tiles(two_rows)
    out_final[...] = final[...]
    out_nodes[...] = grad_nodes[...]
    out_edges[...] = grad_edges[...]

    def put(target, full, start, rows):
        for layer in range(layers):
            for part in range(sections):
                value = full[layer, part, start : start + whole_tiles(rows)]
                target[layer, :, part * quarter : (part + 1) * quarter] = value.astype(f32)[0:rows]

    put(grads[w_one], edge_full, 0, three_rows)
    put(grads[w_two], lift_full, 0, one_rows)
    put(grads[6 + w_one], node_full, 0, two_rows)
    put(grads[6 + w_two], node_full, node_start, one_rows)

    def take_columns(value):
        per = quarter // one_rows
        taken = jnp.zeros((vector_rows, one_rows), f32)
        for place in range(per):
            taken = taken + jnp.where(
                row % per == place, value[:, place * one_rows : (place + 1) * one_rows], 0.0
            )
        return taken

    holder = row // (quarter // one_rows)
    for layer in range(layers):
        for first, full, start in (
            (0, lift_full, whole_tiles(one_rows)),
            (6, node_full, node_start + whole_tiles(one_rows)),
        ):
            vectors = take_columns(full[layer, holder, start : start + vector_rows].astype(f32))
            for place, kind in enumerate((b_one, b_two, gain, shift)):
                grads[first + kind][layer : layer + 1] = vectors[place : place + 1]


def fused(sections, shards, node_features, edge_features, owner, local, receivers, cotangent, *weights):
    micro_count, node_dev, width = node_features.shape
    edge_dev = edge_features.shape[1]
    layers = weights[0].shape[0]
    quarter, pairs, plane = width // sections, shards // 2, 2 * sections
    nodes_total = shards * node_dev

    def shape(*dims, kind=f32):
        return jax.ShapeDtypeStruct(dims, kind)

    def vmem(*dims, kind=bf16):
        return pltpu.VMEM(dims, kind)

    def sems(*dims):
        return pltpu.SemaphoreType.DMA(dims)

    inputs = dict(
        node_features=node_features,
        edge_features=edge_features,
        owner=owner,
        local=local,
        receivers=receivers,
        cotangent=cotangent,
    )
    outputs = dict(
        final=shape(1, node_dev, width, kind=bf16),
        grad_nodes=shape(1, node_dev, width),
        grad_edges=shape(1, edge_dev, width),
    )
    weight_grads = [
        shape(layers, weight.shape[1] // shards, *weight.shape[2:]) for weight in weights
    ]
    lift_block = whole_tiles(width // shards) + vector_rows
    blocks = (
        whole_tiles(3 * width // shards),
        lift_block,
        whole_tiles(2 * width // shards) + lift_block,
    )
    fulls = [shape(layers, sections, block, quarter, kind=bf16) for block in blocks]
    blank = SimpleNamespace(
        load_sem=sems(14 + 4 * layers),
        owner_v=vmem(1, edge_dev, kind=jnp.int32),
        local_v=vmem(1, edge_dev, kind=jnp.int32),
        receivers_v=vmem(1, edge_dev, kind=jnp.int32),
        cotangent_v=vmem(node_dev, width),
        from_nodes=vmem(edge_dev, nodes_total),
        to_nodes=vmem(nodes_total, edge_dev),
        from_targets=vmem(edge_dev, node_dev),
        to_targets=vmem(node_dev, edge_dev),
        work=vmem(edge_dev, width, kind=f32),
        grad_node=vmem(node_dev, width, kind=f32),
        grad_edge=vmem(edge_dev, width, kind=f32),
        product=vmem(3 * width, quarter, kind=f32),
        edge_in=vmem(layers, edge_dev, width),
        edge_hidden=vmem(layers, edge_dev, width),
        edge_slope=vmem(layers, edge_dev, width, kind=f32),
        edge_normed=vmem(layers, edge_dev, width, kind=f32),
        edge_scale=vmem(layers, edge_dev, 1, kind=f32),
        node_slope=vmem(layers, node_dev, width, kind=f32),
        node_normed=vmem(layers, node_dev, width, kind=f32),
        node_scale=vmem(layers, node_dev, 1, kind=f32),
        nodes=vmem(layers, shards, node_dev, width),
        nodes_send=sems(layers, shards),
        nodes_recv=sems(layers, shards),
        sums=vmem(layers, shards, node_dev, width),
        sums_in=vmem(layers, shards, node_dev, width),
        sums_send=sems(layers, shards),
        sums_recv=sems(layers, shards),
        final_v=vmem(1, node_dev, width),
        grad_nodes_v=vmem(1, node_dev, width, kind=f32),
        grad_edges_v=vmem(1, edge_dev, width, kind=f32),
        write_sem=sems(3),
        own_sem=sems(3),
        mate_left=vmem(layers, edge_dev, width),
        mate_left_send=sems(layers),
        mate_left_recv=sems(layers),
        mate_right=vmem(layers, edge_dev + vector_rows, width),
        mate_right_send=sems(layers),
        mate_right_recv=sems(layers),
        pre_own=vmem(layers, edge_dev, width),
        lift_own=vmem(layers, edge_dev + vector_rows, width),
        parts=vmem(layers, sections, width + vector_rows, quarter),
        parts_in=vmem(layers, sections, width + vector_rows, quarter),
        parts_send=sems(layers, sections),
        parts_recv=sems(layers, sections),
        node_lefts_own=vmem(layers, 3 * node_dev, width),
        node_lefts=vmem(layers, plane, 3 * node_dev, width),
        node_lefts_send=sems(layers, plane),
        node_lefts_recv=sems(layers, plane),
        node_rights_own=vmem(layers, sections, 2 * node_dev + vector_rows, quarter),
        node_rights=vmem(layers, plane, 2 * node_dev + vector_rows, quarter),
        node_rights_send=sems(layers, plane),
        node_rights_recv=sems(layers, plane),
        sum_rights_own=vmem(layers, sections, 2 * node_dev, quarter),
        sum_rights=vmem(layers, plane, 2 * node_dev, quarter),
        sum_rights_send=sems(layers, plane),
        sum_rights_recv=sems(layers, plane),
    )
    scratch = vars(blank)
    pair_groups = []
    for block in blocks:
        pair_groups += [
            vmem(layers, pairs, 2, block, quarter),
            vmem(layers, pairs, 2, block, quarter),
            sems(layers, pairs),
            sems(layers, pairs),
            vmem(layers, 2, block, quarter),
            sems(layers, plane),
            sems(layers, sections),
        ]
    weights_v = [pltpu.VMEM(weight.shape, weight.dtype) for weight in weights]
    ins, outs = len(inputs) + len(weights), len(outputs) + len(fulls)
    names = (
        list(inputs)
        + list(range(len(weights)))
        + list(outputs)
        + list(range(len(fulls)))
        + list(scratch)
    )
    plan = SimpleNamespace(
        names=[str(name) for name in names],
        weights=len(inputs),
        fulls=ins + len(outputs),
        pair_groups=ins + outs + len(scratch),
        weights_v=ins + outs + len(scratch) + len(pair_groups),
        layers=layers,
        sections=sections,
        shards=shards,
        node_dev=node_dev,
        edge_dev=edge_dev,
        width=width,
    )
    results = pl.pallas_call(
        functools.partial(kernel, plan),
        out_shape=list(outputs.values()) + fulls,
        in_specs=[pl.BlockSpec(memory_space=pltpu.HBM)] * ins,
        out_specs=[pl.BlockSpec(memory_space=pltpu.HBM)] * outs,
        scratch_shapes=list(scratch.values()) + pair_groups + weights_v,
        compiler_params=pltpu.CompilerParams(
            collective_id=0, has_side_effects=True, vmem_limit_bytes=60 << 20
        ),
    )(*inputs.values(), *weights)
    return pl.pallas_call(
        functools.partial(write_kernel, shards),
        out_shape=list(outputs.values()) + weight_grads,
        in_specs=[pl.BlockSpec(memory_space=pltpu.VMEM)] * outs,
        out_specs=[pl.BlockSpec(memory_space=pltpu.VMEM)] * (len(outputs) + len(weight_grads)),
    )(*results)


def solution(mesh):
    sections, shards = mesh.shape["section"], mesh.shape["rows"]

    def body(node_features, edge_features, owner, *rest):
        owner = owner.reshape(owner.shape[:-1])
        return fused(sections, shards, node_features, edge_features, owner, *rest)

    in_specs = (
        P(None, "rows", None),
        P(None, "rows", None),
        P(None, "rows", None, None),
        P(None, "rows", None),
        P(None, "rows", None),
        P(None, "rows", None),
    ) + (P(),) * 12
    state = P("section", "rows", None)
    matrix, vector = P(None, "rows", None), P(None, "rows")
    out_specs = (state,) * 3 + (matrix, vector, matrix, vector, vector, vector) * 2
    return jax.shard_map(body, mesh=mesh, in_specs=in_specs, out_specs=out_specs, check_vma=False)
```

```python
import functools
from types import SimpleNamespace

import jax
import jax.numpy as jnp
import numpy as np
from jax import lax
from jax.experimental import pallas as pl
from jax.experimental.pallas import tpu as pltpu
from jax.sharding import PartitionSpec as P

f32 = jnp.float32
bf16 = jnp.bfloat16
MESH = pl.DeviceIdType.MESH
norm_epsilon = 1e-05
vector_rows = 16
e_one, e_bias_one, e_two, e_bias_two, e_gain, e_shift = range(6)
n_one, n_bias_one, n_two, n_bias_two, n_gain, n_shift = range(6, 12)
matrix_kinds = (e_one, e_two, n_one, n_two)
vector_kinds = (e_bias_one, e_bias_two, e_gain, e_shift, n_bias_one, n_bias_two, n_gain, n_shift)
lanes = 128


def dot(left, right):
    return jnp.dot(left, right, preferred_element_type=f32)


def contract_rows(left, right):
    return lax.dot_general(left, right, (((0,), (0,)), ((), ())), preferred_element_type=f32)


def contract_cols(left, right):
    return lax.dot_general(left, right, (((1,), (1,)), ((), ())), preferred_element_type=f32)


def whole_tiles(rows):
    return -(-rows // 16) * 16


def layer_norm(lifted):
    center = lifted - jnp.mean(lifted, axis=-1, keepdims=True)
    scale = lax.rsqrt(jnp.mean(center * center, axis=-1, keepdims=True) + norm_epsilon)
    return center * scale, scale


def activate(pre):
    sigma = jax.nn.sigmoid(pre)
    return (pre * sigma).astype(bf16), sigma * (1.0 + pre * (1.0 - sigma))


def branch_back(grad_branch, gain_row, normed, scale):
    grad_normed = grad_branch * gain_row
    return (
        scale
        * (
            grad_normed
            - jnp.mean(grad_normed, axis=-1, keepdims=True)
            - normed * jnp.mean(grad_normed * normed, axis=-1, keepdims=True)
        )
    ).astype(bf16)


def column_sums(grad_pre, grad_lifted, grad_branch, normed):
    rows = [
        jnp.sum(grad_pre.astype(f32), axis=0, keepdims=True),
        jnp.sum(grad_lifted.astype(f32), axis=0, keepdims=True),
        jnp.sum(grad_branch * normed, axis=0, keepdims=True),
        jnp.sum(grad_branch, axis=0, keepdims=True),
    ]
    rows.append(jnp.zeros((vector_rows - 4, grad_branch.shape[1]), f32))
    return jnp.concatenate(rows, axis=0).astype(bf16)


def ended(buffer, sem):
    pltpu.make_async_copy(buffer, buffer, sem).wait()


def kernel(plan, *refs):
    v = SimpleNamespace(**dict(zip(plan.names, refs)))
    layers, sections, shards = plan.layers, plan.sections, plan.shards
    node_dev, edge_dev, width = plan.node_dev, plan.edge_dev, plan.width
    quarter, pairs, plane = width // sections, shards // 2, 2 * sections
    nodes_total = shards * node_dev
    three_rows, two_rows, one_rows = (part * width // shards for part in (3, 2, 1))
    weights = refs[plan.weights : plan.weights + 12]
    section, row = lax.axis_index("section"), lax.axis_index("rows")
    pair, core = row // 2, row % 2
    plane_slot = section * 2 + core
    edge_pairs, lift_pairs, node_pairs = (
        SimpleNamespace(
            full=refs[plan.fulls + place],
            **dict(zip(plan.pair_names, refs[plan.pair_groups + 5 * place :])),
        )
        for place in range(3)
    )
    node_lefts = SimpleNamespace(data=v.node_lefts, recv=v.node_lefts_recv)
    node_rights = SimpleNamespace(data=v.node_rights, recv=v.node_rights_recv)
    sum_rights = SimpleNamespace(data=v.sum_rights, recv=v.sum_rights_recv)

    def drained(count, sem):
        ended(v.drain.at[pl.ds(0, count // lanes)], sem)

    started = SimpleNamespace(total=[0, 0], cores=(0, 1), times=1)

    def count_start(source):
        for one in started.cores:
            started.total[one] += started.times * source.size * source.dtype.itemsize // 2

    def send(source, target, recv_sem, device):
        count_start(source)
        pltpu.make_async_remote_copy(
            src_ref=source,
            dst_ref=target,
            send_sem=v.done,
            recv_sem=recv_sem,
            device_id=device,
            device_id_type=MESH,
        ).start()

    def write(source, target):
        count_start(source)
        pltpu.make_async_copy(source, target, v.done).start()

    def on_core(one, act):
        before = started.cores
        started.cores = tuple(x for x in before if x == one)
        pl.when(core == one)(act)
        started.cores = before

    def each(count, visit):
        if count <= 8:
            for i in range(count):
                visit(i)
        else:
            before = started.times

            def step(i, carry):
                started.times = before * count
                visit(i)
                started.times = before
                return carry

            lax.fori_loop(0, count, step, 0)

    barrier = pltpu.get_barrier_semaphore()

    def greet(device):
        pl.semaphore_signal(barrier, inc=1, device_id=device, device_id_type=MESH)

    each(shards - 1, lambda i: greet((section, (row + 1 + i) % shards)))
    for step in range(1, sections):
        for other in range(2):
            greet(((section + step) % sections, pair * 2 + other))

    def peer_rows(visit):
        each(shards - 1, lambda i: visit((row + 1 + i) % shards))

    def send_nodes(layer, source):
        def one(peer):
            send(source, v.nodes.at[layer, row], v.nodes_recv.at[layer], (section, peer))

        peer_rows(one)

    def send_sums(layer):
        def one(peer):
            send(
                v.sums.at[layer, peer],
                v.sums_in.at[layer, row],
                v.sums_recv.at[layer],
                (section, peer),
            )

        peer_rows(one)

    def from_rows(data, sem, layer):
        ended(data.at[layer, pl.ds(0, shards - 1)], sem.at[layer])

    def to_plane(group, layer, sources):
        def one(target_section, other):
            source = sources[other](target_section)
            send(
                source,
                group.data.at[layer, plane_slot, pl.ds(0, source.shape[0])],
                group.recv.at[layer],
                (target_section, pair * 2 + other),
            )

        def keep(other):
            source = sources[other](section)
            group.data[layer, plane_slot, 0 : source.shape[0]] = source[...]

        for other in range(2):
            if sources[other] is not None:
                for step in range(1, sections):
                    one((section + step) % sections, other)
                on_core(1 - other, functools.partial(one, section, other))
                on_core(other, functools.partial(keep, other))

    def from_plane(group, layer, rows):
        drained((plane - 1) * rows * group.data.shape[-1], group.recv.at[layer])

    def to_mate(taker, target, recv_sem, source):
        target = target.at[pl.ds(0, source.shape[0])]
        mate = (section, row + 1 - 2 * core)
        on_core(1 - taker, lambda: send(source, target, recv_sem, mate))

    def send_parts(layer, rows):
        for step in range(1, sections):
            target = (section + step) % sections
            send(
                v.parts.at[layer, target, pl.ds(0, rows)],
                v.parts_in.at[layer, section, pl.ds(0, rows)],
                v.parts_recv.at[layer],
                (target, row),
            )

    def send_pairs(group, layer, relay):
        def one(peer):
            send(
                group.own.at[layer, peer],
                group.come.at[layer, pair],
                group.recv.at[0, layer],
                (section, peer * 2 + core),
            )

        if not relay:
            each(pairs - 1, lambda i: one((pair + 1 + i) % pairs))
            return
        mirror = pairs - 1 - pair

        @pl.when(pair % 3 == 0)
        def _():
            near = (pair + 3) // 3
            send(
                group.own.at[layer, mirror],
                group.relay.at[layer],
                group.recv.at[2, layer],
                (section, near * 2 + core),
            )
            one(near)
            one(3 - near)

        before, started.cores = started.cores, ()

        @pl.when(pair % 3 != 0)
        def _():
            beyond = 3 * (pair - 1)
            one(beyond)
            one(mirror)
            far = 3 - beyond
            ended(group.relay.at[layer], group.recv.at[2, layer])
            group.own[layer, far] = (
                group.own[layer, far].astype(f32) + group.relay[layer].astype(f32)
            ).astype(bf16)
            one(far)

        started.cores = before

    def add_pairs(group, layer, relay):
        def add(peers):
            ended(group.come.at[layer, pl.ds(0, len(peers))], group.recv.at[0, layer])
            total = group.own[layer, pair].astype(f32)
            for peer in peers:
                total = total + group.come[layer, peer].astype(f32)
            group.total[layer] = total.astype(bf16)

        if relay:
            pl.when(pair % 3 == 0)(lambda: add([1, 2]))
            pl.when(pair % 3 != 0)(lambda: add([(pair + step) % 4 for step in (1, 2, 3)]))
        else:
            add([(pair + step) % pairs for step in range(1, pairs)])

        def share(target_section, other):
            send(
                group.total.at[layer, other],
                group.full.at[layer, section],
                group.recv.at[1, layer],
                (target_section, pair * 2 + other),
            )

        for step in range(1, sections):
            for other in range(2):
                share((section + step) % sections, other)
        share(section, 1 - core)
        write(group.total.at[layer, core], group.full.at[layer, section])

    def from_givers(group, layer, giver):
        def wait(other):
            slots = sections - 1 if other == giver else sections
            ended(group.full.at[layer, pl.ds(0, slots)], group.recv.at[1, layer])

        for other in range(2):
            on_core(other, functools.partial(wait, other))

    def store_blocks(target, product, offset, rows):
        padded = whole_tiles(rows)
        for owner in range(shards):
            block = product[owner * rows : (owner + 1) * rows]
            if padded != rows:
                block = jnp.concatenate([block, jnp.zeros((padded - rows, quarter), f32)], axis=0)
            target[owner // 2, owner % 2, offset : offset + padded] = block.astype(bf16)

    def store_vectors(target, total, offset):
        for owner in range(shards):
            target[owner // 2, owner % 2, offset : offset + vector_rows] = total.astype(bf16)

    def quarters(target, offset, value):
        rows = value.shape[0]
        for part in range(sections):
            target[part, offset : offset + rows] = value[
                :, part * quarter : (part + 1) * quarter
            ].astype(bf16)

    def vector(kind, layer):
        return v.vectors[vector_kinds.index(kind)].astype(f32)[layer : layer + 1]

    pl.semaphore_wait(barrier, shards - 1 + 2 * (sections - 1))
    send_nodes(0, v.node_features.at[section])

    def load(source, target, sem):
        pltpu.make_async_copy(source, target, v.load_sem.at[sem]).start()

    def load_matrix(kind, layer, sem):
        rows = weights[kind].shape[1]
        target = v.matrices.at[layer, pl.ds(plan.start[kind], rows)]
        load(weights[kind].at[layer], target, sem)

    def matrix(kind, layer, first=0, count=None):
        rows = weights[kind].shape[1] if count is None else count * width
        start = plan.start[kind] + first * width
        return v.matrices[layer, start : start + rows]

    def loaded(target, sem):
        ended(target, v.load_sem.at[sem])

    load(v.node_features.at[section], v.nodes.at[0, row], 0)
    load(v.edge_features.at[section], v.edge_in.at[0], 1)
    load_matrix(e_one, 0, 2)
    for place, source in enumerate((v.owner, v.local, v.receivers)):
        load(source.at[section], v.index.at[place], 3 + place)
    for place, kind in enumerate(vector_kinds):
        load(weights[kind], v.vectors.at[place], 6 + place)
    for kind in (e_two, n_one, n_two):
        load_matrix(kind, 0, 14)
    for layer in range(1, layers):
        for kind in matrix_kinds:
            load_matrix(kind, layer, 14 + layer)
    load(v.cotangent.at[section], v.cotangent_v, 14 + layers)

    loaded(v.nodes.at[0, row], 0)
    loaded(v.edge_in.at[0], 1)
    to_mate(0, v.mate_left.at[0], v.mate_recv.at[0], v.edge_in.at[0])

    for place in range(3):
        loaded(v.index.at[place], 3 + place)
    sender_row, target_row = v.index[0] * node_dev + v.index[1], v.index[2]
    eye = lax.broadcasted_iota(jnp.int32, (edge_dev, edge_dev), 0) == lax.broadcasted_iota(
        jnp.int32, (edge_dev, edge_dev), 1
    )

    def to_column(values):
        spread = jnp.broadcast_to(values, (edge_dev, edge_dev))
        column = jnp.sum(jnp.where(eye, spread, 0).astype(f32), axis=1, keepdims=True)
        return column.astype(jnp.int32)

    def one_hot(values, count, axis):
        places = (count, edge_dev) if axis == 0 else (edge_dev, count)
        match = lax.broadcasted_iota(jnp.int32, places, axis) == values
        return jnp.where(match, 1.0, 0.0).astype(bf16)

    v.from_nodes[...] = one_hot(to_column(sender_row), nodes_total, 1)
    v.to_nodes[...] = one_hot(sender_row, nodes_total, 0)
    v.from_targets[...] = one_hot(to_column(target_row), node_dev, 1)
    v.to_targets[...] = one_hot(target_row, node_dev, 0)
    for place in range(len(vector_kinds)):
        loaded(v.vectors.at[place], 6 + place)

    def edge_forward(layer):
        node = v.nodes[layer, row]
        edge = v.edge_in[layer]
        if layer == 0:
            loaded(v.matrices.at[0, pl.ds(0, 3 * width)], 2)
        else:
            loaded(v.matrices.at[layer], 14 + layer)
        received = dot(v.from_targets[...], node).astype(bf16)
        v.work[...] = (
            dot(edge, matrix(e_one, layer, 0, 1))
            + dot(received, matrix(e_one, layer, 2, 1))
            + vector(e_bias_one, layer)
        )
        from_rows(v.nodes, v.nodes_recv, layer)
        sent = dot(v.from_nodes[...], v.nodes[layer].reshape(nodes_total, width)).astype(bf16)
        hidden, slope = activate(
            v.work[...] + dot(sent, matrix(e_one, layer, 1, 1))
        )
        v.edge_hidden[layer] = hidden
        v.edge_slope[layer] = slope
        to_mate(1, v.mate_left.at[layer], v.mate_recv.at[layer], v.edge_hidden.at[layer])
        if layer == 0:
            loaded(v.matrices.at[0, pl.ds(3 * width, v.matrices.shape[1] - 3 * width)], 14)
        normed, scale = layer_norm(
            dot(hidden, matrix(e_two, layer)) + vector(e_bias_two, layer)
        )
        v.edge_normed[layer] = normed
        v.edge_scale[layer] = scale
        edge = (
            edge.astype(f32)
            + (normed * vector(e_gain, layer) + vector(e_shift, layer))
        ).astype(bf16)
        if layer + 1 < layers:
            v.edge_in[layer + 1] = edge
            to_mate(
                0, v.mate_left.at[layer + 1], v.mate_recv.at[layer + 1], v.edge_in.at[layer + 1]
            )
        return node, dot(v.to_targets[...], edge).astype(bf16)

    def node_forward(layer, node, gathered):
        hidden, slope = activate(
            dot(node, matrix(n_one, layer, 0, 1))
            + dot(gathered, matrix(n_one, layer, 1, 1))
            + vector(n_bias_one, layer)
        )
        v.node_slope[layer] = slope
        normed, scale = layer_norm(
            dot(hidden, matrix(n_two, layer)) + vector(n_bias_two, layer)
        )
        v.node_normed[layer] = normed
        v.node_scale[layer] = scale
        new_node = (
            node.astype(f32)
            + (normed * vector(n_gain, layer) + vector(n_shift, layer))
        ).astype(bf16)
        if layer + 1 < layers:
            v.nodes[layer + 1, row] = new_node
            send_nodes(layer + 1, v.nodes.at[layer + 1, row])
        else:
            v.final_v[0] = new_node
            write(v.final_v, v.final)
        v.node_lefts_own[layer, 0:node_dev] = node
        v.node_lefts_own[layer, node_dev : 2 * node_dev] = gathered
        v.node_lefts_own[layer, 2 * node_dev : 3 * node_dev] = hidden
        to_plane(
            node_lefts,
            layer,
            (
                lambda s: v.node_lefts_own.at[layer, pl.ds(0, node_dev)],
                lambda s: v.node_lefts_own.at[layer],
            ),
        )

    for layer in range(layers):
        node, gathered = edge_forward(layer)
        node_forward(layer, node, gathered)

    def node_products(layer, relay):
        def act():
            from_plane(node_lefts, layer, 3 * node_dev)
            from_plane(node_rights, layer, 2 * node_dev + vector_rows)
            own = plane * node_dev
            state = v.node_lefts[layer, :, 0:node_dev].reshape(own, width)
            gathered = v.node_lefts[layer, :, node_dev : 2 * node_dev].reshape(own, width)
            hidden = v.node_lefts[layer, :, 2 * node_dev : 3 * node_dev].reshape(own, width)
            grad_pre = v.node_rights[layer, :, 0:node_dev].reshape(own, quarter)
            grad_lifted = v.node_rights[layer, :, node_dev : 2 * node_dev].reshape(own, quarter)
            vectors = v.node_rights[layer, :, 2 * node_dev : 2 * node_dev + vector_rows]
            v.product[0:width] = contract_rows(state, grad_pre)
            v.product[width : 2 * width] = contract_rows(gathered, grad_pre)
            v.product[2 * width : 3 * width] = contract_rows(hidden, grad_lifted)
            target = node_pairs.own.at[layer]
            store_blocks(target, v.product, 0, two_rows)
            start = whole_tiles(two_rows)
            store_blocks(target, v.product.at[pl.ds(2 * width, width)], start, one_rows)
            start += whole_tiles(one_rows)
            store_vectors(target, jnp.sum(vectors.astype(f32), axis=0), start)
            send_pairs(node_pairs, layer, relay)

        on_core(1, act)

    def edge_parts(layer):
        def multiply(own_left, own_right):
            left = jnp.concatenate([own_left[layer], v.mate_left[layer]], axis=0)
            right = jnp.concatenate(
                [own_right[layer, 0:edge_dev], v.mate_right[layer, 0:edge_dev]], axis=0
            )
            for part in range(sections):
                columns = slice(part * quarter, (part + 1) * quarter)
                v.parts[layer, part, 0:width] = contract_rows(left, right[:, columns]).astype(bf16)

        def act_one():
            drained(2 * edge_dev * width, v.mate_recv.at[layer])
            multiply(v.edge_in, v.pre_own)
            send_parts(layer, width)

        def act_two():
            drained((2 * edge_dev + vector_rows) * width, v.mate_recv.at[layer])
            multiply(v.edge_hidden, v.lift_own)
            vectors = (
                v.lift_own[layer, edge_dev : edge_dev + vector_rows].astype(f32)
                + v.mate_right[layer, edge_dev : edge_dev + vector_rows].astype(f32)
            ).astype(bf16)
            for part in range(sections):
                v.parts[layer, part, width : width + vector_rows] = vectors[
                    :, part * quarter : (part + 1) * quarter
                ]
            send_parts(layer, width + vector_rows)

        on_core(0, act_one)
        on_core(1, act_two)

    def from_parts(layer, rows):
        drained((sections - 1) * rows * quarter, v.parts_recv.at[layer])

    def add_parts(layer, start, rows):
        total = v.parts[layer, section, start : start + rows].astype(f32)
        for step in range(1, sections):
            other = (section + step) % sections
            total = total + v.parts_in[layer, other, start : start + rows].astype(f32)
        return total

    def edge_products(layer, relay):
        def act_one():
            from_plane(node_lefts, layer, node_dev)
            from_plane(sum_rights, layer, 2 * node_dev)
            own = plane * node_dev
            state = v.node_lefts[layer, :, 0:node_dev].reshape(own, width)
            for part in range(2):
                start = part * node_dev
                v.product[(1 + part) * width : (2 + part) * width] = contract_rows(
                    state, v.sum_rights[layer, :, start : start + node_dev].reshape(own, quarter)
                )
            from_parts(layer, width)
            v.product[0:width] = add_parts(layer, 0, width)
            store_blocks(edge_pairs.own.at[layer], v.product, 0, three_rows)
            send_pairs(edge_pairs, layer, relay)

        def act_two():
            from_parts(layer, width + vector_rows)
            v.product[0:width] = add_parts(layer, 0, width)
            target = lift_pairs.own.at[layer]
            store_blocks(target, v.product, 0, one_rows)
            store_vectors(target, add_parts(layer, width, vector_rows), whole_tiles(one_rows))
            send_pairs(lift_pairs, layer, relay)

        on_core(0, act_one)
        on_core(1, act_two)

    def add_node_products(layer, relay):
        on_core(1, lambda: add_pairs(node_pairs, layer, relay))

    def add_edge_products(layer, relay):
        on_core(0, lambda: add_pairs(edge_pairs, layer, relay))
        on_core(1, lambda: add_pairs(lift_pairs, layer, relay))

    def node_backward(layer):
        grad_branch = v.grad_node[...]
        normed = v.node_normed[layer]
        grad_lifted = branch_back(
            grad_branch, vector(n_gain, layer), normed, v.node_scale[layer]
        )
        grad_hidden = contract_cols(grad_lifted, matrix(n_two, layer))
        grad_pre = (grad_hidden * v.node_slope[layer]).astype(bf16)
        aggregate = contract_cols(grad_pre, matrix(n_one, layer, 1, 1))
        high = aggregate.astype(bf16)
        low = (aggregate - high.astype(f32)).astype(bf16)
        grad_edge = dot(v.from_targets[...], high) + dot(v.from_targets[...], low)
        if layer + 1 < layers:
            grad_edge = grad_edge + v.grad_edge[...]
        v.grad_edge[...] = grad_edge.astype(bf16).astype(f32)
        grad_node = grad_branch + contract_cols(grad_pre, matrix(n_one, layer, 0, 1))
        v.grad_node[...] = grad_node.astype(bf16).astype(f32)
        target = v.node_rights_own.at[layer]
        quarters(target, 0, grad_pre)
        quarters(target, node_dev, grad_lifted)
        quarters(target, 2 * node_dev, column_sums(grad_pre, grad_lifted, grad_branch, normed))
        to_plane(node_rights, layer, (None, lambda s: v.node_rights_own.at[layer, s]))

    def edge_backward(layer):
        grad_branch = v.grad_edge[...]
        normed = v.edge_normed[layer]
        grad_lifted = branch_back(
            grad_branch, vector(e_gain, layer), normed, v.edge_scale[layer]
        )
        grad_hidden = contract_cols(grad_lifted, matrix(e_two, layer))
        grad_pre = (grad_hidden * v.edge_slope[layer]).astype(bf16)
        sums = dot(v.to_nodes[...], grad_pre).astype(bf16)
        v.sums[layer] = sums.reshape(shards, node_dev, width)
        send_sums(layer)
        v.pre_own[layer] = grad_pre
        v.lift_own[layer, 0:edge_dev] = grad_lifted
        v.lift_own[layer, edge_dev : edge_dev + vector_rows] = column_sums(
            grad_pre, grad_lifted, grad_branch, normed
        )
        to_mate(0, v.mate_right.at[layer], v.mate_recv.at[layer], v.pre_own.at[layer])
        to_mate(1, v.mate_right.at[layer], v.mate_recv.at[layer], v.lift_own.at[layer])
        grad_edge = grad_branch + contract_cols(grad_pre, matrix(e_one, layer, 0, 1))
        by_target = dot(v.to_targets[...], grad_pre).astype(bf16)
        v.grad_node[...] = v.grad_node[...] + contract_cols(
            by_target, matrix(e_one, layer, 2, 1)
        )
        if layer > 0:
            v.grad_edge[...] = grad_edge.astype(bf16).astype(f32)
        else:
            v.grad_edges_v[0] = grad_edge
            write(v.grad_edges_v, v.grad_edges)
        return by_target

    def sender_backward(layer, by_target):
        from_rows(v.sums_in, v.sums_recv, layer)
        v.sums_in[layer, row] = v.sums[layer, row]
        by_sender = jnp.sum(v.sums_in[layer].astype(f32), axis=0).astype(bf16)
        target = v.sum_rights_own.at[layer]
        quarters(target, 0, by_sender)
        quarters(target, node_dev, by_target)
        to_plane(sum_rights, layer, (lambda s: v.sum_rights_own.at[layer, s], None))
        grad_node = v.grad_node[...] + contract_cols(
            by_sender, matrix(e_one, layer, 1, 1)
        )
        if layer > 0:
            v.grad_node[...] = grad_node.astype(bf16).astype(f32)
        else:
            v.grad_nodes_v[0] = grad_node
            write(v.grad_nodes_v, v.grad_nodes)

    loaded(v.cotangent_v, 14 + layers)
    v.grad_node[...] = v.cotangent_v[...].astype(f32)
    relay = pairs == 4
    for layer in reversed(range(layers)):
        node_backward(layer)
        by_target = edge_backward(layer)
        edge_parts(layer)
        node_products(layer, False)
        sender_backward(layer, by_target)
    edge_products(1, relay)
    add_node_products(1, False)
    edge_products(0, relay)
    add_edge_products(1, relay)
    add_node_products(0, False)
    add_edge_products(0, relay)

    for layer in range(layers):
        from_givers(edge_pairs, layer, 0)
        from_givers(lift_pairs, layer, 1)
        from_givers(node_pairs, layer, 1)
    for one in range(2):
        pl.when(core == one)(
            lambda: drained(started.total[one], v.done)
        )


def write_kernel(shards, *refs):
    final, grad_nodes, grad_edges, edge_full, lift_full, node_full = refs[:6]
    out_final, out_nodes, out_edges = refs[6:9]
    grads = refs[9:]
    row = lax.axis_index("rows")
    layers, sections, quarter = edge_full.shape[0], edge_full.shape[1], edge_full.shape[3]
    width = sections * quarter
    three_rows, two_rows, one_rows = (part * width // shards for part in (3, 2, 1))
    node_start = whole_tiles(two_rows)
    out_final[...] = final[...]
    out_nodes[...] = grad_nodes[...]
    out_edges[...] = grad_edges[...]

    def put(target, full, start, rows):
        for layer in range(layers):
            for part in range(sections):
                value = full[layer, part, start : start + whole_tiles(rows)]
                target[layer, :, part * quarter : (part + 1) * quarter] = value.astype(f32)[0:rows]

    put(grads[e_one], edge_full, 0, three_rows)
    put(grads[e_two], lift_full, 0, one_rows)
    put(grads[n_one], node_full, 0, two_rows)
    put(grads[n_two], node_full, node_start, one_rows)

    def take_columns(value):
        per = quarter // one_rows
        taken = jnp.zeros((vector_rows, one_rows), f32)
        for place in range(per):
            taken = taken + jnp.where(
                row % per == place, value[:, place * one_rows : (place + 1) * one_rows], 0.0
            )
        return taken

    holder = row // (quarter // one_rows)
    for layer in range(layers):
        for kinds, full, start in (
            (vector_kinds[:4], lift_full, whole_tiles(one_rows)),
            (vector_kinds[4:], node_full, node_start + whole_tiles(one_rows)),
        ):
            vectors = take_columns(full[layer, holder, start : start + vector_rows].astype(f32))
            for place, kind in enumerate(kinds):
                grads[kind][layer : layer + 1] = vectors[place : place + 1]


def fused(sections, shards, node_features, edge_features, owner, local, receivers, cotangent, *weights):
    micro_count, node_dev, width = node_features.shape
    edge_dev = edge_features.shape[1]
    layers = weights[0].shape[0]
    quarter, pairs, plane = width // sections, shards // 2, 2 * sections
    nodes_total = shards * node_dev

    def shape(*dims, kind=f32):
        return jax.ShapeDtypeStruct(dims, kind)

    def vmem(*dims, kind=bf16):
        return pltpu.VMEM(dims, kind)

    def sems(*dims):
        return pltpu.SemaphoreType.DMA(dims)

    inputs = dict(
        node_features=node_features,
        edge_features=edge_features,
        owner=owner,
        local=local,
        receivers=receivers,
        cotangent=cotangent,
    )
    outputs = dict(
        final=shape(1, node_dev, width, kind=bf16),
        grad_nodes=shape(1, node_dev, width),
        grad_edges=shape(1, edge_dev, width),
    )
    weight_grads = [
        shape(layers, weight.shape[1] // shards, *weight.shape[2:]) for weight in weights
    ]
    lift_block = whole_tiles(width // shards) + vector_rows
    blocks = (
        whole_tiles(3 * width // shards),
        lift_block,
        whole_tiles(2 * width // shards) + lift_block,
    )
    fulls = [shape(layers, sections, block, quarter, kind=bf16) for block in blocks]
    starts = np.cumsum([0] + [weights[kind].shape[1] for kind in matrix_kinds])
    scratch = dict(
        done=pltpu.SemaphoreType.DMA,
        drain=vmem(1024 * (24 + shards // 2), lanes),
        load_sem=sems(15 + layers),
        index=vmem(3, 1, edge_dev, kind=jnp.int32),
        vectors=vmem(len(vector_kinds), layers, width),
        matrices=vmem(layers, int(starts[-1]), width),
        cotangent_v=vmem(node_dev, width),
        from_nodes=vmem(edge_dev, nodes_total),
        to_nodes=vmem(nodes_total, edge_dev),
        from_targets=vmem(edge_dev, node_dev),
        to_targets=vmem(node_dev, edge_dev),
        work=vmem(edge_dev, width, kind=f32),
        grad_node=vmem(node_dev, width, kind=f32),
        grad_edge=vmem(edge_dev, width, kind=f32),
        product=vmem(3 * width, quarter, kind=f32),
        edge_in=vmem(layers, edge_dev, width),
        edge_hidden=vmem(layers, edge_dev, width),
        edge_slope=vmem(layers, edge_dev, width, kind=f32),
        edge_normed=vmem(layers, edge_dev, width, kind=f32),
        edge_scale=vmem(layers, edge_dev, 1, kind=f32),
        node_slope=vmem(layers, node_dev, width, kind=f32),
        node_normed=vmem(layers, node_dev, width, kind=f32),
        node_scale=vmem(layers, node_dev, 1, kind=f32),
        nodes=vmem(layers, shards, node_dev, width),
        nodes_recv=sems(layers),
        sums=vmem(layers, shards, node_dev, width),
        sums_in=vmem(layers, shards, node_dev, width),
        sums_recv=sems(layers),
        final_v=vmem(1, node_dev, width),
        grad_nodes_v=vmem(1, node_dev, width, kind=f32),
        grad_edges_v=vmem(1, edge_dev, width, kind=f32),
        mate_left=vmem(layers, edge_dev, width),
        mate_right=vmem(layers, edge_dev + vector_rows, width),
        mate_recv=sems(layers),
        pre_own=vmem(layers, edge_dev, width),
        lift_own=vmem(layers, edge_dev + vector_rows, width),
        parts=vmem(layers, sections, width + vector_rows, quarter),
        parts_in=vmem(layers, sections, width + vector_rows, quarter),
        parts_recv=sems(layers),
        node_lefts_own=vmem(layers, 3 * node_dev, width),
        node_lefts=vmem(layers, plane, 3 * node_dev, width),
        node_lefts_recv=sems(layers),
        node_rights_own=vmem(layers, sections, 2 * node_dev + vector_rows, quarter),
        node_rights=vmem(layers, plane, 2 * node_dev + vector_rows, quarter),
        node_rights_recv=sems(layers),
        sum_rights_own=vmem(layers, sections, 2 * node_dev, quarter),
        sum_rights=vmem(layers, plane, 2 * node_dev, quarter),
        sum_rights_recv=sems(layers),
    )
    pair_groups = []
    for block in blocks:
        group = dict(
            own=vmem(layers, pairs, 2, block, quarter),
            come=vmem(layers, pairs, 2, block, quarter),
            total=vmem(layers, 2, block, quarter),
            relay=vmem(layers, 2, block, quarter),
            recv=sems(3, layers),
        )
        pair_groups += group.values()
    ins, outs = len(inputs) + len(weights), len(outputs) + len(fulls)
    names = (
        list(inputs)
        + list(range(len(weights)))
        + list(outputs)
        + list(range(len(fulls)))
        + list(scratch)
    )
    plan = SimpleNamespace(
        names=[str(name) for name in names],
        weights=len(inputs),
        fulls=ins + len(outputs),
        pair_groups=ins + outs + len(scratch),
        pair_names=list(group),
        start=dict(zip(matrix_kinds, map(int, starts))),
        layers=layers,
        sections=sections,
        shards=shards,
        node_dev=node_dev,
        edge_dev=edge_dev,
        width=width,
    )
    results = pl.pallas_call(
        functools.partial(kernel, plan),
        out_shape=list(outputs.values()) + fulls,
        in_specs=[pl.BlockSpec(memory_space=pltpu.HBM)] * ins,
        out_specs=[pl.BlockSpec(memory_space=pltpu.HBM)] * outs,
        scratch_shapes=list(scratch.values()) + pair_groups,
        compiler_params=pltpu.CompilerParams(
            collective_id=0, has_side_effects=True, vmem_limit_bytes=60 << 20
        ),
    )(*inputs.values(), *weights)
    return pl.pallas_call(
        functools.partial(write_kernel, shards),
        out_shape=list(outputs.values()) + weight_grads,
        in_specs=[pl.BlockSpec(memory_space=pltpu.VMEM)] * outs,
        out_specs=[pl.BlockSpec(memory_space=pltpu.VMEM)] * (len(outputs) + len(weight_grads)),
    )(*results)


def solution(mesh):
    sections, shards = mesh.shape["section"], mesh.shape["rows"]

    def body(node_features, edge_features, owner, *rest):
        owner = owner.reshape(owner.shape[:-1])
        return fused(sections, shards, node_features, edge_features, owner, *rest)

    in_specs = (
        P(None, "rows", None),
        P(None, "rows", None),
        P(None, "rows", None, None),
        P(None, "rows", None),
        P(None, "rows", None),
        P(None, "rows", None),
    ) + (P(),) * 12
    state = P("section", "rows", None)
    matrix, vector = P(None, "rows", None), P(None, "rows")
    out_specs = (state,) * 3 + (matrix, vector, matrix, vector, vector, vector) * 2
    return jax.shard_map(body, mesh=mesh, in_specs=in_specs, out_specs=out_specs, check_vma=False)
```

```python
import functools
from types import SimpleNamespace

import jax
import jax.numpy as jnp
import numpy as np
from jax import lax
from jax.experimental import pallas as pl
from jax.experimental.pallas import tpu as pltpu
from jax.sharding import PartitionSpec as P

f32 = jnp.float32
bf16 = jnp.bfloat16
MESH = pl.DeviceIdType.MESH
norm_epsilon = 1e-05
vector_rows = 16
e_one, e_bias_one, e_two, e_bias_two, e_gain, e_shift = range(6)
n_one, n_bias_one, n_two, n_bias_two, n_gain, n_shift = range(6, 12)
matrix_kinds = (e_one, e_two, n_one, n_two)
vector_kinds = (e_bias_one, e_bias_two, e_gain, e_shift, n_bias_one, n_bias_two, n_gain, n_shift)
lanes = 128


def dot(left, right):
    return jnp.dot(left, right, preferred_element_type=f32)


def contract_rows(left, right):
    return lax.dot_general(left, right, (((0,), (0,)), ((), ())), preferred_element_type=f32)


def contract_cols(left, right):
    return lax.dot_general(left, right, (((1,), (1,)), ((), ())), preferred_element_type=f32)


def whole_tiles(rows):
    return -(-rows // 16) * 16


def layer_norm(lifted):
    center = lifted - jnp.mean(lifted, axis=-1, keepdims=True)
    scale = lax.rsqrt(jnp.mean(center * center, axis=-1, keepdims=True) + norm_epsilon)
    return center * scale, scale


def activate(pre):
    sigma = jax.nn.sigmoid(pre)
    return (pre * sigma).astype(bf16), sigma * (1.0 + pre * (1.0 - sigma))


def branch_back(grad_branch, gain_row, normed, scale):
    grad_normed = grad_branch * gain_row
    return (
        scale
        * (
            grad_normed
            - jnp.mean(grad_normed, axis=-1, keepdims=True)
            - normed * jnp.mean(grad_normed * normed, axis=-1, keepdims=True)
        )
    ).astype(bf16)


def column_sums(grad_pre, grad_lifted, grad_branch, normed, first):
    rows = [
        jnp.sum(grad_pre.astype(f32), axis=0, keepdims=True),
        jnp.sum(grad_lifted.astype(f32), axis=0, keepdims=True),
        jnp.sum(grad_branch * normed, axis=0, keepdims=True),
        jnp.sum(grad_branch, axis=0, keepdims=True),
    ]
    zeros = jnp.zeros((vector_rows, grad_branch.shape[1]), f32)
    rows = ([zeros[:first]] if first else []) + rows + [zeros[first + 4 :]]
    return jnp.concatenate(rows, axis=0).astype(bf16)


def ended(buffer, sem):
    pltpu.make_async_copy(buffer, buffer, sem).wait()


def kernel(plan, *refs):
    v = SimpleNamespace(**dict(zip(plan.names, refs)))
    layers, sections, shards = plan.layers, plan.sections, plan.shards
    node_dev, edge_dev, width = plan.node_dev, plan.edge_dev, plan.width
    quarter, pairs, plane = width // sections, shards // 2, 2 * sections
    nodes_total = shards * node_dev
    three_rows, two_rows, one_rows = (part * width // shards for part in (3, 2, 1))
    weights = refs[plan.weights : plan.weights + 12]
    section, row = lax.axis_index("section"), lax.axis_index("rows")
    pair, core = row // 2, row % 2
    plane_slot = core * sections + section
    edge_pairs, lift_pairs, node_pairs = (
        SimpleNamespace(
            full=refs[plan.fulls + place],
            **dict(zip(plan.pair_names, refs[plan.pair_groups + 5 * place :])),
        )
        for place in range(3)
    )
    rights = SimpleNamespace(data=v.rights, recv=v.rights_recv)
    node_lefts = SimpleNamespace(data=v.node_lefts, recv=v.node_lefts_recv)
    node_rights = SimpleNamespace(data=v.node_rights, recv=v.node_rights_recv)
    sum_rights = SimpleNamespace(data=v.sum_rights, recv=v.sum_rights_recv)

    def drained(count, sem):
        ended(v.drain.at[pl.ds(0, count // lanes)], sem)

    started = SimpleNamespace(total=[0, 0], cores=(0, 1), times=1)

    def count_start(source):
        for one in started.cores:
            started.total[one] += started.times * source.size * source.dtype.itemsize // 2

    def send(source, target, recv_sem, device):
        count_start(source)
        pltpu.make_async_remote_copy(
            src_ref=source,
            dst_ref=target,
            send_sem=v.done,
            recv_sem=recv_sem,
            device_id=device,
            device_id_type=MESH,
        ).start()

    def write(source, target):
        count_start(source)
        pltpu.make_async_copy(source, target, v.done).start()

    def on_core(one, act):
        before = started.cores
        started.cores = tuple(x for x in before if x == one)
        pl.when(core == one)(act)
        started.cores = before

    def each(count, visit):
        if count <= 8:
            for i in range(count):
                visit(i)
        else:
            before = started.times

            def step(i, carry):
                started.times = before * count
                visit(i)
                started.times = before
                return carry

            lax.fori_loop(0, count, step, 0)

    barrier = pltpu.get_barrier_semaphore()

    def greet(device):
        pl.semaphore_signal(barrier, inc=1, device_id=device, device_id_type=MESH)

    each(shards - 1, lambda i: greet((section, (row + 1 + i) % shards)))
    for step in range(1, sections):
        for other in range(2):
            greet(((section + step) % sections, pair * 2 + other))

    def peer_rows(visit):
        if pairs == 4:
            for peer in (3 - pair, (pair + 2) % 4, pair + 1 - 2 * (pair % 2)):
                visit(2 * peer + core)
                visit(2 * peer + 1 - core)
            visit(row + 1 - 2 * core)
        else:
            each(shards - 1, lambda i: visit((row + 1 + i) % shards))

    def send_nodes(layer, source):
        def one(peer):
            send(source, v.nodes.at[layer, row], v.nodes_recv.at[layer], (section, peer))

        peer_rows(one)

    def send_sums(layer):
        ended(v.mate_sums.at[layer], v.mate_sums_recv.at[layer])
        both = v.sums[layer, core].astype(f32) + v.mate_sums[layer].astype(f32)
        v.both_sums[layer] = both.astype(bf16)

        def one(peer):
            send(
                v.both_sums.at[layer, peer],
                v.sums_in.at[layer, pair],
                v.sums_recv.at[layer],
                (section, peer * 2 + core),
            )

        peer_pairs(one)

    def peer_pairs(visit):
        if pairs == 4:
            for peer in (3 - pair, (pair + 2) % 4, pair + 1 - 2 * (pair % 2)):
                visit(peer)
        else:
            each(pairs - 1, lambda i: visit((pair + 1 + i) % pairs))

    def from_rows(data, sem, layer):
        ended(data.at[layer, pl.ds(0, shards - 1)], sem.at[layer])

    def to_plane(group, layer, sources):
        def one(target_section, other):
            source = sources[other](target_section)
            send(
                source,
                group.data.at[layer, plane_slot, pl.ds(0, source.shape[0])],
                group.recv.at[layer],
                (target_section, pair * 2 + other),
            )

        def keep(other):
            source = sources[other](section)
            group.data[layer, plane_slot, 0 : source.shape[0]] = source[...]

        for other in range(2):
            if sources[other] is not None:
                for step in range(1, sections):
                    one((section + step) % sections, other)
                on_core(1 - other, functools.partial(one, section, other))
                on_core(other, functools.partial(keep, other))

    def from_plane(group, layer, rows):
        drained((plane - 1) * rows * group.data.shape[-1], group.recv.at[layer])

    def to_mate(taker, target, recv_sem, source):
        target = target.at[pl.ds(0, source.shape[0])]
        mate = (section, row + 1 - 2 * core)
        on_core(1 - taker, lambda: send(source, target, recv_sem, mate))

    def send_parts(layer, rows):
        for step in range(1, sections):
            target = (section + step) % sections
            send(
                v.parts.at[layer, target, pl.ds(0, rows)],
                v.parts_in.at[layer, section, pl.ds(0, rows)],
                v.parts_recv.at[layer],
                (target, row),
            )

    def send_pairs(group, layer, relay):
        def one(peer):
            send(
                group.own.at[layer, peer],
                group.come.at[layer, pair],
                group.recv.at[0, layer],
                (section, peer * 2 + core),
            )

        if not relay:
            peer_pairs(one)
            return
        mirror = pairs - 1 - pair

        @pl.when(pair % 3 == 0)
        def _():
            near = (pair + 3) // 3
            send(
                group.own.at[layer, mirror],
                group.relay.at[layer],
                group.recv.at[2, layer],
                (section, near * 2 + core),
            )
            one(near)
            one(3 - near)

        before, started.cores = started.cores, ()

        @pl.when(pair % 3 != 0)
        def _():
            one(3 * (pair - 1))
            one(mirror)

        started.cores = before

    def relay_pairs(group, layer):
        before, started.cores = started.cores, ()

        @pl.when(pair % 3 != 0)
        def _():
            far = 3 - 3 * (pair - 1)
            ended(group.relay.at[layer], group.recv.at[2, layer])
            group.own[layer, far] = (
                group.own[layer, far].astype(f32) + group.relay[layer].astype(f32)
            ).astype(bf16)
            send(
                group.own.at[layer, far],
                group.come.at[layer, pair],
                group.recv.at[0, layer],
                (section, far * 2 + core),
            )

        started.cores = before

    def add_pairs(group, layer, relay):
        def add(peers):
            ended(group.come.at[layer, pl.ds(0, len(peers))], group.recv.at[0, layer])
            total = group.own[layer, pair].astype(f32)
            for peer in peers:
                total = total + group.come[layer, peer].astype(f32)
            group.total[layer] = total.astype(bf16)

        if relay:
            pl.when(pair % 3 == 0)(lambda: add([1, 2]))
            pl.when(pair % 3 != 0)(lambda: add([(pair + step) % 4 for step in (1, 2, 3)]))
        else:
            add([(pair + step) % pairs for step in range(1, pairs)])

        def share(target_section, other):
            send(
                group.total.at[layer, other],
                group.full.at[layer, section],
                group.recv.at[1, layer],
                (target_section, pair * 2 + other),
            )

        for step in range(1, sections):
            for other in range(2):
                share((section + step) % sections, other)
        share(section, 1 - core)
        write(group.total.at[layer, core], group.full.at[layer, section])

    def from_givers(group, layer, giver):
        def wait(other):
            slots = sections - 1 if other == giver else sections
            ended(group.full.at[layer, pl.ds(0, slots)], group.recv.at[1, layer])

        for other in range(2):
            on_core(other, functools.partial(wait, other))

    def store_blocks(target, product, offset, rows):
        padded = whole_tiles(rows)
        for owner in range(shards):
            block = product[owner * rows : (owner + 1) * rows]
            if padded != rows:
                block = jnp.concatenate([block, jnp.zeros((padded - rows, quarter), f32)], axis=0)
            target[owner // 2, owner % 2, offset : offset + padded] = block.astype(bf16)

    def store_vectors(target, total, offset):
        for owner in range(shards):
            target[owner // 2, owner % 2, offset : offset + vector_rows] = total.astype(bf16)

    def quarters(target, offset, value):
        rows = value.shape[0]
        for part in range(sections):
            target[part, offset : offset + rows] = value[
                :, part * quarter : (part + 1) * quarter
            ].astype(bf16)

    def vector(kind, layer):
        return v.vectors[vector_kinds.index(kind)].astype(f32)[layer : layer + 1]

    pl.semaphore_wait(barrier, shards - 1 + 2 * (sections - 1))
    send_nodes(0, v.node_features.at[section])

    def load(source, target, sem):
        pltpu.make_async_copy(source, target, v.load_sem.at[sem]).start()

    def load_matrix(kind, layer, sem):
        rows = weights[kind].shape[1]
        target = v.matrices.at[layer, pl.ds(plan.start[kind], rows)]
        load(weights[kind].at[layer], target, sem)

    def matrix(kind, layer, first=0, count=None):
        rows = weights[kind].shape[1] if count is None else count * width
        start = plan.start[kind] + first * width
        return v.matrices[layer, start : start + rows]

    def loaded(target, sem):
        ended(target, v.load_sem.at[sem])

    load(v.node_features.at[section], v.nodes.at[0, row], 0)
    load(v.edge_features.at[section], v.edge_in.at[0], 1)
    load_matrix(e_one, 0, 2)
    for place, source in enumerate((v.owner, v.local, v.receivers)):
        load(source.at[section], v.index.at[place], 3 + place)
    for place, kind in enumerate(vector_kinds):
        load(weights[kind], v.vectors.at[place], 6 + place)
    for kind in (e_two, n_one, n_two):
        load_matrix(kind, 0, 14)
    for layer in range(1, layers):
        for kind in matrix_kinds:
            load_matrix(kind, layer, 14 + layer)
    load(v.cotangent.at[section], v.cotangent_v, 14 + layers)

    on_core(0, lambda: load(v.edge_features, v.lefts.at[pl.ds(0, sections)], 15 + layers))
    to_mate(0, v.lefts.at[pl.ds(sections, sections)], v.lefts_recv, v.edge_features)

    loaded(v.nodes.at[0, row], 0)
    loaded(v.edge_in.at[0], 1)

    for place in range(3):
        loaded(v.index.at[place], 3 + place)
    sender_row, target_row = v.index[0] * node_dev + v.index[1], v.index[2]
    eye = lax.broadcasted_iota(jnp.int32, (edge_dev, edge_dev), 0) == lax.broadcasted_iota(
        jnp.int32, (edge_dev, edge_dev), 1
    )

    def to_column(values):
        spread = jnp.broadcast_to(values, (edge_dev, edge_dev))
        column = jnp.sum(jnp.where(eye, spread, 0).astype(f32), axis=1, keepdims=True)
        return column.astype(jnp.int32)

    def one_hot(values, count, axis):
        places = (count, edge_dev) if axis == 0 else (edge_dev, count)
        match = lax.broadcasted_iota(jnp.int32, places, axis) == values
        return jnp.where(match, 1.0, 0.0).astype(bf16)

    v.from_nodes[...] = one_hot(to_column(sender_row), nodes_total, 1)
    v.to_nodes[...] = one_hot(sender_row, nodes_total, 0)
    v.from_targets[...] = one_hot(to_column(target_row), node_dev, 1)
    v.to_targets[...] = one_hot(target_row, node_dev, 0)
    for place in range(len(vector_kinds)):
        loaded(v.vectors.at[place], 6 + place)

    def edge_forward(layer):
        node = v.nodes[layer, row]
        edge = v.edge_in[layer]
        if layer == 0:
            loaded(v.matrices.at[0, pl.ds(0, 3 * width)], 2)
        else:
            loaded(v.matrices.at[layer], 14 + layer)
        received = dot(v.from_targets[...], node).astype(bf16)
        v.work[...] = (
            dot(edge, matrix(e_one, layer, 0, 1))
            + dot(received, matrix(e_one, layer, 2, 1))
            + vector(e_bias_one, layer)
        )
        from_rows(v.nodes, v.nodes_recv, layer)
        sent = dot(v.from_nodes[...], v.nodes[layer].reshape(nodes_total, width)).astype(bf16)
        hidden, slope = activate(
            v.work[...] + dot(sent, matrix(e_one, layer, 1, 1))
        )
        v.edge_hidden[layer] = hidden
        v.edge_slope[layer] = slope
        to_mate(1, v.mate_left.at[layer], v.mate_recv.at[layer], v.edge_hidden.at[layer])
        if layer == 0:
            loaded(v.matrices.at[0, pl.ds(3 * width, v.matrices.shape[1] - 3 * width)], 14)
        normed, scale = layer_norm(
            dot(hidden, matrix(e_two, layer)) + vector(e_bias_two, layer)
        )
        v.edge_normed[layer] = normed
        v.edge_scale[layer] = scale
        edge = (
            edge.astype(f32)
            + (normed * vector(e_gain, layer) + vector(e_shift, layer))
        ).astype(bf16)
        if layer + 1 < layers:
            v.edge_in[layer + 1] = edge
            to_mate(
                0, v.pre_left.at[layer + 1], v.pre_recv.at[layer + 1], v.edge_in.at[layer + 1]
            )
        return node, dot(v.to_targets[...], edge).astype(bf16)

    def node_forward(layer, node, gathered):
        hidden, slope = activate(
            dot(node, matrix(n_one, layer, 0, 1))
            + dot(gathered, matrix(n_one, layer, 1, 1))
            + vector(n_bias_one, layer)
        )
        v.node_slope[layer] = slope
        normed, scale = layer_norm(
            dot(hidden, matrix(n_two, layer)) + vector(n_bias_two, layer)
        )
        v.node_normed[layer] = normed
        v.node_scale[layer] = scale
        new_node = (
            node.astype(f32)
            + (normed * vector(n_gain, layer) + vector(n_shift, layer))
        ).astype(bf16)
        if layer + 1 < layers:
            v.nodes[layer + 1, row] = new_node
            send_nodes(layer + 1, v.nodes.at[layer + 1, row])
        else:
            v.final_v[0] = new_node
            write(v.final_v, v.final)
        v.node_lefts_own[layer, 0:node_dev] = node
        v.node_lefts_own[layer, node_dev : 2 * node_dev] = gathered
        v.node_lefts_own[layer, 2 * node_dev : 3 * node_dev] = hidden
        to_plane(node_lefts, layer, (None, lambda s: v.node_lefts_own.at[layer]))

    for layer in range(layers):
        node, gathered = edge_forward(layer)
        node_forward(layer, node, gathered)

    def hand_states(layer):
        def act():
            from_plane(node_lefts, layer, 3 * node_dev)
            send(
                v.node_lefts.at[layer, :, pl.ds(0, node_dev)],
                v.states.at[layer],
                v.states_recv.at[layer],
                (section, row + 1 - 2 * core),
            )

        on_core(1, act)

    def node_products(layer, relay):
        def act():
            from_plane(node_rights, layer, 2 * node_dev + vector_rows)
            own = plane * node_dev
            state = v.node_lefts[layer, :, 0:node_dev].reshape(own, width)
            gathered = v.node_lefts[layer, :, node_dev : 2 * node_dev].reshape(own, width)
            hidden = v.node_lefts[layer, :, 2 * node_dev : 3 * node_dev].reshape(own, width)
            grad_pre = v.node_rights[layer, :, 0:node_dev].reshape(own, quarter)
            grad_lifted = v.node_rights[layer, :, node_dev : 2 * node_dev].reshape(own, quarter)
            vectors = v.node_rights[layer, :, 2 * node_dev : 2 * node_dev + vector_rows]
            v.product[0:width] = contract_rows(state, grad_pre)
            v.product[width : 2 * width] = contract_rows(gathered, grad_pre)
            v.product[2 * width : 3 * width] = contract_rows(hidden, grad_lifted)
            target = node_pairs.own.at[layer]
            store_blocks(target, v.product, 0, two_rows)
            start = whole_tiles(two_rows)
            store_blocks(target, v.product.at[pl.ds(2 * width, width)], start, one_rows)
            v.node_vectors[layer] = jnp.sum(vectors.astype(f32), axis=0)
            send_pairs(node_pairs, layer, relay)

        on_core(1, act)

    def edge_parts(layer):
        def multiply(lefts, rights):
            left = jnp.concatenate(lefts, axis=0)
            right = jnp.concatenate(rights, axis=0)
            for part in range(sections):
                columns = slice(part * quarter, (part + 1) * quarter)
                v.parts[layer, part, 0:width] = contract_rows(left, right[:, columns]).astype(bf16)

        def act_one():
            drained(2 * edge_dev * width, v.pre_recv.at[layer])
            multiply([v.edge_in[layer], v.pre_left[layer]], [v.pre_own[layer], v.pre_right[layer]])
            send_parts(layer, width)

        def act_two():
            drained((2 * edge_dev + vector_rows) * width, v.mate_recv.at[layer])
            multiply(
                [v.edge_hidden[layer], v.mate_left[layer]],
                [v.lift_own[layer, 0:edge_dev], v.mate_right[layer, 0:edge_dev]],
            )
            vectors = (
                v.lift_own[layer, edge_dev : edge_dev + vector_rows].astype(f32)
                + v.mate_right[layer, edge_dev : edge_dev + vector_rows].astype(f32)
            ).astype(bf16)
            for part in range(sections):
                columns = slice(part * quarter, (part + 1) * quarter)
                v.parts[layer, part, width : width + vector_rows] = vectors[:, columns]
            send_parts(layer, width + vector_rows)

        if layer > 0:
            on_core(0, act_one)
        on_core(1, act_two)

    def from_parts(layer, rows):
        drained((sections - 1) * rows * quarter, v.parts_recv.at[layer])

    def add_parts(layer, start, rows):
        total = v.parts[layer, section, start : start + rows].astype(f32)
        for step in range(1, sections):
            other = (section + step) % sections
            total = total + v.parts_in[layer, other, start : start + rows].astype(f32)
        return total

    def edge_products(layer, relay):
        def act():
            if layer == 0:
                loaded(v.lefts.at[pl.ds(0, sections)], 15 + layers)
                ended(v.lefts.at[pl.ds(sections, sections)], v.lefts_recv)
                from_plane(rights, 0, edge_dev)
                v.product[0:width] = contract_rows(
                    v.lefts[...].reshape(plane * edge_dev, width),
                    v.rights[0].reshape(plane * edge_dev, quarter),
                )
            ended(v.states.at[layer], v.states_recv.at[layer])
            from_plane(sum_rights, layer, 2 * node_dev)
            own = plane * node_dev
            state = v.states[layer].reshape(own, width)
            for part in range(2):
                start = part * node_dev
                v.product[(1 + part) * width : (2 + part) * width] = contract_rows(
                    state, v.sum_rights[layer, :, start : start + node_dev].reshape(own, quarter)
                )
            if layer > 0:
                from_parts(layer, width)
                v.product[0:width] = add_parts(layer, 0, width)
            store_blocks(edge_pairs.own.at[layer], v.product, 0, three_rows)
            send_pairs(edge_pairs, layer, relay)

        on_core(0, act)

    def lift_products(layer, relay):
        def act():
            from_parts(layer, width + vector_rows)
            v.product[0:width] = add_parts(layer, 0, width)
            target = lift_pairs.own.at[layer]
            store_blocks(target, v.product, 0, one_rows)
            vectors = add_parts(layer, width, vector_rows) + v.node_vectors[layer]
            store_vectors(target, vectors, whole_tiles(one_rows))
            send_pairs(lift_pairs, layer, relay)

        on_core(1, act)

    def relay_products(group, giver, layer, relay):
        if relay:
            on_core(giver, lambda: relay_pairs(group, layer))

    def add_products(group, giver, layer, relay):
        on_core(giver, lambda: add_pairs(group, layer, relay))

    def node_backward(layer):
        grad_branch = v.grad_node[...]
        normed = v.node_normed[layer]
        grad_lifted = branch_back(
            grad_branch, vector(n_gain, layer), normed, v.node_scale[layer]
        )
        grad_hidden = contract_cols(grad_lifted, matrix(n_two, layer))
        grad_pre = (grad_hidden * v.node_slope[layer]).astype(bf16)
        aggregate = contract_cols(grad_pre, matrix(n_one, layer, 1, 1))
        high = aggregate.astype(bf16)
        low = (aggregate - high.astype(f32)).astype(bf16)
        grad_edge = dot(v.from_targets[...], high) + dot(v.from_targets[...], low)
        if layer + 1 < layers:
            grad_edge = grad_edge + v.grad_edge[...]
        v.grad_edge[...] = grad_edge.astype(bf16).astype(f32)
        grad_node = grad_branch + contract_cols(grad_pre, matrix(n_one, layer, 0, 1))
        v.grad_node[...] = grad_node.astype(bf16).astype(f32)
        target = v.node_rights_own.at[layer]
        quarters(target, 0, grad_pre)
        quarters(target, node_dev, grad_lifted)
        quarters(target, 2 * node_dev, column_sums(grad_pre, grad_lifted, grad_branch, normed, 4))
        to_plane(node_rights, layer, (None, lambda s: v.node_rights_own.at[layer, s]))

    def edge_backward(layer):
        grad_branch = v.grad_edge[...]
        normed = v.edge_normed[layer]
        grad_lifted = branch_back(
            grad_branch, vector(e_gain, layer), normed, v.edge_scale[layer]
        )
        grad_hidden = contract_cols(grad_lifted, matrix(e_two, layer))
        grad_pre = (grad_hidden * v.edge_slope[layer]).astype(bf16)
        sums = dot(v.to_nodes[...], grad_pre).astype(bf16)
        for place in range(shards):
            block = sums[place * node_dev : (place + 1) * node_dev]
            v.sums[layer, place % 2, place // 2] = block
        mate = (section, row + 1 - 2 * core)
        send(v.sums.at[layer, 1 - core], v.mate_sums.at[layer], v.mate_sums_recv.at[layer], mate)
        if layer == 0:
            quarters(v.pre_rights_own, 0, grad_pre)
            to_plane(rights, 0, (lambda s: v.pre_rights_own.at[s], None))
        else:
            v.pre_own[layer] = grad_pre
            to_mate(0, v.pre_right.at[layer], v.pre_recv.at[layer], v.pre_own.at[layer])
        v.lift_own[layer, 0:edge_dev] = grad_lifted
        v.lift_own[layer, edge_dev : edge_dev + vector_rows] = column_sums(
            grad_pre, grad_lifted, grad_branch, normed, 0
        )
        to_mate(1, v.mate_right.at[layer], v.mate_recv.at[layer], v.lift_own.at[layer])
        send_sums(layer)
        grad_edge = grad_branch + contract_cols(grad_pre, matrix(e_one, layer, 0, 1))
        by_target = dot(v.to_targets[...], grad_pre).astype(bf16)
        v.grad_node[...] = v.grad_node[...] + contract_cols(
            by_target, matrix(e_one, layer, 2, 1)
        )
        if layer > 0:
            v.grad_edge[...] = grad_edge.astype(bf16).astype(f32)
        else:
            v.grad_edges_v[0] = grad_edge
            write(v.grad_edges_v, v.grad_edges)
        return by_target

    def sender_backward(layer, by_target):
        ended(v.sums_in.at[layer, pl.ds(0, pairs - 1)], v.sums_recv.at[layer])
        v.sums_in[layer, pair] = v.both_sums[layer, pair]
        by_sender = jnp.sum(v.sums_in[layer].astype(f32), axis=0).astype(bf16)
        target = v.sum_rights_own.at[layer]
        quarters(target, 0, by_sender)
        quarters(target, node_dev, by_target)
        to_plane(sum_rights, layer, (lambda s: v.sum_rights_own.at[layer, s], None))
        grad_node = v.grad_node[...] + contract_cols(
            by_sender, matrix(e_one, layer, 1, 1)
        )
        if layer > 0:
            v.grad_node[...] = grad_node.astype(bf16).astype(f32)
        else:
            v.grad_nodes_v[0] = grad_node
            write(v.grad_nodes_v, v.grad_nodes)

    loaded(v.cotangent_v, 14 + layers)
    v.grad_node[...] = v.cotangent_v[...].astype(f32)
    relay = pairs == 4
    for layer in reversed(range(1, layers)):
        node_backward(layer)
        by_target = edge_backward(layer)
        edge_parts(layer)
        sender_backward(layer, by_target)
        hand_states(layer)
        node_products(layer, relay)
    node_backward(0)
    by_target = edge_backward(0)
    edge_parts(0)
    hand_states(0)
    for layer in reversed(range(1, layers)):
        edge_products(layer, relay)
        lift_products(layer, relay)
        relay_products(node_pairs, 1, layer, relay)
        relay_products(lift_pairs, 1, layer, relay)
    node_products(0, relay)
    sender_backward(0, by_target)
    edge_products(0, relay)
    for layer in reversed(range(layers)):
        relay_products(edge_pairs, 0, layer, relay)
    for layer in reversed(range(1, layers)):
        add_products(node_pairs, 1, layer, relay)
        add_products(lift_pairs, 1, layer, relay)
    for layer in reversed(range(layers)):
        add_products(edge_pairs, 0, layer, relay)
    lift_products(0, relay)
    relay_products(node_pairs, 1, 0, relay)
    relay_products(lift_pairs, 1, 0, relay)
    add_products(node_pairs, 1, 0, relay)
    add_products(lift_pairs, 1, 0, relay)

    for layer in range(layers):
        from_givers(edge_pairs, layer, 0)
        from_givers(lift_pairs, layer, 1)
        from_givers(node_pairs, layer, 1)
    for one in range(2):
        pl.when(core == one)(
            lambda: drained(started.total[one], v.done)
        )


def write_kernel(shards, *refs):
    final, grad_nodes, grad_edges, edge_full, lift_full, node_full = refs[:6]
    out_final, out_nodes, out_edges = refs[6:9]
    grads = refs[9:]
    row = lax.axis_index("rows")
    layers, sections, quarter = edge_full.shape[0], edge_full.shape[1], edge_full.shape[3]
    width = sections * quarter
    three_rows, two_rows, one_rows = (part * width // shards for part in (3, 2, 1))
    node_start = whole_tiles(two_rows)
    out_final[...] = final[...]
    out_nodes[...] = grad_nodes[...]
    out_edges[...] = grad_edges[...]

    def put(target, full, start, rows):
        for layer in range(layers):
            for part in range(sections):
                value = full[layer, part, start : start + whole_tiles(rows)]
                target[layer, :, part * quarter : (part + 1) * quarter] = value.astype(f32)[0:rows]

    put(grads[e_one], edge_full, 0, three_rows)
    put(grads[e_two], lift_full, 0, one_rows)
    put(grads[n_one], node_full, 0, two_rows)
    put(grads[n_two], node_full, node_start, one_rows)

    def take_columns(value):
        per = quarter // one_rows
        taken = jnp.zeros((vector_rows, one_rows), f32)
        for place in range(per):
            taken = taken + jnp.where(
                row % per == place, value[:, place * one_rows : (place + 1) * one_rows], 0.0
            )
        return taken

    holder = row // (quarter // one_rows)
    for layer in range(layers):
        start = whole_tiles(one_rows)
        taken = take_columns(lift_full[layer, holder, start : start + vector_rows].astype(f32))
        for place, kind in enumerate(vector_kinds):
            grads[kind][layer : layer + 1] = taken[place : place + 1]


def fused(sections, shards, node_features, edge_features, owner, local, receivers, cotangent, *weights):
    micro_count, node_dev, width = node_features.shape
    edge_dev = edge_features.shape[1]
    layers = weights[0].shape[0]
    quarter, pairs, plane = width // sections, shards // 2, 2 * sections
    nodes_total = shards * node_dev

    def shape(*dims, kind=f32):
        return jax.ShapeDtypeStruct(dims, kind)

    def vmem(*dims, kind=bf16):
        return pltpu.VMEM(dims, kind)

    def sems(*dims):
        return pltpu.SemaphoreType.DMA(dims)

    inputs = dict(
        node_features=node_features,
        edge_features=edge_features,
        owner=owner,
        local=local,
        receivers=receivers,
        cotangent=cotangent,
    )
    outputs = dict(
        final=shape(1, node_dev, width, kind=bf16),
        grad_nodes=shape(1, node_dev, width),
        grad_edges=shape(1, edge_dev, width),
    )
    weight_grads = [
        shape(layers, weight.shape[1] // shards, *weight.shape[2:]) for weight in weights
    ]
    lift_block = whole_tiles(width // shards) + vector_rows
    blocks = (
        whole_tiles(3 * width // shards),
        lift_block,
        whole_tiles(2 * width // shards) + whole_tiles(width // shards),
    )
    fulls = [shape(layers, sections, block, quarter, kind=bf16) for block in blocks]
    starts = np.cumsum([0] + [weights[kind].shape[1] for kind in matrix_kinds])
    scratch = dict(
        done=pltpu.SemaphoreType.DMA,
        drain=vmem(1024 * (24 + shards // 2), lanes),
        load_sem=sems(16 + layers),
        index=vmem(3, 1, edge_dev, kind=jnp.int32),
        vectors=vmem(len(vector_kinds), layers, width),
        matrices=vmem(layers, int(starts[-1]), width),
        cotangent_v=vmem(node_dev, width),
        from_nodes=vmem(edge_dev, nodes_total),
        to_nodes=vmem(nodes_total, edge_dev),
        from_targets=vmem(edge_dev, node_dev),
        to_targets=vmem(node_dev, edge_dev),
        work=vmem(edge_dev, width, kind=f32),
        grad_node=vmem(node_dev, width, kind=f32),
        grad_edge=vmem(edge_dev, width, kind=f32),
        product=vmem(3 * width, quarter, kind=f32),
        edge_in=vmem(layers, edge_dev, width),
        edge_hidden=vmem(layers, edge_dev, width),
        edge_slope=vmem(layers, edge_dev, width, kind=f32),
        edge_normed=vmem(layers, edge_dev, width, kind=f32),
        edge_scale=vmem(layers, edge_dev, 1, kind=f32),
        node_slope=vmem(layers, node_dev, width, kind=f32),
        node_normed=vmem(layers, node_dev, width, kind=f32),
        node_scale=vmem(layers, node_dev, 1, kind=f32),
        nodes=vmem(layers, shards, node_dev, width),
        nodes_recv=sems(layers),
        sums=vmem(layers, 2, pairs, node_dev, width),
        mate_sums=vmem(layers, pairs, node_dev, width),
        mate_sums_recv=sems(layers),
        both_sums=vmem(layers, pairs, node_dev, width),
        sums_in=vmem(layers, pairs, node_dev, width),
        sums_recv=sems(layers),
        final_v=vmem(1, node_dev, width),
        grad_nodes_v=vmem(1, node_dev, width, kind=f32),
        grad_edges_v=vmem(1, edge_dev, width, kind=f32),
        node_vectors=vmem(layers, vector_rows, quarter, kind=f32),
        mate_left=vmem(layers, edge_dev, width),
        mate_right=vmem(layers, edge_dev + vector_rows, width),
        mate_recv=sems(layers),
        lefts=vmem(plane, edge_dev, width),
        lefts_recv=pltpu.SemaphoreType.DMA,
        pre_rights_own=vmem(sections, edge_dev, quarter),
        rights=vmem(1, plane, edge_dev, quarter),
        rights_recv=sems(1),
        pre_own=vmem(layers, edge_dev, width),
        pre_left=vmem(layers, edge_dev, width),
        pre_right=vmem(layers, edge_dev, width),
        pre_recv=sems(layers),
        states=vmem(layers, plane, node_dev, width),
        states_recv=sems(layers),
        lift_own=vmem(layers, edge_dev + vector_rows, width),
        parts=vmem(layers, sections, width + vector_rows, quarter),
        parts_in=vmem(layers, sections, width + vector_rows, quarter),
        parts_recv=sems(layers),
        node_lefts_own=vmem(layers, 3 * node_dev, width),
        node_lefts=vmem(layers, plane, 3 * node_dev, width),
        node_lefts_recv=sems(layers),
        node_rights_own=vmem(layers, sections, 2 * node_dev + vector_rows, quarter),
        node_rights=vmem(layers, plane, 2 * node_dev + vector_rows, quarter),
        node_rights_recv=sems(layers),
        sum_rights_own=vmem(layers, sections, 2 * node_dev, quarter),
        sum_rights=vmem(layers, plane, 2 * node_dev, quarter),
        sum_rights_recv=sems(layers),
    )
    pair_groups = []
    for block in blocks:
        group = dict(
            own=vmem(layers, pairs, 2, block, quarter),
            come=vmem(layers, pairs, 2, block, quarter),
            total=vmem(layers, 2, block, quarter),
            relay=vmem(layers, 2, block, quarter),
            recv=sems(3, layers),
        )
        pair_groups += group.values()
    ins, outs = len(inputs) + len(weights), len(outputs) + len(fulls)
    names = (
        list(inputs)
        + list(range(len(weights)))
        + list(outputs)
        + list(range(len(fulls)))
        + list(scratch)
    )
    plan = SimpleNamespace(
        names=[str(name) for name in names],
        weights=len(inputs),
        fulls=ins + len(outputs),
        pair_groups=ins + outs + len(scratch),
        pair_names=list(group),
        start=dict(zip(matrix_kinds, map(int, starts))),
        layers=layers,
        sections=sections,
        shards=shards,
        node_dev=node_dev,
        edge_dev=edge_dev,
        width=width,
    )
    results = pl.pallas_call(
        functools.partial(kernel, plan),
        out_shape=list(outputs.values()) + fulls,
        in_specs=[pl.BlockSpec(memory_space=pltpu.HBM)] * ins,
        out_specs=[pl.BlockSpec(memory_space=pl.ANY)] * outs,
        scratch_shapes=list(scratch.values()) + pair_groups,
        compiler_params=pltpu.CompilerParams(
            collective_id=0, has_side_effects=True, vmem_limit_bytes=40 << 20
        ),
    )(*(pltpu.with_memory_space_constraint(x, pltpu.HBM) for x in (*inputs.values(), *weights)))
    return pl.pallas_call(
        functools.partial(write_kernel, shards),
        out_shape=list(outputs.values()) + weight_grads,
        in_specs=[pl.BlockSpec(memory_space=pltpu.VMEM)] * outs,
        out_specs=[pl.BlockSpec(memory_space=pltpu.VMEM)] * (len(outputs) + len(weight_grads)),
        compiler_params=pltpu.CompilerParams(vmem_limit_bytes=16 << 20),
    )(*results)


def solution(mesh):
    sections, shards = mesh.shape["section"], mesh.shape["rows"]

    def body(node_features, edge_features, owner, *rest):
        owner = owner.reshape(owner.shape[:-1])
        return fused(sections, shards, node_features, edge_features, owner, *rest)

    in_specs = (
        P(None, "rows", None),
        P(None, "rows", None),
        P(None, "rows", None, None),
        P(None, "rows", None),
        P(None, "rows", None),
        P(None, "rows", None),
    ) + (P(),) * 12
    state = P("section", "rows", None)
    matrix, vector = P(None, "rows", None), P(None, "rows")
    out_specs = (state,) * 3 + (matrix, vector, matrix, vector, vector, vector) * 2
    return jax.shard_map(body, mesh=mesh, in_specs=in_specs, out_specs=out_specs, check_vma=False)
```

```python
import functools
from types import SimpleNamespace

import jax
import jax.numpy as jnp
import numpy as np
from jax import lax
from jax.experimental import pallas as pl
from jax.experimental.pallas import tpu as pltpu
from jax.sharding import PartitionSpec as P

f32 = jnp.float32
bf16 = jnp.bfloat16
MESH = pl.DeviceIdType.MESH
norm_epsilon = 1e-05
vector_rows = 16
e_one, e_bias_one, e_two, e_bias_two, e_gain, e_shift = range(6)
n_one, n_bias_one, n_two, n_bias_two, n_gain, n_shift = range(6, 12)
matrix_kinds = (e_one, e_two, n_one, n_two)
vector_kinds = (e_bias_one, e_bias_two, e_gain, e_shift, n_bias_one, n_bias_two, n_gain, n_shift)
lanes = 128


def dot(left, right):
    return jnp.dot(left, right, preferred_element_type=f32)


def contract_rows(left, right):
    return lax.dot_general(left, right, (((0,), (0,)), ((), ())), preferred_element_type=f32)


def contract_cols(left, right):
    return lax.dot_general(left, right, (((1,), (1,)), ((), ())), preferred_element_type=f32)


def whole_tiles(rows):
    return -(-rows // 16) * 16


def layer_norm(lifted):
    center = lifted - jnp.mean(lifted, axis=-1, keepdims=True)
    scale = lax.rsqrt(jnp.mean(center * center, axis=-1, keepdims=True) + norm_epsilon)
    return center * scale, scale


def activate(pre):
    sigma = jax.nn.sigmoid(pre)
    return (pre * sigma).astype(bf16), sigma * (1.0 + pre * (1.0 - sigma))


def branch_back(grad_branch, gain_row, normed, scale):
    grad_normed = grad_branch * gain_row
    return (
        scale
        * (
            grad_normed
            - jnp.mean(grad_normed, axis=-1, keepdims=True)
            - normed * jnp.mean(grad_normed * normed, axis=-1, keepdims=True)
        )
    ).astype(bf16)


def column_sums(grad_pre, grad_lifted, grad_branch, normed, first):
    rows = [
        jnp.sum(grad_pre.astype(f32), axis=0, keepdims=True),
        jnp.sum(grad_lifted.astype(f32), axis=0, keepdims=True),
        jnp.sum(grad_branch * normed, axis=0, keepdims=True),
        jnp.sum(grad_branch, axis=0, keepdims=True),
    ]
    zeros = jnp.zeros((vector_rows, grad_branch.shape[1]), f32)
    rows = ([zeros[:first]] if first else []) + rows + [zeros[first + 4 :]]
    return jnp.concatenate(rows, axis=0).astype(bf16)


def ended(buffer, sem):
    pltpu.make_async_copy(buffer, buffer, sem).wait()


def kernel(plan, *refs):
    v = SimpleNamespace(**dict(zip(plan.names, refs)))
    layers, sections, shards = plan.layers, plan.sections, plan.shards
    node_dev, edge_dev, width = plan.node_dev, plan.edge_dev, plan.width
    quarter, pairs, plane = width // sections, shards // 2, 2 * sections
    nodes_total = shards * node_dev
    three_rows, two_rows, one_rows = (part * width // shards for part in (3, 2, 1))
    weights = refs[plan.weights : plan.weights + 12]
    section, row = lax.axis_index("section"), lax.axis_index("rows")
    pair, core = row // 2, row % 2
    plane_slot = core * sections + section
    edge_pairs, lift_pairs, node_pairs = (
        SimpleNamespace(
            full=refs[plan.fulls + place],
            **dict(zip(plan.pair_names, refs[plan.pair_groups + 5 * place :])),
        )
        for place in range(3)
    )
    rights = SimpleNamespace(data=v.rights, recv=v.rights_recv)
    node_lefts = SimpleNamespace(data=v.node_lefts, recv=v.node_lefts_recv)
    node_rights = SimpleNamespace(data=v.node_rights, recv=v.node_rights_recv)
    sum_rights = SimpleNamespace(data=v.sum_rights, recv=v.sum_rights_recv)
    target_rights = SimpleNamespace(data=v.target_rights, recv=v.target_rights_recv)

    def drained(count, sem):
        ended(v.drain.at[pl.ds(0, count // lanes)], sem)

    started = SimpleNamespace(total=[0, 0], cores=(0, 1), times=1)

    def count_start(source):
        for one in started.cores:
            started.total[one] += started.times * source.size * source.dtype.itemsize // 2

    def send(source, target, recv_sem, device):
        count_start(source)
        pltpu.make_async_remote_copy(
            src_ref=source,
            dst_ref=target,
            send_sem=v.done,
            recv_sem=recv_sem,
            device_id=device,
            device_id_type=MESH,
        ).start()

    def write(source, target):
        count_start(source)
        pltpu.make_async_copy(source, target, v.done).start()

    def on_core(one, act):
        before = started.cores
        started.cores = tuple(x for x in before if x == one)
        pl.when(core == one)(act)
        started.cores = before

    def each(count, visit):
        if count <= 8:
            for i in range(count):
                visit(i)
        else:
            before = started.times

            def step(i, carry):
                started.times = before * count
                visit(i)
                started.times = before
                return carry

            lax.fori_loop(0, count, step, 0)

    barrier = pltpu.get_barrier_semaphore()

    def greet(device):
        pl.semaphore_signal(barrier, inc=1, device_id=device, device_id_type=MESH)

    each(shards - 1, lambda i: greet((section, (row + 1 + i) % shards)))
    for step in range(1, sections):
        for other in range(2):
            greet(((section + step) % sections, pair * 2 + other))

    def peer_rows(visit):
        if pairs == 4:
            for peer in (3 - pair, (pair + 2) % 4, pair + 1 - 2 * (pair % 2)):
                visit(2 * peer + core)
                visit(2 * peer + 1 - core)
            visit(row + 1 - 2 * core)
        else:
            each(shards - 1, lambda i: visit((row + 1 + i) % shards))

    def send_nodes(layer, source):
        def one(peer):
            send(source, v.nodes.at[layer, row], v.nodes_recv.at[layer], (section, peer))

        peer_rows(one)

    def send_sums(layer):
        ended(v.mate_sums.at[layer], v.mate_sums_recv.at[layer])
        both = v.sums[layer, core].astype(f32) + v.mate_sums[layer].astype(f32)
        v.both_sums[layer] = both.astype(bf16)

        def one(peer):
            send(
                v.both_sums.at[layer, peer],
                v.sums_in.at[layer, pair],
                v.sums_recv.at[layer],
                (section, peer * 2 + core),
            )

        peer_pairs(one)

    def peer_pairs(visit):
        if pairs == 4:
            for peer in (3 - pair, (pair + 2) % 4, pair + 1 - 2 * (pair % 2)):
                visit(peer)
        else:
            each(pairs - 1, lambda i: visit((pair + 1 + i) % pairs))

    def send_sums_alone():
        def one(peer, other):
            send(
                v.sums.at[0, other, peer],
                v.sums_all.at[row],
                v.sums_recv.at[0],
                (section, peer * 2 + other),
            )

        def both(peer):
            one(peer, core)
            one(peer, 1 - core)

        peer_pairs(both)
        one(pair, 1 - core)

    def from_rows(data, sem, layer):
        ended(data.at[layer, pl.ds(0, shards - 1)], sem.at[layer])

    def to_plane(group, layer, sources):
        def one(target_section, other):
            source = sources[other](target_section)
            send(
                source,
                group.data.at[layer, plane_slot, pl.ds(0, source.shape[0])],
                group.recv.at[layer],
                (target_section, pair * 2 + other),
            )

        def keep(other):
            source = sources[other](section)
            group.data[layer, plane_slot, 0 : source.shape[0]] = source[...]

        for other in range(2):
            if sources[other] is not None:
                for step in range(1, sections):
                    one((section + step) % sections, other)
                on_core(1 - other, functools.partial(one, section, other))
                on_core(other, functools.partial(keep, other))

    def from_plane(group, layer, rows):
        drained((plane - 1) * rows * group.data.shape[-1], group.recv.at[layer])

    def to_mate(taker, target, recv_sem, source):
        target = target.at[pl.ds(0, source.shape[0])]
        mate = (section, row + 1 - 2 * core)
        on_core(1 - taker, lambda: send(source, target, recv_sem, mate))

    def send_parts(layer, rows):
        for step in range(1, sections):
            target = (section + step) % sections
            send(
                v.parts.at[layer, target, pl.ds(0, rows)],
                v.parts_in.at[layer, section, pl.ds(0, rows)],
                v.parts_recv.at[layer],
                (target, row),
            )

    def send_pairs(group, layer, relay, outer=True, inner=True):
        def one(peer):
            send(
                group.own.at[layer, peer],
                group.come.at[layer, pair],
                group.recv.at[0, layer],
                (section, peer * 2 + core),
            )

        if not relay:
            peer_pairs(one)
            return
        mirror = pairs - 1 - pair

        @pl.when(pair % 3 == 0)
        def _():
            near = (pair + 3) // 3
            if outer:
                send(
                    group.own.at[layer, mirror],
                    group.relay.at[layer],
                    group.recv.at[2, layer],
                    (section, near * 2 + core),
                )
            if inner:
                one(near)
                one(3 - near)

        before, started.cores = started.cores, ()

        @pl.when(pair % 3 != 0)
        def _():
            if outer:
                one(3 * (pair - 1))
            if inner:
                one(mirror)

        started.cores = before

    def relay_pairs(group, layer):
        before, started.cores = started.cores, ()

        @pl.when(pair % 3 != 0)
        def _():
            far = 3 - 3 * (pair - 1)
            ended(group.relay.at[layer], group.recv.at[2, layer])
            group.own[layer, far] = (
                group.own[layer, far].astype(f32) + group.relay[layer].astype(f32)
            ).astype(bf16)
            send(
                group.own.at[layer, far],
                group.come.at[layer, pair],
                group.recv.at[0, layer],
                (section, far * 2 + core),
            )

        started.cores = before

    def add_pairs(group, layer, relay):
        def add(peers):
            ended(group.come.at[layer, pl.ds(0, len(peers))], group.recv.at[0, layer])
            total = group.own[layer, pair].astype(f32)
            for peer in peers:
                total = total + group.come[layer, peer].astype(f32)
            group.total[layer] = total.astype(bf16)

        if relay:
            pl.when(pair % 3 == 0)(lambda: add([1, 2]))
            pl.when(pair % 3 != 0)(lambda: add([(pair + step) % 4 for step in (1, 2, 3)]))
        else:
            add([(pair + step) % pairs for step in range(1, pairs)])

        def share(target_section, other):
            send(
                group.total.at[layer, other],
                group.full.at[layer, section],
                group.recv.at[1, layer],
                (target_section, pair * 2 + other),
            )

        for step in range(1, sections):
            for other in range(2):
                share((section + step) % sections, other)
        share(section, 1 - core)
        write(group.total.at[layer, core], group.full.at[layer, section])

    def from_givers(group, layer, giver):
        def wait(other):
            slots = sections - 1 if other == giver else sections
            ended(group.full.at[layer, pl.ds(0, slots)], group.recv.at[1, layer])

        for other in range(2):
            on_core(other, functools.partial(wait, other))

    def store_blocks(target, product, offset, rows, owners=range(shards)):
        padded = whole_tiles(rows)
        for owner in owners:
            block = product[owner * rows : (owner + 1) * rows]
            if padded != rows:
                block = jnp.concatenate([block, jnp.zeros((padded - rows, quarter), f32)], axis=0)
            target[owner // 2, owner % 2, offset : offset + padded] = block.astype(bf16)

    def store_vectors(target, total, offset):
        for owner in range(shards):
            target[owner // 2, owner % 2, offset : offset + vector_rows] = total.astype(bf16)

    def quarters(target, offset, value):
        rows = value.shape[0]
        for part in range(sections):
            target[part, offset : offset + rows] = value[
                :, part * quarter : (part + 1) * quarter
            ].astype(bf16)

    def vector(kind, layer):
        return v.vectors[vector_kinds.index(kind)].astype(f32)[layer : layer + 1]

    pl.semaphore_wait(barrier, shards - 1 + 2 * (sections - 1))
    send_nodes(0, v.node_features.at[section])

    def load(source, target, sem):
        pltpu.make_async_copy(source, target, v.load_sem.at[sem]).start()

    def load_matrix(kind, layer, sem):
        rows = weights[kind].shape[1]
        target = v.matrices.at[layer, pl.ds(plan.start[kind], rows)]
        load(weights[kind].at[layer], target, sem)

    def matrix(kind, layer, first=0, count=None):
        rows = weights[kind].shape[1] if count is None else count * width
        start = plan.start[kind] + first * width
        return v.matrices[layer, start : start + rows]

    def loaded(target, sem):
        ended(target, v.load_sem.at[sem])

    load(v.node_features.at[section], v.nodes.at[0, row], 0)
    load(v.edge_features.at[section], v.edge_in.at[0], 1)
    load_matrix(e_one, 0, 2)
    for place, source in enumerate((v.owner, v.local, v.receivers)):
        load(source.at[section], v.index.at[place], 3 + place)
    for place, kind in enumerate(vector_kinds):
        load(weights[kind], v.vectors.at[place], 6 + place)
    for kind in (e_two, n_one, n_two):
        load_matrix(kind, 0, 14)
    for layer in range(1, layers):
        for kind in matrix_kinds:
            load_matrix(kind, layer, 14 + layer)
    load(v.cotangent.at[section], v.cotangent_v, 14 + layers)

    on_core(0, lambda: load(v.edge_features, v.lefts.at[pl.ds(0, sections)], 15 + layers))
    to_mate(0, v.lefts.at[pl.ds(sections, sections)], v.lefts_recv, v.edge_features)

    loaded(v.nodes.at[0, row], 0)
    loaded(v.edge_in.at[0], 1)

    for place in range(3):
        loaded(v.index.at[place], 3 + place)
    sender_row, target_row = v.index[0] * node_dev + v.index[1], v.index[2]
    eye = lax.broadcasted_iota(jnp.int32, (edge_dev, edge_dev), 0) == lax.broadcasted_iota(
        jnp.int32, (edge_dev, edge_dev), 1
    )

    def to_column(values):
        spread = jnp.broadcast_to(values, (edge_dev, edge_dev))
        column = jnp.sum(jnp.where(eye, spread, 0).astype(f32), axis=1, keepdims=True)
        return column.astype(jnp.int32)

    def one_hot(values, count, axis):
        places = (count, edge_dev) if axis == 0 else (edge_dev, count)
        match = lax.broadcasted_iota(jnp.int32, places, axis) == values
        return jnp.where(match, 1.0, 0.0).astype(bf16)

    v.from_nodes[...] = one_hot(to_column(sender_row), nodes_total, 1)
    v.to_nodes[...] = one_hot(sender_row, nodes_total, 0)
    v.from_targets[...] = one_hot(to_column(target_row), node_dev, 1)
    v.to_targets[...] = one_hot(target_row, node_dev, 0)
    for place in range(len(vector_kinds)):
        loaded(v.vectors.at[place], 6 + place)

    def edge_forward(layer):
        node = v.nodes[layer, row]
        edge = v.edge_in[layer]
        if layer == 0:
            loaded(v.matrices.at[0, pl.ds(0, 3 * width)], 2)
        else:
            loaded(v.matrices.at[layer], 14 + layer)
        received = dot(v.from_targets[...], node).astype(bf16)
        v.work[...] = (
            dot(edge, matrix(e_one, layer, 0, 1))
            + dot(received, matrix(e_one, layer, 2, 1))
            + vector(e_bias_one, layer)
        )
        if layer == 0:
            loaded(v.matrices.at[0, pl.ds(3 * width, v.matrices.shape[1] - 3 * width)], 14)
        v.node_work[...] = dot(node, matrix(n_one, layer, 0, 1)) + vector(n_bias_one, layer)
        from_rows(v.nodes, v.nodes_recv, layer)
        sent = dot(v.from_nodes[...], v.nodes[layer].reshape(nodes_total, width)).astype(bf16)
        hidden, slope = activate(
            v.work[...] + dot(sent, matrix(e_one, layer, 1, 1))
        )
        v.edge_hidden[layer] = hidden
        v.edge_slope[layer] = slope
        to_mate(1, v.mate_left.at[layer], v.mate_recv.at[layer], v.edge_hidden.at[layer])
        normed, scale = layer_norm(
            dot(hidden, matrix(e_two, layer)) + vector(e_bias_two, layer)
        )
        v.edge_normed[layer] = normed
        v.edge_scale[layer] = scale
        edge = (
            edge.astype(f32)
            + (normed * vector(e_gain, layer) + vector(e_shift, layer))
        ).astype(bf16)
        if layer + 1 < layers:
            v.edge_in[layer + 1] = edge
            to_mate(
                0, v.pre_left.at[layer + 1], v.pre_recv.at[layer + 1], v.edge_in.at[layer + 1]
            )
        return node, dot(v.to_targets[...], edge).astype(bf16)

    def node_forward(layer, node, gathered):
        hidden, slope = activate(
            v.node_work[...] + dot(gathered, matrix(n_one, layer, 1, 1))
        )
        v.node_slope[layer] = slope
        normed, scale = layer_norm(
            dot(hidden, matrix(n_two, layer)) + vector(n_bias_two, layer)
        )
        v.node_normed[layer] = normed
        v.node_scale[layer] = scale
        new_node = (
            node.astype(f32)
            + (normed * vector(n_gain, layer) + vector(n_shift, layer))
        ).astype(bf16)
        if layer + 1 < layers:
            v.nodes[layer + 1, row] = new_node
            send_nodes(layer + 1, v.nodes.at[layer + 1, row])
        else:
            v.final_v[0] = new_node
            write(v.final_v, v.final)
        v.node_lefts_own[layer, 0:node_dev] = node
        v.node_lefts_own[layer, node_dev : 2 * node_dev] = gathered
        v.node_lefts_own[layer, 2 * node_dev : 3 * node_dev] = hidden
        to_plane(node_lefts, layer, (None, lambda s: v.node_lefts_own.at[layer]))

    for layer in range(layers):
        node, gathered = edge_forward(layer)
        node_forward(layer, node, gathered)

    def hand_states(layer):
        def act():
            from_plane(node_lefts, layer, 3 * node_dev)
            send(
                v.node_lefts.at[layer, :, pl.ds(0, node_dev)],
                v.states.at[layer],
                v.states_recv.at[layer],
                (section, row + 1 - 2 * core),
            )

        on_core(1, act)

    def node_products(layer, relay):
        def act():
            from_plane(node_rights, layer, 2 * node_dev + vector_rows)
            own = plane * node_dev
            state = v.node_lefts[layer, :, 0:node_dev].reshape(own, width)
            gathered = v.node_lefts[layer, :, node_dev : 2 * node_dev].reshape(own, width)
            hidden = v.node_lefts[layer, :, 2 * node_dev : 3 * node_dev].reshape(own, width)
            grad_pre = v.node_rights[layer, :, 0:node_dev].reshape(own, quarter)
            grad_lifted = v.node_rights[layer, :, node_dev : 2 * node_dev].reshape(own, quarter)
            vectors = v.node_rights[layer, :, 2 * node_dev : 2 * node_dev + vector_rows]
            v.product[0:width] = contract_rows(state, grad_pre)
            v.product[width : 2 * width] = contract_rows(gathered, grad_pre)
            v.product[2 * width : 3 * width] = contract_rows(hidden, grad_lifted)
            target = node_pairs.own.at[layer]
            store_blocks(target, v.product, 0, two_rows)
            start = whole_tiles(two_rows)
            store_blocks(target, v.product.at[pl.ds(2 * width, width)], start, one_rows)
            v.node_vectors[layer] = jnp.sum(vectors.astype(f32), axis=0)
            send_pairs(node_pairs, layer, relay)

        on_core(1, act)

    def edge_parts(layer):
        def multiply(lefts, rights):
            left = jnp.concatenate(lefts, axis=0)
            right = jnp.concatenate(rights, axis=0)
            for part in range(sections):
                columns = slice(part * quarter, (part + 1) * quarter)
                v.parts[layer, part, 0:width] = contract_rows(left, right[:, columns]).astype(bf16)

        def act_one():
            drained(2 * edge_dev * width, v.pre_recv.at[layer])
            multiply([v.edge_in[layer], v.pre_left[layer]], [v.pre_own[layer], v.pre_right[layer]])
            send_parts(layer, width)

        def act_two():
            drained((2 * edge_dev + vector_rows) * width, v.mate_recv.at[layer])
            multiply(
                [v.edge_hidden[layer], v.mate_left[layer]],
                [v.lift_own[layer, 0:edge_dev], v.mate_right[layer, 0:edge_dev]],
            )
            vectors = (
                v.lift_own[layer, edge_dev : edge_dev + vector_rows].astype(f32)
                + v.mate_right[layer, edge_dev : edge_dev + vector_rows].astype(f32)
            ).astype(bf16)
            for part in range(sections):
                columns = slice(part * quarter, (part + 1) * quarter)
                v.parts[layer, part, width : width + vector_rows] = vectors[:, columns]
            send_parts(layer, width + vector_rows)

        if layer > 0:
            on_core(0, act_one)
        on_core(1, act_two)

    def from_parts(layer, rows):
        drained((sections - 1) * rows * quarter, v.parts_recv.at[layer])

    def add_parts(layer, start, rows):
        total = v.parts[layer, section, start : start + rows].astype(f32)
        for step in range(1, sections):
            other = (section + step) % sections
            total = total + v.parts_in[layer, other, start : start + rows].astype(f32)
        return total

    outer_owners = [0, 1, shards - 2, shards - 1]
    inner_owners = [owner for owner in range(shards) if owner not in outer_owners]

    def state_products(layer, group, place):
        own = plane * node_dev
        from_plane(group, layer, node_dev)
        v.edge_product[layer, place * width : (place + 1) * width] = contract_rows(
            v.states[layer].reshape(own, width), group.data[layer].reshape(own, quarter)
        )

    def edge_products(layer, relay):
        def act():
            if layer == 0:
                loaded(v.lefts.at[pl.ds(0, sections)], 15 + layers)
                ended(v.lefts.at[pl.ds(sections, sections)], v.lefts_recv)
                from_plane(rights, 0, edge_dev)
                v.edge_product[0, 0:width] = contract_rows(
                    v.lefts[...].reshape(plane * edge_dev, width),
                    v.rights[0].reshape(plane * edge_dev, quarter),
                )
            else:
                from_parts(layer, width)
                v.edge_product[layer, 0:width] = add_parts(layer, 0, width)
            ended(v.states.at[layer], v.states_recv.at[layer])
            state_products(layer, target_rights, 2)
            if relay:
                blocks, product = edge_pairs.own.at[layer], v.edge_product.at[layer]
                store_blocks(blocks, product, 0, three_rows, outer_owners)
                send_pairs(edge_pairs, layer, True, inner=False)

        on_core(0, act)

    def sender_products(layer, relay):
        def act():
            state_products(layer, sum_rights, 1)
            owners = inner_owners if relay else range(shards)
            blocks, product = edge_pairs.own.at[layer], v.edge_product.at[layer]
            store_blocks(blocks, product, 0, three_rows, owners)
            send_pairs(edge_pairs, layer, relay, outer=False)

        on_core(0, act)

    def lift_products(layer, relay):
        def act():
            from_parts(layer, width + vector_rows)
            v.product[0:width] = add_parts(layer, 0, width)
            target = lift_pairs.own.at[layer]
            store_blocks(target, v.product, 0, one_rows)
            vectors = add_parts(layer, width, vector_rows) + v.node_vectors[layer]
            store_vectors(target, vectors, whole_tiles(one_rows))
            send_pairs(lift_pairs, layer, relay)

        on_core(1, act)

    def relay_products(group, giver, layer, relay):
        if relay:
            on_core(giver, lambda: relay_pairs(group, layer))

    def add_products(group, giver, layer, relay):
        on_core(giver, lambda: add_pairs(group, layer, relay))

    def node_backward(layer):
        grad_branch = v.grad_node[...]
        normed = v.node_normed[layer]
        grad_lifted = branch_back(
            grad_branch, vector(n_gain, layer), normed, v.node_scale[layer]
        )
        grad_hidden = contract_cols(grad_lifted, matrix(n_two, layer))
        grad_pre = (grad_hidden * v.node_slope[layer]).astype(bf16)
        aggregate = contract_cols(grad_pre, matrix(n_one, layer, 1, 1))
        high = aggregate.astype(bf16)
        low = (aggregate - high.astype(f32)).astype(bf16)
        grad_edge = dot(v.from_targets[...], high) + dot(v.from_targets[...], low)
        if layer + 1 < layers:
            grad_edge = grad_edge + v.grad_edge[...]
        v.grad_edge[...] = grad_edge.astype(bf16).astype(f32)
        target = v.node_rights_own.at[layer]
        quarters(target, 0, grad_pre)
        quarters(target, node_dev, grad_lifted)
        quarters(target, 2 * node_dev, column_sums(grad_pre, grad_lifted, grad_branch, normed, 4))
        to_plane(node_rights, layer, (None, lambda s: v.node_rights_own.at[layer, s]))
        return grad_branch, grad_pre

    def node_backward_rest(layer, grad_branch, grad_pre):
        grad_node = grad_branch + contract_cols(grad_pre, matrix(n_one, layer, 0, 1))
        v.grad_node[...] = grad_node.astype(bf16).astype(f32)

    def edge_backward(layer, rest):
        grad_branch = v.grad_edge[...]
        normed = v.edge_normed[layer]
        grad_lifted = branch_back(
            grad_branch, vector(e_gain, layer), normed, v.edge_scale[layer]
        )
        grad_hidden = contract_cols(grad_lifted, matrix(e_two, layer))
        grad_pre = (grad_hidden * v.edge_slope[layer]).astype(bf16)
        sums = dot(v.to_nodes[...], grad_pre).astype(bf16)
        for place in range(shards):
            block = sums[place * node_dev : (place + 1) * node_dev]
            v.sums[layer, place % 2, place // 2] = block
        mate = (section, row + 1 - 2 * core)
        if layer == 0:
            send_sums_alone()
        else:
            send(
                v.sums.at[layer, 1 - core], v.mate_sums.at[layer], v.mate_sums_recv.at[layer], mate
            )
        if layer == 0:
            quarters(v.pre_rights_own, 0, grad_pre)
            to_plane(rights, 0, (lambda s: v.pre_rights_own.at[s], None))
        else:
            v.pre_own[layer] = grad_pre
            to_mate(0, v.pre_right.at[layer], v.pre_recv.at[layer], v.pre_own.at[layer])
        v.lift_own[layer, 0:edge_dev] = grad_lifted
        v.lift_own[layer, edge_dev : edge_dev + vector_rows] = column_sums(
            grad_pre, grad_lifted, grad_branch, normed, 0
        )
        to_mate(1, v.mate_right.at[layer], v.mate_recv.at[layer], v.lift_own.at[layer])
        node_backward_rest(layer, *rest)
        if layer > 0:
            send_sums(layer)
        grad_edge = grad_branch + contract_cols(grad_pre, matrix(e_one, layer, 0, 1))
        by_target = dot(v.to_targets[...], grad_pre).astype(bf16)
        quarters(v.target_rights_own.at[layer], 0, by_target)
        to_plane(target_rights, layer, (lambda s: v.target_rights_own.at[layer, s], None))
        v.grad_node[...] = v.grad_node[...] + contract_cols(
            by_target, matrix(e_one, layer, 2, 1)
        )
        if layer > 0:
            v.grad_edge[...] = grad_edge.astype(bf16).astype(f32)
        else:
            v.grad_edges_v[0] = grad_edge
            write(v.grad_edges_v, v.grad_edges)

    def sender_backward(layer):
        if layer == 0:
            ended(v.sums_all.at[pl.ds(0, shards - 1)], v.sums_recv.at[0])
            v.sums_all[row] = v.sums[0, core, pair]
            parts = v.sums_all[...]
        else:
            ended(v.sums_in.at[layer, pl.ds(0, pairs - 1)], v.sums_recv.at[layer])
            v.sums_in[layer, pair] = v.both_sums[layer, pair]
            parts = v.sums_in[layer]
        by_sender = jnp.sum(parts.astype(f32), axis=0).astype(bf16)
        target = v.sum_rights_own.at[layer]
        quarters(target, 0, by_sender)
        to_plane(sum_rights, layer, (lambda s: v.sum_rights_own.at[layer, s], None))
        grad_node = v.grad_node[...] + contract_cols(
            by_sender, matrix(e_one, layer, 1, 1)
        )
        if layer > 0:
            v.grad_node[...] = grad_node.astype(bf16).astype(f32)
        else:
            v.grad_nodes_v[0] = grad_node
            write(v.grad_nodes_v, v.grad_nodes)

    loaded(v.cotangent_v, 14 + layers)
    v.grad_node[...] = v.cotangent_v[...].astype(f32)
    relay = pairs == 4
    later = list(reversed(range(1, layers)))
    for layer in later:
        edge_backward(layer, node_backward(layer))
        edge_parts(layer)
        sender_backward(layer)
        hand_states(layer)
        node_products(layer, relay)
    edge_backward(0, node_backward(0))
    edge_parts(0)
    hand_states(0)
    for layer in later + [0]:
        edge_products(layer, relay)
    for layer in later:
        sender_products(layer, relay)
        lift_products(layer, relay)
        relay_products(node_pairs, 1, layer, relay)
        relay_products(lift_pairs, 1, layer, relay)
    node_products(0, relay)
    sender_backward(0)
    for layer in later + [0]:
        relay_products(edge_pairs, 0, layer, relay)
    sender_products(0, relay)
    lift_products(0, relay)
    relay_products(node_pairs, 1, 0, relay)
    relay_products(lift_pairs, 1, 0, relay)
    for layer in later + [0]:
        add_products(node_pairs, 1, layer, relay)
        add_products(lift_pairs, 1, layer, relay)
        add_products(edge_pairs, 0, layer, relay)

    for layer in range(layers):
        from_givers(edge_pairs, layer, 0)
        from_givers(lift_pairs, layer, 1)
        from_givers(node_pairs, layer, 1)
    for one in range(2):
        pl.when(core == one)(
            lambda: drained(started.total[one], v.done)
        )


def write_kernel(shards, *refs):
    final, grad_nodes, grad_edges, edge_full, lift_full, node_full = refs[:6]
    out_final, out_nodes, out_edges = refs[6:9]
    grads = refs[9:]
    row = lax.axis_index("rows")
    layers, sections, quarter = edge_full.shape[0], edge_full.shape[1], edge_full.shape[3]
    width = sections * quarter
    three_rows, two_rows, one_rows = (part * width // shards for part in (3, 2, 1))
    node_start = whole_tiles(two_rows)
    out_final[...] = final[...]
    out_nodes[...] = grad_nodes[...]
    out_edges[...] = grad_edges[...]

    def put(target, full, start, rows):
        for layer in range(layers):
            for part in range(sections):
                value = full[layer, part, start : start + whole_tiles(rows)]
                target[layer, :, part * quarter : (part + 1) * quarter] = value.astype(f32)[0:rows]

    put(grads[e_one], edge_full, 0, three_rows)
    put(grads[e_two], lift_full, 0, one_rows)
    put(grads[n_one], node_full, 0, two_rows)
    put(grads[n_two], node_full, node_start, one_rows)

    def take_columns(value):
        per = quarter // one_rows
        taken = jnp.zeros((vector_rows, one_rows), f32)
        for place in range(per):
            taken = taken + jnp.where(
                row % per == place, value[:, place * one_rows : (place + 1) * one_rows], 0.0
            )
        return taken

    holder = row // (quarter // one_rows)
    for layer in range(layers):
        start = whole_tiles(one_rows)
        taken = take_columns(lift_full[layer, holder, start : start + vector_rows].astype(f32))
        for place, kind in enumerate(vector_kinds):
            grads[kind][layer : layer + 1] = taken[place : place + 1]


def fused(sections, shards, node_features, edge_features, owner, local, receivers, cotangent, *weights):
    micro_count, node_dev, width = node_features.shape
    edge_dev = edge_features.shape[1]
    layers = weights[0].shape[0]
    quarter, pairs, plane = width // sections, shards // 2, 2 * sections
    nodes_total = shards * node_dev

    def shape(*dims, kind=f32):
        return jax.ShapeDtypeStruct(dims, kind)

    def vmem(*dims, kind=bf16):
        return pltpu.VMEM(dims, kind)

    def sems(*dims):
        return pltpu.SemaphoreType.DMA(dims)

    inputs = dict(
        node_features=node_features,
        edge_features=edge_features,
        owner=owner,
        local=local,
        receivers=receivers,
        cotangent=cotangent,
    )
    outputs = dict(
        final=shape(1, node_dev, width, kind=bf16),
        grad_nodes=shape(1, node_dev, width),
        grad_edges=shape(1, edge_dev, width),
    )
    weight_grads = [
        shape(layers, weight.shape[1] // shards, *weight.shape[2:]) for weight in weights
    ]
    lift_block = whole_tiles(width // shards) + vector_rows
    blocks = (
        whole_tiles(3 * width // shards),
        lift_block,
        whole_tiles(2 * width // shards) + whole_tiles(width // shards),
    )
    fulls = [shape(layers, sections, block, quarter, kind=bf16) for block in blocks]
    starts = np.cumsum([0] + [weights[kind].shape[1] for kind in matrix_kinds])
    scratch = dict(
        done=pltpu.SemaphoreType.DMA,
        drain=vmem(1024 * (24 + shards // 2), lanes),
        load_sem=sems(16 + layers),
        index=vmem(3, 1, edge_dev, kind=jnp.int32),
        vectors=vmem(len(vector_kinds), layers, width),
        matrices=vmem(layers, int(starts[-1]), width),
        cotangent_v=vmem(node_dev, width),
        from_nodes=vmem(edge_dev, nodes_total),
        to_nodes=vmem(nodes_total, edge_dev),
        from_targets=vmem(edge_dev, node_dev),
        to_targets=vmem(node_dev, edge_dev),
        work=vmem(edge_dev, width, kind=f32),
        node_work=vmem(node_dev, width, kind=f32),
        grad_node=vmem(node_dev, width, kind=f32),
        grad_edge=vmem(edge_dev, width, kind=f32),
        product=vmem(3 * width, quarter, kind=f32),
        edge_in=vmem(layers, edge_dev, width),
        edge_hidden=vmem(layers, edge_dev, width),
        edge_slope=vmem(layers, edge_dev, width, kind=f32),
        edge_normed=vmem(layers, edge_dev, width, kind=f32),
        edge_scale=vmem(layers, edge_dev, 1, kind=f32),
        node_slope=vmem(layers, node_dev, width, kind=f32),
        node_normed=vmem(layers, node_dev, width, kind=f32),
        node_scale=vmem(layers, node_dev, 1, kind=f32),
        nodes=vmem(layers, shards, node_dev, width),
        nodes_recv=sems(layers),
        sums=vmem(layers, 2, pairs, node_dev, width),
        mate_sums=vmem(layers, pairs, node_dev, width),
        mate_sums_recv=sems(layers),
        both_sums=vmem(layers, pairs, node_dev, width),
        sums_in=vmem(layers, pairs, node_dev, width),
        sums_all=vmem(shards, node_dev, width),
        sums_recv=sems(layers),
        final_v=vmem(1, node_dev, width),
        grad_nodes_v=vmem(1, node_dev, width, kind=f32),
        grad_edges_v=vmem(1, edge_dev, width, kind=f32),
        node_vectors=vmem(layers, vector_rows, quarter, kind=f32),
        mate_left=vmem(layers, edge_dev, width),
        mate_right=vmem(layers, edge_dev + vector_rows, width),
        mate_recv=sems(layers),
        lefts=vmem(plane, edge_dev, width),
        lefts_recv=pltpu.SemaphoreType.DMA,
        pre_rights_own=vmem(sections, edge_dev, quarter),
        rights=vmem(1, plane, edge_dev, quarter),
        rights_recv=sems(1),
        pre_own=vmem(layers, edge_dev, width),
        pre_left=vmem(layers, edge_dev, width),
        pre_right=vmem(layers, edge_dev, width),
        pre_recv=sems(layers),
        states=vmem(layers, plane, node_dev, width),
        states_recv=sems(layers),
        lift_own=vmem(layers, edge_dev + vector_rows, width),
        parts=vmem(layers, sections, width + vector_rows, quarter),
        parts_in=vmem(layers, sections, width + vector_rows, quarter),
        parts_recv=sems(layers),
        node_lefts_own=vmem(layers, 3 * node_dev, width),
        node_lefts=vmem(layers, plane, 3 * node_dev, width),
        node_lefts_recv=sems(layers),
        node_rights_own=vmem(layers, sections, 2 * node_dev + vector_rows, quarter),
        node_rights=vmem(layers, plane, 2 * node_dev + vector_rows, quarter),
        node_rights_recv=sems(layers),
        edge_product=vmem(layers, 3 * width, quarter, kind=f32),
        target_rights_own=vmem(layers, sections, node_dev, quarter),
        target_rights=vmem(layers, plane, node_dev, quarter),
        target_rights_recv=sems(layers),
        sum_rights_own=vmem(layers, sections, node_dev, quarter),
        sum_rights=vmem(layers, plane, node_dev, quarter),
        sum_rights_recv=sems(layers),
    )
    pair_groups = []
    for block in blocks:
        group = dict(
            own=vmem(layers, pairs, 2, block, quarter),
            come=vmem(layers, pairs, 2, block, quarter),
            total=vmem(layers, 2, block, quarter),
            relay=vmem(layers, 2, block, quarter),
            recv=sems(3, layers),
        )
        pair_groups += group.values()
    ins, outs = len(inputs) + len(weights), len(outputs) + len(fulls)
    names = (
        list(inputs)
        + list(range(len(weights)))
        + list(outputs)
        + list(range(len(fulls)))
        + list(scratch)
    )
    plan = SimpleNamespace(
        names=[str(name) for name in names],
        weights=len(inputs),
        fulls=ins + len(outputs),
        pair_groups=ins + outs + len(scratch),
        pair_names=list(group),
        start=dict(zip(matrix_kinds, map(int, starts))),
        layers=layers,
        sections=sections,
        shards=shards,
        node_dev=node_dev,
        edge_dev=edge_dev,
        width=width,
    )
    results = pl.pallas_call(
        functools.partial(kernel, plan),
        out_shape=list(outputs.values()) + fulls,
        in_specs=[pl.BlockSpec(memory_space=pltpu.HBM)] * ins,
        out_specs=[pl.BlockSpec(memory_space=pl.ANY)] * outs,
        scratch_shapes=list(scratch.values()) + pair_groups,
        compiler_params=pltpu.CompilerParams(
            collective_id=0, has_side_effects=True, vmem_limit_bytes=40 << 20
        ),
    )(*(pltpu.with_memory_space_constraint(x, pltpu.HBM) for x in (*inputs.values(), *weights)))
    return pl.pallas_call(
        functools.partial(write_kernel, shards),
        out_shape=list(outputs.values()) + weight_grads,
        in_specs=[pl.BlockSpec(memory_space=pltpu.VMEM)] * outs,
        out_specs=[pl.BlockSpec(memory_space=pltpu.VMEM)] * (len(outputs) + len(weight_grads)),
        compiler_params=pltpu.CompilerParams(vmem_limit_bytes=16 << 20),
    )(*results)


def solution(mesh):
    sections, shards = mesh.shape["section"], mesh.shape["rows"]

    def body(node_features, edge_features, owner, *rest):
        owner = owner.reshape(owner.shape[:-1])
        return fused(sections, shards, node_features, edge_features, owner, *rest)

    in_specs = (
        P(None, "rows", None),
        P(None, "rows", None),
        P(None, "rows", None, None),
        P(None, "rows", None),
        P(None, "rows", None),
        P(None, "rows", None),
    ) + (P(),) * 12
    state = P("section", "rows", None)
    matrix, vector = P(None, "rows", None), P(None, "rows")
    out_specs = (state,) * 3 + (matrix, vector, matrix, vector, vector, vector) * 2
    return jax.shard_map(body, mesh=mesh, in_specs=in_specs, out_specs=out_specs, check_vma=False)
```

```python
import functools
from types import SimpleNamespace

import jax
import jax.numpy as jnp
import numpy as np
from jax import lax
from jax.experimental import pallas as pl
from jax.experimental.pallas import tpu as pltpu
from jax.sharding import PartitionSpec as P

f32 = jnp.float32
bf16 = jnp.bfloat16
MESH = pl.DeviceIdType.MESH
norm_epsilon = 1e-05
vector_rows = 16
e_one, e_bias_one, e_two, e_bias_two, e_gain, e_shift = range(6)
n_one, n_bias_one, n_two, n_bias_two, n_gain, n_shift = range(6, 12)
matrix_kinds = (e_one, e_two, n_one, n_two)
vector_kinds = (e_bias_one, e_bias_two, e_gain, e_shift, n_bias_one, n_bias_two, n_gain, n_shift)
lanes = 128


def dot(left, right):
    return jnp.dot(left, right, preferred_element_type=f32)


def contract_rows(left, right):
    return lax.dot_general(left, right, (((0,), (0,)), ((), ())), preferred_element_type=f32)


def contract_cols(left, right):
    return lax.dot_general(left, right, (((1,), (1,)), ((), ())), preferred_element_type=f32)


def whole_tiles(rows):
    return -(-rows // 16) * 16


def layer_norm(lifted):
    center = lifted - jnp.mean(lifted, axis=-1, keepdims=True)
    scale = lax.rsqrt(jnp.mean(center * center, axis=-1, keepdims=True) + norm_epsilon)
    return center * scale, scale


def activate(pre):
    sigma = jax.nn.sigmoid(pre)
    return (pre * sigma).astype(bf16), sigma * (1.0 + pre * (1.0 - sigma))


def branch_back(grad_branch, gain_row, normed, scale):
    grad_normed = grad_branch * gain_row
    return (
        scale
        * (
            grad_normed
            - jnp.mean(grad_normed, axis=-1, keepdims=True)
            - normed * jnp.mean(grad_normed * normed, axis=-1, keepdims=True)
        )
    ).astype(bf16)


def column_sums(grad_pre, grad_lifted, grad_branch, normed, first):
    rows = [
        jnp.sum(grad_pre.astype(f32), axis=0, keepdims=True),
        jnp.sum(grad_lifted.astype(f32), axis=0, keepdims=True),
        jnp.sum(grad_branch * normed, axis=0, keepdims=True),
        jnp.sum(grad_branch, axis=0, keepdims=True),
    ]
    zeros = jnp.zeros((vector_rows, grad_branch.shape[1]), f32)
    rows = ([zeros[:first]] if first else []) + rows + [zeros[first + 4 :]]
    return jnp.concatenate(rows, axis=0).astype(bf16)


def ended(buffer, sem):
    pltpu.make_async_copy(buffer, buffer, sem).wait()


def kernel(plan, *refs):
    v = SimpleNamespace(**dict(zip(plan.names, refs)))
    layers, sections, shards = plan.layers, plan.sections, plan.shards
    node_dev, edge_dev, width = plan.node_dev, plan.edge_dev, plan.width
    quarter, pairs, plane = width // sections, shards // 2, 2 * sections
    nodes_total = shards * node_dev
    three_rows, two_rows, one_rows = (part * width // shards for part in (3, 2, 1))
    weights = refs[plan.weights : plan.weights + 12]
    section, row = lax.axis_index("section"), lax.axis_index("rows")
    pair, core = row // 2, row % 2
    plane_slot = core * sections + section
    edge_pairs, lift_pairs, node_pairs = (
        SimpleNamespace(
            full=refs[plan.fulls + place],
            **dict(zip(plan.pair_names, refs[plan.pair_groups + 5 * place :])),
        )
        for place in range(3)
    )
    rights = SimpleNamespace(data=v.rights, recv=v.rights_recv)
    node_lefts = SimpleNamespace(data=v.node_lefts, recv=v.node_lefts_recv)
    node_rights = SimpleNamespace(data=v.node_rights, recv=v.node_rights_recv)
    sum_rights = SimpleNamespace(data=v.sum_rights, recv=v.sum_rights_recv)
    target_rights = SimpleNamespace(data=v.target_rights, recv=v.target_rights_recv)

    def drained(count, sem):
        ended(v.drain.at[pl.ds(0, count // lanes)], sem)

    started = SimpleNamespace(total=[0, 0], cores=(0, 1), times=1)

    def count_start(source):
        for one in started.cores:
            started.total[one] += started.times * source.size * source.dtype.itemsize // 2

    def send(source, target, recv_sem, device):
        count_start(source)
        pltpu.make_async_remote_copy(
            src_ref=source,
            dst_ref=target,
            send_sem=v.done,
            recv_sem=recv_sem,
            device_id=device,
            device_id_type=MESH,
        ).start()

    def write(source, target):
        count_start(source)
        pltpu.make_async_copy(source, target, v.done).start()

    def on_core(one, act):
        before = started.cores
        started.cores = tuple(x for x in before if x == one)
        pl.when(core == one)(act)
        started.cores = before

    def each(count, visit):
        if count <= 8:
            for i in range(count):
                visit(i)
        else:
            before = started.times

            def step(i, carry):
                started.times = before * count
                visit(i)
                started.times = before
                return carry

            lax.fori_loop(0, count, step, 0)

    barrier = pltpu.get_barrier_semaphore()

    def greet(device):
        pl.semaphore_signal(barrier, inc=1, device_id=device, device_id_type=MESH)

    each(shards - 1, lambda i: greet((section, (row + 1 + i) % shards)))
    for step in range(1, sections):
        for other in range(2):
            greet(((section + step) % sections, pair * 2 + other))

    def peer_rows(visit):
        if pairs == 4:
            for peer in (3 - pair, (pair + 2) % 4, pair + 1 - 2 * (pair % 2)):
                visit(2 * peer + core)
                visit(2 * peer + 1 - core)
            visit(row + 1 - 2 * core)
        else:
            each(shards - 1, lambda i: visit((row + 1 + i) % shards))

    def send_nodes(layer, source):
        def one(peer):
            send(source, v.nodes.at[layer, row], v.nodes_recv.at[layer], (section, peer))

        peer_rows(one)

    def send_sums(layer):
        ended(v.mate_sums.at[layer], v.mate_sums_recv.at[layer])
        both = v.sums[layer, core].astype(f32) + v.mate_sums[layer].astype(f32)
        v.both_sums[layer] = both.astype(bf16)

        def one(peer):
            send(
                v.both_sums.at[layer, peer],
                v.sums_in.at[layer, pair],
                v.sums_recv.at[layer],
                (section, peer * 2 + core),
            )

        peer_pairs(one)

    def peer_pairs(visit):
        if pairs == 4:
            for peer in (3 - pair, (pair + 2) % 4, pair + 1 - 2 * (pair % 2)):
                visit(peer)
        else:
            each(pairs - 1, lambda i: visit((pair + 1 + i) % pairs))

    def send_sums_alone():
        def one(peer, other):
            send(
                v.sums.at[0, other, peer],
                v.sums_all.at[row],
                v.sums_recv.at[0],
                (section, peer * 2 + other),
            )

        def both(peer):
            one(peer, core)
            one(peer, 1 - core)

        peer_pairs(both)
        one(pair, 1 - core)

    def from_rows(data, sem, layer):
        ended(data.at[layer, pl.ds(0, shards - 1)], sem.at[layer])

    def to_plane(group, layer, sources):
        def one(target_section, other):
            source = sources[other](target_section)
            send(
                source,
                group.data.at[layer, plane_slot, pl.ds(0, source.shape[0])],
                group.recv.at[layer],
                (target_section, pair * 2 + other),
            )

        def keep(other):
            source = sources[other](section)
            group.data[layer, plane_slot, 0 : source.shape[0]] = source[...]

        for other in range(2):
            if sources[other] is not None:
                for step in range(1, sections):
                    one((section + step) % sections, other)
                on_core(1 - other, functools.partial(one, section, other))
                on_core(other, functools.partial(keep, other))

    def from_plane(group, layer, rows):
        drained((plane - 1) * rows * group.data.shape[-1], group.recv.at[layer])

    def to_mate(taker, target, recv_sem, source):
        target = target.at[pl.ds(0, source.shape[0])]
        mate = (section, row + 1 - 2 * core)
        on_core(1 - taker, lambda: send(source, target, recv_sem, mate))

    def send_parts(layer, rows):
        for step in range(1, sections):
            target = (section + step) % sections
            send(
                v.parts.at[layer, target, pl.ds(0, rows)],
                v.parts_in.at[layer, section, pl.ds(0, rows)],
                v.parts_recv.at[layer],
                (target, row),
            )

    def send_pairs(group, layer, relay, outer=True, inner=True):
        def one(peer):
            send(
                group.own.at[layer, peer],
                group.come.at[layer, pair],
                group.recv.at[0, layer],
                (section, peer * 2 + core),
            )

        if not relay:
            peer_pairs(one)
            return
        mirror = pairs - 1 - pair

        @pl.when(pair % 3 == 0)
        def _():
            near = (pair + 3) // 3
            if outer:
                send(
                    group.own.at[layer, mirror],
                    group.relay.at[layer],
                    group.recv.at[2, layer],
                    (section, near * 2 + core),
                )
            if inner:
                one(near)
                one(3 - near)

        before, started.cores = started.cores, ()

        @pl.when(pair % 3 != 0)
        def _():
            if outer:
                one(3 * (pair - 1))
            if inner:
                one(mirror)

        started.cores = before

    def relay_pairs(group, layer):
        before, started.cores = started.cores, ()

        @pl.when(pair % 3 != 0)
        def _():
            far = 3 - 3 * (pair - 1)
            ended(group.relay.at[layer], group.recv.at[2, layer])
            group.own[layer, far] = (
                group.own[layer, far].astype(f32) + group.relay[layer].astype(f32)
            ).astype(bf16)
            send(
                group.own.at[layer, far],
                group.come.at[layer, pair],
                group.recv.at[0, layer],
                (section, far * 2 + core),
            )

        started.cores = before

    def add_pairs(group, layer, relay):
        def add(peers):
            ended(group.come.at[layer, pl.ds(0, len(peers))], group.recv.at[0, layer])
            total = group.own[layer, pair].astype(f32)
            for peer in peers:
                total = total + group.come[layer, peer].astype(f32)
            group.total[layer] = total.astype(bf16)

        if relay:
            pl.when(pair % 3 == 0)(lambda: add([1, 2]))
            pl.when(pair % 3 != 0)(lambda: add([(pair + step) % 4 for step in (1, 2, 3)]))
        else:
            add([(pair + step) % pairs for step in range(1, pairs)])

        def share(target_section, other):
            send(
                group.total.at[layer, other],
                group.full.at[layer, section],
                group.recv.at[1, layer],
                (target_section, pair * 2 + other),
            )

        for step in range(1, sections):
            for other in range(2):
                share((section + step) % sections, other)
        share(section, 1 - core)
        write(group.total.at[layer, core], group.full.at[layer, section])

    def from_givers(group, layer, giver):
        def wait(other):
            slots = sections - 1 if other == giver else sections
            ended(group.full.at[layer, pl.ds(0, slots)], group.recv.at[1, layer])

        for other in range(2):
            on_core(other, functools.partial(wait, other))

    def store_blocks(target, product, offset, rows, owners=range(shards)):
        padded = whole_tiles(rows)
        for owner in owners:
            block = product[owner * rows : (owner + 1) * rows]
            if padded != rows:
                block = jnp.concatenate([block, jnp.zeros((padded - rows, quarter), f32)], axis=0)
            target[owner // 2, owner % 2, offset : offset + padded] = block.astype(bf16)

    def store_vectors(target, total, offset):
        for owner in range(shards):
            target[owner // 2, owner % 2, offset : offset + vector_rows] = total.astype(bf16)

    def quarters(target, offset, value):
        rows = value.shape[0]
        for part in range(sections):
            target[part, offset : offset + rows] = value[
                :, part * quarter : (part + 1) * quarter
            ].astype(bf16)

    def vector(kind, layer):
        return v.vectors[vector_kinds.index(kind)].astype(f32)[layer : layer + 1]

    pl.semaphore_wait(barrier, shards - 1 + 2 * (sections - 1))
    send_nodes(0, v.node_features.at[section])

    def load(source, target, sem):
        pltpu.make_async_copy(source, target, v.load_sem.at[sem]).start()

    def load_matrix(kind, layer, sem):
        rows = weights[kind].shape[1]
        target = v.matrices.at[layer, pl.ds(plan.start[kind], rows)]
        load(weights[kind].at[layer], target, sem)

    def matrix(kind, layer, first=0, count=None):
        rows = weights[kind].shape[1] if count is None else count * width
        start = plan.start[kind] + first * width
        return v.matrices[layer, start : start + rows]

    def loaded(target, sem):
        ended(target, v.load_sem.at[sem])

    load(v.node_features.at[section], v.nodes.at[0, row], 0)
    load(v.edge_features.at[section], v.edge_in.at[0], 1)
    load_matrix(e_one, 0, 2)
    for place, source in enumerate((v.owner, v.local, v.receivers)):
        load(source.at[section], v.index.at[place], 3)
    for place, kind in enumerate(vector_kinds):
        load(weights[kind], v.vectors.at[place], 4)
    for kind in (e_two, n_one, n_two):
        load_matrix(kind, 0, 5)
    for layer in range(1, layers):
        for kind in matrix_kinds:
            load_matrix(kind, layer, 5 + layer)
    load(v.cotangent.at[section], v.cotangent_v, 5 + layers)

    on_core(0, lambda: load(v.edge_features, v.lefts.at[pl.ds(0, sections)], 6 + layers))
    to_mate(0, v.lefts.at[pl.ds(sections, sections)], v.lefts_recv, v.edge_features)

    loaded(v.nodes.at[0, row], 0)
    loaded(v.edge_in.at[0], 1)

    loaded(v.index, 3)
    sender_row, target_row = v.index[0] * node_dev + v.index[1], v.index[2]
    eye = lax.broadcasted_iota(jnp.int32, (edge_dev, edge_dev), 0) == lax.broadcasted_iota(
        jnp.int32, (edge_dev, edge_dev), 1
    )

    def to_column(values):
        spread = jnp.broadcast_to(values, (edge_dev, edge_dev))
        column = jnp.sum(jnp.where(eye, spread, 0).astype(f32), axis=1, keepdims=True)
        return column.astype(jnp.int32)

    def one_hot(values, count, axis):
        places = (count, edge_dev) if axis == 0 else (edge_dev, count)
        match = lax.broadcasted_iota(jnp.int32, places, axis) == values
        return jnp.where(match, 1.0, 0.0).astype(bf16)

    v.from_nodes[...] = one_hot(to_column(sender_row), nodes_total, 1)
    v.to_nodes[...] = one_hot(sender_row, nodes_total, 0)
    v.from_targets[...] = one_hot(to_column(target_row), node_dev, 1)
    v.to_targets[...] = one_hot(target_row, node_dev, 0)
    loaded(v.vectors, 4)

    def edge_forward(layer):
        node = v.nodes[layer, row]
        edge = v.edge_in[layer]
        if layer == 0:
            loaded(v.matrices.at[0, pl.ds(0, 3 * width)], 2)
        else:
            loaded(v.matrices.at[layer], 5 + layer)
        received = dot(v.from_targets[...], node).astype(bf16)
        v.work[...] = (
            dot(edge, matrix(e_one, layer, 0, 1))
            + dot(received, matrix(e_one, layer, 2, 1))
            + vector(e_bias_one, layer)
        )
        if layer == 0:
            loaded(v.matrices.at[0, pl.ds(3 * width, v.matrices.shape[1] - 3 * width)], 5)
        v.node_work[...] = dot(node, matrix(n_one, layer, 0, 1)) + vector(n_bias_one, layer)
        from_rows(v.nodes, v.nodes_recv, layer)
        sent = dot(v.from_nodes[...], v.nodes[layer].reshape(nodes_total, width)).astype(bf16)
        hidden, slope = activate(
            v.work[...] + dot(sent, matrix(e_one, layer, 1, 1))
        )
        v.edge_hidden[layer] = hidden
        v.edge_slope[layer] = slope
        to_mate(1, v.mate_left.at[layer], v.mate_recv.at[layer], v.edge_hidden.at[layer])
        normed, scale = layer_norm(
            dot(hidden, matrix(e_two, layer)) + vector(e_bias_two, layer)
        )
        v.edge_normed[layer] = normed
        v.edge_scale[layer] = scale
        edge = (
            edge.astype(f32)
            + (normed * vector(e_gain, layer) + vector(e_shift, layer))
        ).astype(bf16)
        if layer + 1 < layers:
            v.edge_in[layer + 1] = edge
            to_mate(
                0, v.pre_left.at[layer + 1], v.pre_recv.at[layer + 1], v.edge_in.at[layer + 1]
            )
        return node, dot(v.to_targets[...], edge).astype(bf16)

    def node_forward(layer, node, gathered):
        hidden, slope = activate(
            v.node_work[...] + dot(gathered, matrix(n_one, layer, 1, 1))
        )
        v.node_slope[layer] = slope
        normed, scale = layer_norm(
            dot(hidden, matrix(n_two, layer)) + vector(n_bias_two, layer)
        )
        v.node_normed[layer] = normed
        v.node_scale[layer] = scale
        new_node = (
            node.astype(f32)
            + (normed * vector(n_gain, layer) + vector(n_shift, layer))
        ).astype(bf16)
        if layer + 1 < layers:
            v.nodes[layer + 1, row] = new_node
            send_nodes(layer + 1, v.nodes.at[layer + 1, row])
        else:
            v.final_v[0] = new_node
            write(v.final_v, v.final)
        v.node_lefts_own[layer, 0:node_dev] = node
        v.node_lefts_own[layer, node_dev : 2 * node_dev] = gathered
        v.node_lefts_own[layer, 2 * node_dev : 3 * node_dev] = hidden
        to_plane(node_lefts, layer, (None, lambda s: v.node_lefts_own.at[layer]))

    for layer in range(layers):
        node, gathered = edge_forward(layer)
        node_forward(layer, node, gathered)

    def hand_states(layer):
        def act():
            from_plane(node_lefts, layer, 3 * node_dev)
            send(
                v.node_lefts.at[layer, :, pl.ds(0, node_dev)],
                v.states.at[layer],
                v.states_recv.at[layer],
                (section, row + 1 - 2 * core),
            )

        on_core(1, act)

    def node_products(layer, relay):
        def act():
            from_plane(node_rights, layer, 2 * node_dev + vector_rows)
            own = plane * node_dev
            state = v.node_lefts[layer, :, 0:node_dev].reshape(own, width)
            gathered = v.node_lefts[layer, :, node_dev : 2 * node_dev].reshape(own, width)
            hidden = v.node_lefts[layer, :, 2 * node_dev : 3 * node_dev].reshape(own, width)
            grad_pre = v.node_rights[layer, :, 0:node_dev].reshape(own, quarter)
            grad_lifted = v.node_rights[layer, :, node_dev : 2 * node_dev].reshape(own, quarter)
            vectors = v.node_rights[layer, :, 2 * node_dev : 2 * node_dev + vector_rows]
            v.product[0:width] = contract_rows(state, grad_pre)
            v.product[width : 2 * width] = contract_rows(gathered, grad_pre)
            v.product[2 * width : 3 * width] = contract_rows(hidden, grad_lifted)
            target = node_pairs.own.at[layer]
            store_blocks(target, v.product, 0, two_rows)
            start = whole_tiles(two_rows)
            store_blocks(target, v.product.at[pl.ds(2 * width, width)], start, one_rows)
            v.node_vectors[layer] = jnp.sum(vectors.astype(f32), axis=0)
            send_pairs(node_pairs, layer, relay)

        on_core(1, act)

    def edge_parts(layer):
        def multiply(lefts, rights):
            left = jnp.concatenate(lefts, axis=0)
            right = jnp.concatenate(rights, axis=0)
            for part in range(sections):
                columns = slice(part * quarter, (part + 1) * quarter)
                v.parts[layer, part, 0:width] = contract_rows(left, right[:, columns]).astype(bf16)

        def act_one():
            drained(2 * edge_dev * width, v.pre_recv.at[layer])
            multiply([v.edge_in[layer], v.pre_left[layer]], [v.pre_own[layer], v.pre_right[layer]])
            send_parts(layer, width)

        def act_two():
            drained((2 * edge_dev + vector_rows) * width, v.mate_recv.at[layer])
            multiply(
                [v.edge_hidden[layer], v.mate_left[layer]],
                [v.lift_own[layer, 0:edge_dev], v.mate_right[layer, 0:edge_dev]],
            )
            vectors = (
                v.lift_own[layer, edge_dev : edge_dev + vector_rows].astype(f32)
                + v.mate_right[layer, edge_dev : edge_dev + vector_rows].astype(f32)
            ).astype(bf16)
            for part in range(sections):
                columns = slice(part * quarter, (part + 1) * quarter)
                v.parts[layer, part, width : width + vector_rows] = vectors[:, columns]
            send_parts(layer, width + vector_rows)

        if layer > 0:
            on_core(0, act_one)
        on_core(1, act_two)

    def from_parts(layer, rows):
        drained((sections - 1) * rows * quarter, v.parts_recv.at[layer])

    def add_parts(layer, start, rows):
        total = v.parts[layer, section, start : start + rows].astype(f32)
        for step in range(1, sections):
            other = (section + step) % sections
            total = total + v.parts_in[layer, other, start : start + rows].astype(f32)
        return total

    outer_owners = [0, 1, shards - 2, shards - 1]
    inner_owners = [owner for owner in range(shards) if owner not in outer_owners]

    def state_products(layer, group, place):
        own = plane * node_dev
        from_plane(group, layer, node_dev)
        v.edge_product[layer, place * width : (place + 1) * width] = contract_rows(
            v.states[layer].reshape(own, width), group.data[layer].reshape(own, quarter)
        )

    def edge_products(layer, relay):
        def act():
            if layer == 0:
                loaded(v.lefts.at[pl.ds(0, sections)], 6 + layers)
                ended(v.lefts.at[pl.ds(sections, sections)], v.lefts_recv)
                from_plane(rights, 0, edge_dev)
                v.edge_product[0, 0:width] = contract_rows(
                    v.lefts[...].reshape(plane * edge_dev, width),
                    v.rights[0].reshape(plane * edge_dev, quarter),
                )
            else:
                from_parts(layer, width)
                v.edge_product[layer, 0:width] = add_parts(layer, 0, width)
            ended(v.states.at[layer], v.states_recv.at[layer])
            state_products(layer, target_rights, 2)
            if relay:
                blocks, product = edge_pairs.own.at[layer], v.edge_product.at[layer]
                store_blocks(blocks, product, 0, three_rows, outer_owners)
                send_pairs(edge_pairs, layer, True, inner=False)

        on_core(0, act)

    def sender_products(layer, relay):
        def act():
            state_products(layer, sum_rights, 1)
            owners = inner_owners if relay else range(shards)
            blocks, product = edge_pairs.own.at[layer], v.edge_product.at[layer]
            store_blocks(blocks, product, 0, three_rows, owners)
            send_pairs(edge_pairs, layer, relay, outer=False)

        on_core(0, act)

    def lift_products(layer, relay):
        def act():
            from_parts(layer, width + vector_rows)
            v.product[0:width] = add_parts(layer, 0, width)
            target = lift_pairs.own.at[layer]
            store_blocks(target, v.product, 0, one_rows)
            vectors = add_parts(layer, width, vector_rows) + v.node_vectors[layer]
            store_vectors(target, vectors, whole_tiles(one_rows))
            send_pairs(lift_pairs, layer, relay)

        on_core(1, act)

    def relay_products(group, giver, layer, relay):
        if relay:
            on_core(giver, lambda: relay_pairs(group, layer))

    def add_products(group, giver, layer, relay):
        on_core(giver, lambda: add_pairs(group, layer, relay))

    def node_backward(layer):
        grad_branch = v.grad_node[...]
        normed = v.node_normed[layer]
        grad_lifted = branch_back(
            grad_branch, vector(n_gain, layer), normed, v.node_scale[layer]
        )
        grad_hidden = contract_cols(grad_lifted, matrix(n_two, layer))
        grad_pre = (grad_hidden * v.node_slope[layer]).astype(bf16)
        aggregate = contract_cols(grad_pre, matrix(n_one, layer, 1, 1))
        high = aggregate.astype(bf16)
        low = (aggregate - high.astype(f32)).astype(bf16)
        grad_edge = dot(v.from_targets[...], high) + dot(v.from_targets[...], low)
        if layer + 1 < layers:
            grad_edge = grad_edge + v.grad_edge[...]
        v.grad_edge[...] = grad_edge.astype(bf16).astype(f32)
        target = v.node_rights_own.at[layer]
        quarters(target, 0, grad_pre)
        quarters(target, node_dev, grad_lifted)
        quarters(target, 2 * node_dev, column_sums(grad_pre, grad_lifted, grad_branch, normed, 4))
        to_plane(node_rights, layer, (None, lambda s: v.node_rights_own.at[layer, s]))
        return grad_branch, grad_pre

    def node_backward_rest(layer, grad_branch, grad_pre):
        grad_node = grad_branch + contract_cols(grad_pre, matrix(n_one, layer, 0, 1))
        v.grad_node[...] = grad_node.astype(bf16).astype(f32)

    def edge_backward(layer, rest):
        grad_branch = v.grad_edge[...]
        normed = v.edge_normed[layer]
        grad_lifted = branch_back(
            grad_branch, vector(e_gain, layer), normed, v.edge_scale[layer]
        )
        grad_hidden = contract_cols(grad_lifted, matrix(e_two, layer))
        grad_pre = (grad_hidden * v.edge_slope[layer]).astype(bf16)
        sums = dot(v.to_nodes[...], grad_pre).astype(bf16)
        for place in range(shards):
            block = sums[place * node_dev : (place + 1) * node_dev]
            v.sums[layer, place % 2, place // 2] = block
        mate = (section, row + 1 - 2 * core)
        if layer == 0:
            send_sums_alone()
        else:
            send(
                v.sums.at[layer, 1 - core], v.mate_sums.at[layer], v.mate_sums_recv.at[layer], mate
            )
        if layer == 0:
            quarters(v.pre_rights_own, 0, grad_pre)
            to_plane(rights, 0, (lambda s: v.pre_rights_own.at[s], None))
        else:
            v.pre_own[layer] = grad_pre
            to_mate(0, v.pre_right.at[layer], v.pre_recv.at[layer], v.pre_own.at[layer])
        v.lift_own[layer, 0:edge_dev] = grad_lifted
        v.lift_own[layer, edge_dev : edge_dev + vector_rows] = column_sums(
            grad_pre, grad_lifted, grad_branch, normed, 0
        )
        to_mate(1, v.mate_right.at[layer], v.mate_recv.at[layer], v.lift_own.at[layer])
        node_backward_rest(layer, *rest)
        if layer > 0:
            send_sums(layer)
        grad_edge = grad_branch + contract_cols(grad_pre, matrix(e_one, layer, 0, 1))
        by_target = dot(v.to_targets[...], grad_pre).astype(bf16)
        quarters(v.target_rights_own.at[layer], 0, by_target)
        to_plane(target_rights, layer, (lambda s: v.target_rights_own.at[layer, s], None))
        v.grad_node[...] = v.grad_node[...] + contract_cols(
            by_target, matrix(e_one, layer, 2, 1)
        )
        if layer > 0:
            v.grad_edge[...] = grad_edge.astype(bf16).astype(f32)
        else:
            v.grad_edges_v[0] = grad_edge
            write(v.grad_edges_v, v.grad_edges)

    def sender_backward(layer):
        if layer == 0:
            ended(v.sums_all.at[pl.ds(0, shards - 1)], v.sums_recv.at[0])
            v.sums_all[row] = v.sums[0, core, pair]
            parts = v.sums_all[...]
        else:
            ended(v.sums_in.at[layer, pl.ds(0, pairs - 1)], v.sums_recv.at[layer])
            v.sums_in[layer, pair] = v.both_sums[layer, pair]
            parts = v.sums_in[layer]
        by_sender = jnp.sum(parts.astype(f32), axis=0).astype(bf16)
        target = v.sum_rights_own.at[layer]
        quarters(target, 0, by_sender)
        to_plane(sum_rights, layer, (lambda s: v.sum_rights_own.at[layer, s], None))
        grad_node = v.grad_node[...] + contract_cols(
            by_sender, matrix(e_one, layer, 1, 1)
        )
        if layer > 0:
            v.grad_node[...] = grad_node.astype(bf16).astype(f32)
        else:
            v.grad_nodes_v[0] = grad_node
            write(v.grad_nodes_v, v.grad_nodes)

    loaded(v.cotangent_v, 5 + layers)
    v.grad_node[...] = v.cotangent_v[...].astype(f32)
    relay = pairs == 4
    later = list(reversed(range(1, layers)))
    for layer in later:
        edge_backward(layer, node_backward(layer))
        edge_parts(layer)
        sender_backward(layer)
        hand_states(layer)
        node_products(layer, relay)
    edge_backward(0, node_backward(0))
    edge_parts(0)
    hand_states(0)
    for layer in later + [0]:
        edge_products(layer, relay)
    for layer in later:
        lift_products(layer, relay)
        relay_products(node_pairs, 1, layer, relay)
    node_products(0, relay)
    for layer in later:
        relay_products(lift_pairs, 1, layer, relay)
    sender_backward(0)
    for layer in later:
        sender_products(layer, relay)
    for layer in later + [0]:
        relay_products(edge_pairs, 0, layer, relay)
    sender_products(0, relay)
    lift_products(0, relay)
    relay_products(node_pairs, 1, 0, relay)
    relay_products(lift_pairs, 1, 0, relay)
    for layer in later + [0]:
        add_products(node_pairs, 1, layer, relay)
        add_products(lift_pairs, 1, layer, relay)
        add_products(edge_pairs, 0, layer, relay)

    for layer in range(layers):
        from_givers(edge_pairs, layer, 0)
        from_givers(lift_pairs, layer, 1)
        from_givers(node_pairs, layer, 1)
    for one in range(2):
        pl.when(core == one)(
            lambda: drained(started.total[one], v.done)
        )


def write_kernel(shards, *refs):
    final, grad_nodes, grad_edges, edge_full, lift_full, node_full = refs[:6]
    out_final, out_nodes, out_edges = refs[6:9]
    grads = refs[9:]
    row = lax.axis_index("rows")
    layers, sections, quarter = edge_full.shape[0], edge_full.shape[1], edge_full.shape[3]
    width = sections * quarter
    three_rows, two_rows, one_rows = (part * width // shards for part in (3, 2, 1))
    node_start = whole_tiles(two_rows)
    out_final[...] = final[...]
    out_nodes[...] = grad_nodes[...]
    out_edges[...] = grad_edges[...]

    def put(target, full, start, rows):
        for layer in range(layers):
            for part in range(sections):
                value = full[layer, part, start : start + whole_tiles(rows)]
                target[layer, :, part * quarter : (part + 1) * quarter] = value.astype(f32)[0:rows]

    put(grads[e_one], edge_full, 0, three_rows)
    put(grads[e_two], lift_full, 0, one_rows)
    put(grads[n_one], node_full, 0, two_rows)
    put(grads[n_two], node_full, node_start, one_rows)

    def take_columns(value):
        per = quarter // one_rows
        taken = jnp.zeros((vector_rows, one_rows), f32)
        for place in range(per):
            taken = taken + jnp.where(
                row % per == place, value[:, place * one_rows : (place + 1) * one_rows], 0.0
            )
        return taken

    holder = row // (quarter // one_rows)
    for layer in range(layers):
        start = whole_tiles(one_rows)
        taken = take_columns(lift_full[layer, holder, start : start + vector_rows].astype(f32))
        for place, kind in enumerate(vector_kinds):
            grads[kind][layer : layer + 1] = taken[place : place + 1]


def fused(sections, shards, node_features, edge_features, owner, local, receivers, cotangent, *weights):
    micro_count, node_dev, width = node_features.shape
    edge_dev = edge_features.shape[1]
    layers = weights[0].shape[0]
    quarter, pairs, plane = width // sections, shards // 2, 2 * sections
    nodes_total = shards * node_dev

    def shape(*dims, kind=f32):
        return jax.ShapeDtypeStruct(dims, kind)

    def vmem(*dims, kind=bf16):
        return pltpu.VMEM(dims, kind)

    def sems(*dims):
        return pltpu.SemaphoreType.DMA(dims)

    inputs = dict(
        node_features=node_features,
        edge_features=edge_features,
        owner=owner,
        local=local,
        receivers=receivers,
        cotangent=cotangent,
    )
    outputs = dict(
        final=shape(1, node_dev, width, kind=bf16),
        grad_nodes=shape(1, node_dev, width),
        grad_edges=shape(1, edge_dev, width),
    )
    weight_grads = [
        shape(layers, weight.shape[1] // shards, *weight.shape[2:]) for weight in weights
    ]
    lift_block = whole_tiles(width // shards) + vector_rows
    blocks = (
        whole_tiles(3 * width // shards),
        lift_block,
        whole_tiles(2 * width // shards) + whole_tiles(width // shards),
    )
    fulls = [shape(layers, sections, block, quarter, kind=bf16) for block in blocks]
    starts = np.cumsum([0] + [weights[kind].shape[1] for kind in matrix_kinds])
    scratch = dict(
        done=pltpu.SemaphoreType.DMA,
        drain=vmem(1024 * (24 + shards // 2), lanes),
        load_sem=sems(7 + layers),
        index=vmem(3, 1, edge_dev, kind=jnp.int32),
        vectors=vmem(len(vector_kinds), layers, width),
        matrices=vmem(layers, int(starts[-1]), width),
        cotangent_v=vmem(node_dev, width),
        from_nodes=vmem(edge_dev, nodes_total),
        to_nodes=vmem(nodes_total, edge_dev),
        from_targets=vmem(edge_dev, node_dev),
        to_targets=vmem(node_dev, edge_dev),
        work=vmem(edge_dev, width, kind=f32),
        node_work=vmem(node_dev, width, kind=f32),
        grad_node=vmem(node_dev, width, kind=f32),
        grad_edge=vmem(edge_dev, width, kind=f32),
        product=vmem(3 * width, quarter, kind=f32),
        edge_in=vmem(layers, edge_dev, width),
        edge_hidden=vmem(layers, edge_dev, width),
        edge_slope=vmem(layers, edge_dev, width, kind=f32),
        edge_normed=vmem(layers, edge_dev, width, kind=f32),
        edge_scale=vmem(layers, edge_dev, 1, kind=f32),
        node_slope=vmem(layers, node_dev, width, kind=f32),
        node_normed=vmem(layers, node_dev, width, kind=f32),
        node_scale=vmem(layers, node_dev, 1, kind=f32),
        nodes=vmem(layers, shards, node_dev, width),
        nodes_recv=sems(layers),
        sums=vmem(layers, 2, pairs, node_dev, width),
        mate_sums=vmem(layers, pairs, node_dev, width),
        mate_sums_recv=sems(layers),
        both_sums=vmem(layers, pairs, node_dev, width),
        sums_in=vmem(layers, pairs, node_dev, width),
        sums_all=vmem(shards, node_dev, width),
        sums_recv=sems(layers),
        final_v=vmem(1, node_dev, width),
        grad_nodes_v=vmem(1, node_dev, width, kind=f32),
        grad_edges_v=vmem(1, edge_dev, width, kind=f32),
        node_vectors=vmem(layers, vector_rows, quarter, kind=f32),
        mate_left=vmem(layers, edge_dev, width),
        mate_right=vmem(layers, edge_dev + vector_rows, width),
        mate_recv=sems(layers),
        lefts=vmem(plane, edge_dev, width),
        lefts_recv=pltpu.SemaphoreType.DMA,
        pre_rights_own=vmem(sections, edge_dev, quarter),
        rights=vmem(1, plane, edge_dev, quarter),
        rights_recv=sems(1),
        pre_own=vmem(layers, edge_dev, width),
        pre_left=vmem(layers, edge_dev, width),
        pre_right=vmem(layers, edge_dev, width),
        pre_recv=sems(layers),
        states=vmem(layers, plane, node_dev, width),
        states_recv=sems(layers),
        lift_own=vmem(layers, edge_dev + vector_rows, width),
        parts=vmem(layers, sections, width + vector_rows, quarter),
        parts_in=vmem(layers, sections, width + vector_rows, quarter),
        parts_recv=sems(layers),
        node_lefts_own=vmem(layers, 3 * node_dev, width),
        node_lefts=vmem(layers, plane, 3 * node_dev, width),
        node_lefts_recv=sems(layers),
        node_rights_own=vmem(layers, sections, 2 * node_dev + vector_rows, quarter),
        node_rights=vmem(layers, plane, 2 * node_dev + vector_rows, quarter),
        node_rights_recv=sems(layers),
        edge_product=vmem(layers, 3 * width, quarter, kind=f32),
        target_rights_own=vmem(layers, sections, node_dev, quarter),
        target_rights=vmem(layers, plane, node_dev, quarter),
        target_rights_recv=sems(layers),
        sum_rights_own=vmem(layers, sections, node_dev, quarter),
        sum_rights=vmem(layers, plane, node_dev, quarter),
        sum_rights_recv=sems(layers),
    )
    pair_groups = []
    for block in blocks:
        group = dict(
            own=vmem(layers, pairs, 2, block, quarter),
            come=vmem(layers, pairs, 2, block, quarter),
            total=vmem(layers, 2, block, quarter),
            relay=vmem(layers, 2, block, quarter),
            recv=sems(3, layers),
        )
        pair_groups += group.values()
    ins, outs = len(inputs) + len(weights), len(outputs) + len(fulls)
    names = (
        list(inputs)
        + list(range(len(weights)))
        + list(outputs)
        + list(range(len(fulls)))
        + list(scratch)
    )
    plan = SimpleNamespace(
        names=[str(name) for name in names],
        weights=len(inputs),
        fulls=ins + len(outputs),
        pair_groups=ins + outs + len(scratch),
        pair_names=list(group),
        start=dict(zip(matrix_kinds, map(int, starts))),
        layers=layers,
        sections=sections,
        shards=shards,
        node_dev=node_dev,
        edge_dev=edge_dev,
        width=width,
    )
    results = pl.pallas_call(
        functools.partial(kernel, plan),
        out_shape=list(outputs.values()) + fulls,
        in_specs=[pl.BlockSpec(memory_space=pltpu.HBM)] * ins,
        out_specs=[pl.BlockSpec(memory_space=pl.ANY)] * outs,
        scratch_shapes=list(scratch.values()) + pair_groups,
        compiler_params=pltpu.CompilerParams(
            collective_id=0, has_side_effects=True, vmem_limit_bytes=40 << 20
        ),
    )(*(pltpu.with_memory_space_constraint(x, pltpu.HBM) for x in (*inputs.values(), *weights)))
    return pl.pallas_call(
        functools.partial(write_kernel, shards),
        out_shape=list(outputs.values()) + weight_grads,
        in_specs=[pl.BlockSpec(memory_space=pltpu.VMEM)] * outs,
        out_specs=[pl.BlockSpec(memory_space=pltpu.VMEM)] * (len(outputs) + len(weight_grads)),
        compiler_params=pltpu.CompilerParams(vmem_limit_bytes=16 << 20),
    )(*results)


def solution(mesh):
    sections, shards = mesh.shape["section"], mesh.shape["rows"]

    def body(node_features, edge_features, owner, *rest):
        owner = owner.reshape(owner.shape[:-1])
        return fused(sections, shards, node_features, edge_features, owner, *rest)

    in_specs = (
        P(None, "rows", None),
        P(None, "rows", None),
        P(None, "rows", None, None),
        P(None, "rows", None),
        P(None, "rows", None),
        P(None, "rows", None),
    ) + (P(),) * 12
    state = P("section", "rows", None)
    matrix, vector = P(None, "rows", None), P(None, "rows")
    out_specs = (state,) * 3 + (matrix, vector, matrix, vector, vector, vector) * 2
    return jax.shard_map(body, mesh=mesh, in_specs=in_specs, out_specs=out_specs, check_vma=False)
```
